128 devices in a mesh: slab: 32 (over y, z_hi, x), comp: 4 (over z_lo, core).
Axes of the slice: x: 4, y: 4, z: 4 (z_hi: 2, z_lo: 2; z = z_hi * 2 + z_lo), core: 2. Of those that a mesh axis runs over, the one named last changes fastest.
Arguments:
- current_field: float32 [3, 256, 64, 256], P(None, 'slab', 'comp'), may hold values from -6 to 6
- earlier_field: float32 [3, 256, 64, 256], P(None, 'slab', 'comp'), may hold values from -6 to 6
- wave_coef: float32 [256, 64, 256], P('slab', 'comp'), may hold values from 0.05 to 0.24
- layer_mask: int32 [256, 64, 256], P('slab', 'comp'), may hold values from 0 to 2
- point_xyz: float32 [3, 131072], P(None, ('slab', 'comp')), may hold values from 0 to 4
- point_owner: int32 [131072, 1], P(('slab', 'comp')), may hold values from 0 to 127; in each aligned block of 1024 rows (0 to 1023, 1024 to 2047, ...) at most 16 rows name the same one
- cell_offset: int32 [131072], P(('slab', 'comp')), may hold values from 0 to 32767
- wave_vector: float32 [3, 4096], P(None, 'comp'), may hold values from -8 to 8
- frequency: float32 [4096], P('comp'), may hold values from 0.5 to 8
- amplitude: float32 [3, 4096], P(None, 'comp'), may hold values from -0.09375 to 0.09375
- phase_index: int32 [4096], P('comp'), may hold values from 0 to 255
- phase_table: float32 [256], replicated, may hold values from -3.140625 to 3.140625
Outputs:
- final_field: float32 [3, 256, 64, 256], P(None, 'slab', 'comp')
- prior_field: float32 [3, 256, 64, 256], P(None, 'slab', 'comp')
The draws below stay inside these ranges and needn't reach their ends.
Inputs may be any that keep to these rules, and one draw needn't show every extreme that they name: `point_owner`: the device at position s of slab and c of comp is numbered s times the size of comp plus c. Among the rows of one device at most 16 points name one owner.
All inputs are finite; a program needn't handle non-finite values.
Results may differ from the reference program's by a relative error of at most 0.0003.
Values sent between devices are 32-bit elements; how exact they have to be, the bound alone decides.
A program may use at most 192 MiB of HBM per device.

```python
import math
import jax
import jax.numpy as jnp
import numpy as np
from jax import lax

CX = 8
CY = 16
NZ = 256
PT_DEV = 1024
K = 4096
NPH = 256
STEPS = 3
CAP = 16
NX = 256
NY = 64
POINTS = 131072
N_COMP = 4
DEVICES = 128


def set_ends(values, stream_key, low, top_value):
    longest = values.shape.index(max(values.shape))
    spots = []
    for shift in (0, 1):
        where = [jax.random.randint(jax.random.fold_in(stream_key, axis), (), 0, length) for axis, length in enumerate(values.shape)]
        where[longest] = (where[longest] + shift) % values.shape[longest]
        spots.append(tuple(where))
    return values.at[spots[0]].set(low).at[spots[1]].set(top_value)


def block_levels(own_key, shape, cuts, smallest, largest):
    level, own = 1.0, jax.random.fold_in(own_key, 6)
    for axis_at, shards_of in cuts:
        draws = jnp.exp(jax.random.uniform(jax.random.fold_in(own, axis_at), (shards_of,), jnp.float32, smallest / len(cuts), largest / len(cuts)))
        level = level * jnp.repeat(draws, shape[axis_at] // shards_of).reshape([-1 if axis == axis_at else 1 for axis in range(len(shape))])
    return level


def routed_block(rng, own, number, rows, amount, top, most, lean):
    ranking = jax.random.permutation(rng, amount)
    heavy_load, ordinary = shares(amount, rows * top, most, lean, True), shares(amount, rows * top, most, lean, False)
    places = jnp.arange(amount)

    def named(tallies, turn):
        used = int((tallies > 0).sum())
        fixed = max(1, used // 4)
        moved = fixed + (places - fixed + turn * (used - fixed)) % max(1, amount - fixed)
        return jnp.zeros((amount,), jnp.int32).at[ranking[jnp.where(places < fixed, places, moved)]].set(jnp.asarray(tallies, jnp.int32))

    tallies = jnp.where(number % 4 == 0, named(heavy_load, number // 4), named(ordinary, number - number // 4 - 1))
    mixed = jax.random.permutation(jax.random.fold_in(own, 3), amount)
    donor, sink = mixed[0:amount // 2 * 2:2], mixed[1:amount // 2 * 2:2]
    margin = jnp.minimum(tallies[donor] - 1, most - tallies[sink]) // 2
    margin = jnp.where((donor == ranking[0]) | (sink == ranking[0]) | (tallies[sink] == 0), 0, jnp.maximum(margin, 0))
    moved = jax.random.randint(jax.random.fold_in(own, 4), (amount // 2,), 0, 1 << 20) % (margin + 1)
    tallies = tallies.at[donor].add(-moved).at[sink].add(moved)
    items = jnp.searchsorted(jnp.cumsum(tallies), jnp.arange(rows * top), side="right").astype(jnp.int32)
    listing = items.reshape(top, rows).T
    listing = listing[jax.random.permutation(jax.random.fold_in(own, 1), rows)]
    turn = jax.random.randint(jax.random.fold_in(own, 2), (rows, 1), 0, top)
    return jnp.take_along_axis(listing, (jnp.arange(top)[None, :] + turn) % top, axis=1)


def shares(amount, total, most, slope, full):
    loads = [(1 << 20) // math.isqrt(standing ** slope) + 1 for standing in range(1, amount + 1)]
    largest = most if full else min(most, max(-(-total // amount), total * loads[0] // sum(loads)))
    least = 1 if total - largest >= amount - 1 else 0
    given, rest = [largest] + [least] * (amount - 1), total - largest - least * (amount - 1)
    while rest > 0:
        movable = [i for i in range(1, amount) if given[i] < largest] or [i for i in range(1, amount) if given[i] < most]
        mass, left = sum([loads[i] for i in movable]), rest
        for i in movable:
            addition = min(most - given[i], max(1, left * loads[i] // mass), rest)
            given[i] = given[i] + addition
            rest = rest - addition
    return np.array(given)


def noise(own_key, shape, width, limit, split=(), dtype=jnp.bfloat16):
    loudness = block_levels(own_key, shape, split, -0.22, 0.18) if split else 1.0
    values = jax.random.normal(own_key, shape, jnp.float32) * width * loudness
    return jnp.minimum(jnp.maximum(values, -limit), limit).astype(dtype)


def setup_inputs(seed: int = 0) -> dict:
    seeds = jax.random.split(jax.random.key(seed), 13)
    current_field = noise(seeds[0], (3, NX, NY, NZ), 1.0, 6.0, ((1, 32), (2, 4)), jnp.float32)
    earlier_field = noise(seeds[1], (3, NX, NY, NZ), 1.0, 6.0, ((1, 32), (2, 4)), jnp.float32)
    wave_coef = jnp.clip(jnp.exp(math.log(0.24) - 1.5686159 * jax.random.uniform(seeds[2], (NX, NY, NZ), jnp.float32) ** block_levels(seeds[2], (NX, NY, NZ), ((0, 32), (1, 4)), -0.2, 0.2)), 0.05, 0.24)
    layer_mask = set_ends(jax.random.randint(seeds[3], (NX, NY, NZ), 0, 3), jax.random.fold_in(seeds[3], 1), 0, 2).astype(jnp.int32)
    point_xyz = jnp.clip(4.0 * jax.random.uniform(seeds[4], (3, POINTS), jnp.float32) ** block_levels(seeds[4], (3, POINTS), ((1, 128),), -0.2, 0.2), 0.0, 4.0)
    point_owner_keys = jax.random.split(jax.random.fold_in(seeds[5], 1), POINTS // PT_DEV)
    point_owner_turns = jax.random.permutation(jax.random.fold_in(seeds[5], 3), POINTS // PT_DEV)
    point_owner = jax.vmap(lambda own, number: routed_block(jax.random.fold_in(seeds[5], 2), own, number, PT_DEV, DEVICES, 1, CAP, 2))(point_owner_keys, point_owner_turns).reshape((POINTS, 1))
    cell_offset = set_ends(jax.random.randint(seeds[6], (POINTS,), 0, CX * CY * NZ), jax.random.fold_in(seeds[6], 1), 0, (CX * CY * NZ) - 1).astype(jnp.int32)
    wave_vector = jnp.clip(jax.random.uniform(seeds[7], (3, K), jnp.float32, -8.0, 8.0) * block_levels(seeds[7], (3, K), ((1, 4),), -0.4, 0.0), -8.0, 8.0)
    frequency = jnp.clip(jnp.exp(math.log(8.0) - 2.7725887 * jax.random.uniform(seeds[8], (K,), jnp.float32) ** block_levels(seeds[8], (K,), ((0, 4),), -0.2, 0.2)), 0.5, 8.0)
    amplitude = noise(seeds[9], (3, K), K ** -0.5, 0.09375, ((1, 4),), jnp.float32)
    phase_index = set_ends(jax.random.randint(seeds[10], (K,), 0, NPH), jax.random.fold_in(seeds[10], 1), 0, NPH - 1).astype(jnp.int32)
    phase_table = jnp.clip(jax.random.uniform(seeds[11], (NPH,), jnp.float32, -3.140625, 3.140625), -3.140625, 3.140625)
    return {"current_field": current_field, "earlier_field": earlier_field, "wave_coef": wave_coef, "layer_mask": layer_mask, "point_xyz": point_xyz, "point_owner": point_owner, "cell_offset": cell_offset, "wave_vector": wave_vector, "frequency": frequency, "amplitude": amplitude, "phase_index": phase_index, "phase_table": phase_table}


step_size = 0.05
near_weight = 4.0 / 3.0
far_weight = -1.0 / 12.0
centre_weight = -7.5


def shifted(padded, axis_pos, offset):
    result = padded
    for dim_pos in (1, 2, 3):
        first_cell = 2 + offset if dim_pos == axis_pos else 2
        result = lax.slice_in_dim(result, first_cell, first_cell + padded.shape[dim_pos] - 4, axis=dim_pos)
    return result


def laplace_four(padded):
    summed = centre_weight * shifted(padded, 0, 0)
    for axis_pos in (1, 2, 3):
        summed = summed + near_weight * (shifted(padded, axis_pos, 1) + shifted(padded, axis_pos, -1))
        summed = summed + far_weight * (shifted(padded, axis_pos, 2) + shifted(padded, axis_pos, -2))
    return summed


def incident_terms(comp_block, coords):
    angles = comp_block[0][:, None] * coords[0][None, :] + comp_block[1][:, None] * coords[1][None, :] + comp_block[2][:, None] * coords[2][None, :]
    cosine = jnp.cos(angles)
    sine_part = jnp.sin(angles)
    moments = step_size * (jnp.arange(STEPS) + 1).astype(jnp.float32)
    delays = moments[:, None] * comp_block[3][None, :] - comp_block[7][None, :]
    block_width = comp_block.shape[1]
    left_cos = (jnp.cos(delays)[:, None, :] * comp_block[4:7][None, :, :]).reshape(STEPS * 3, block_width)
    left_sin = (jnp.sin(delays)[:, None, :] * comp_block[4:7][None, :, :]).reshape(STEPS * 3, block_width)
    first_part = jnp.dot(left_cos, cosine, precision=lax.Precision.HIGHEST, preferred_element_type=jnp.float32)
    second_part = jnp.dot(left_sin, sine_part, precision=lax.Precision.HIGHEST, preferred_element_type=jnp.float32)
    return first_part + second_part


def reference(current_field, earlier_field, wave_coef, layer_mask, point_xyz, point_owner, cell_offset, wave_vector, frequency, amplitude, phase_index, phase_table):
    phases = phase_table[phase_index]
    comp_block = jnp.concatenate([wave_vector, frequency[None, :], amplitude, phases[None, :]], axis=0)
    groups = jnp.transpose(point_xyz.reshape(3, DEVICES, PT_DEV), (1, 0, 2))
    incident = lax.map(lambda coords: incident_terms(comp_block, coords), groups)
    incident = jnp.transpose(incident, (1, 0, 2)).reshape(STEPS * 3, POINTS)
    owners = point_owner[:, 0]
    slab_pos = owners // N_COMP
    comp_pos = owners % N_COMP
    local_x = cell_offset // (CY * NZ)
    local_y = (cell_offset // NZ) % CY
    local_z = cell_offset % NZ
    flat_cell = (((slab_pos * CX + local_x) * NY + comp_pos * CY + local_y) * NZ + local_z).astype(jnp.int32)
    forcing = jnp.zeros((STEPS * 3, NX * NY * NZ), jnp.float32).at[:, flat_cell].add(incident)
    sign_field = ((layer_mask == 1).astype(jnp.float32) - (layer_mask == 2).astype(jnp.float32))[None]
    current = current_field
    earlier = earlier_field
    for step_index in range(STEPS):
        padded = jnp.pad(current, ((0, 0), (2, 2), (2, 2), (2, 2)))
        source = forcing[3 * step_index:3 * step_index + 3].reshape(3, NX, NY, NZ)
        following = 2.0 * current - earlier + wave_coef[None] * laplace_four(padded) + sign_field * source
        earlier = current
        current = following
    return current, earlier
```

```python
import functools

import jax
import jax.numpy as jnp
import numpy as np
from jax import lax
from jax.experimental import pallas as pl
from jax.experimental.pallas import tpu as pltpu
from jax.sharding import PartitionSpec as P

STEPS = 3
SLOTS = 16
HALF = 16
MODES = 2 * HALF
FIELDS = 9
F32 = jnp.float32
BF16 = jnp.bfloat16

step_size = 0.05
near_weight = 4.0 / 3.0
far_weight = -1.0 / 12.0
centre_weight = -7.5


def turn_series(degree):
    fits = []
    for h in (
        lambda s: np.cos(2 * np.pi * np.sqrt(s)),
        lambda s: np.sinc(2 * np.sqrt(s)) * 2 * np.pi,
    ):
        fit = np.polynomial.chebyshev.Chebyshev.interpolate(h, degree, domain=[0, 0.25])
        fits.append([float(c) for c in fit.convert(kind=np.polynomial.Polynomial).coef])
    return fits


COS_SERIES, SIN_SERIES = turn_series(7)


def horner(series, s):
    total = jnp.full_like(s, series[-1])
    for c in series[-2::-1]:
        total = total * s + c
    return total


def cos_sin_turns(u):
    r = u - jnp.round(u)
    s = r * r
    return horner(COS_SERIES, s), r * horner(SIN_SERIES, s)


def mode_tables():
    a = np.arange(HALF)
    angle = (2 * a + 1) * np.pi / (2 * MODES)
    nodes = np.cos(angle)
    weight = np.zeros((6 * HALF, 6 * HALF))
    for dim in range(3):
        for parity in (0, 1):
            m = 2 * np.arange(HALF) + parity
            block = 4.0 / MODES * np.cos(m[:, None] * angle[None, :])
            if parity == 0:
                block[0] *= 0.5
            at = (parity * 3 + dim) * HALF
            weight[at : at + HALF, at : at + HALF] = block
    column = np.tile(nodes, 3)[:, None] * np.ones((1, 128))
    return weight.astype(np.float32), column.astype(np.float32)


def split2(x):
    high = x.astype(BF16)
    return high, (x - high.astype(F32)).astype(BF16)


def dot_nt(a, b):
    return lax.dot_general(a, b, (((1,), (1,)), ((), ())), preferred_element_type=F32)


def dot_nn(a, b):
    return lax.dot_general(a, b, (((1,), (0,)), ((), ())), preferred_element_type=F32)


def pack_kernel(owner_ref, xyz_ref, offset_ref, wave_ref, freq_ref, amp_ref, index_ref, table_ref, send_ref, comp_ref):
    points = owner_ref.shape[1]
    devices = send_ref.shape[0]
    hit = owner_ref[...] == lax.broadcasted_iota(jnp.int32, (devices, points), 0)
    match = jnp.where(hit, 1.0, 0.0)
    match16 = match.astype(BF16)
    before = (
        lax.broadcasted_iota(jnp.int32, (points, points), 0)
        < lax.broadcasted_iota(jnp.int32, (points, points), 1)
    )
    count = dot_nn(match16, jnp.where(before, 1.0, 0.0).astype(BF16))
    rank = jnp.sum(count * match, axis=0, keepdims=True)
    slot = rank == lax.broadcasted_iota(jnp.int32, (SLOTS, points), 0).astype(F32)
    values = [xyz_ref[i : i + 1, :] for i in range(3)] + [(offset_ref[...] + 1).astype(F32)]
    spread = jnp.concatenate([jnp.where(slot, v, 0.0) for v in values], axis=0)
    first, rest = split2(spread)
    rest = spread - first.astype(F32)
    second, third = split2(rest)
    send_ref[...] = dot_nt(match16, first) + dot_nt(match16, second) + dot_nt(match16, third)
    entries = table_ref.shape[0]
    found = index_ref[...] == lax.broadcasted_iota(jnp.int32, (entries, index_ref.shape[1]), 0)
    phase = jnp.sum(jnp.where(found, table_ref[...], 0.0), axis=0, keepdims=True)
    comp_ref[0:3, :] = wave_ref[...]
    comp_ref[3:4, :] = freq_ref[...]
    comp_ref[4:7, :] = amp_ref[...]
    comp_ref[7:8, :] = phase


def mode_sums(block, weight, column, q_hi, q_lo, p_hi, p_lo):
    width = block.shape[1]
    turn = 1.0 / (2.0 * np.pi)
    angles = jnp.concatenate(
        [column[d * HALF : (d + 1) * HALF, 0:1] * (block[d : d + 1, :] * (2.0 * turn)) for d in range(3)], axis=0
    )
    cosine, sine = cos_sin_turns(angles)
    series = lax.dot_general(
        weight, jnp.concatenate([cosine, sine], axis=0), (((1,), (0,)), ((), ())),
        precision=lax.Precision.HIGHEST, preferred_element_type=F32,
    )
    cx, cy, cz, sx, sy, sz = [series[i * HALF : (i + 1) * HALF, :] for i in range(6)]
    centre = (2.0 * turn) * (block[0:1, :] + block[1:2, :] + block[2:3, :]) + turn * block[7:8, :]
    for n in range(STEPS):
        shift_cos, shift_sin = cos_sin_turns(centre - block[3:4, :] * (turn * step_size * (n + 1)))
        for i in range(3):
            b = block[4 + i : 5 + i, :] * shift_cos
            c = -block[4 + i : 5 + i, :] * shift_sin
            at = (3 * n + i) * MODES
            for which, part, value in ((0, 0, b * cz), (0, 1, c * sz), (1, 0, c * cz), (1, 1, -(b * sz))):
                rows = pl.ds(at + part * HALF, HALF)
                q_hi[which, rows, :], q_lo[which, rows, :] = split2(value)
    for m in range(HALF):
        rows_a, rows_b = pl.ds(m * HALF, HALF), pl.ds((HALF + m) * HALF, HALF)
        x_even, x_odd = cx[m : m + 1, :], sx[m : m + 1, :]
        p_hi[0, rows_a, :], p_lo[0, rows_a, :] = split2(x_even * cy)
        p_hi[0, rows_b, :], p_lo[0, rows_b, :] = split2(-(x_odd * sy))
        p_hi[1, rows_a, :], p_lo[1, rows_a, :] = split2(x_even * sy)
        p_hi[1, rows_b, :], p_lo[1, rows_b, :] = split2(x_odd * cy)


def mode_products(q_hi, q_lo, p_hi, p_lo, which):
    return (
        dot_nt(q_hi[which], p_hi[which]) + dot_nt(q_hi[which], p_lo[which]) + dot_nt(q_lo[which], p_hi[which])
    )


def slot_rows(arrived):
    turned = arrived.T
    return [
        jnp.concatenate([turned[c * SLOTS + r : c * SLOTS + r + 1, :] for r in range(SLOTS)], axis=1)
        for c in range(4)
    ]


def point_modes(rows, t_ref):
    tau = jnp.concatenate([(r - 2.0) * 0.5 for r in rows], axis=0)
    older, old = jnp.ones_like(tau), tau
    for m in range(MODES):
        at = (m % 2) * HALF + m // 2
        for d in range(3):
            t_ref[d, at : at + 1, :] = older[d : d + 1, :]
        older, old = old, 2.0 * tau * old - older


def point_sums(t_ref, lanes, f_hi, f_lo, w_hi, w_lo, v_ref):
    tx, ty, tz = t_ref[0, :, lanes], t_ref[1, :, lanes], t_ref[2, :, lanes]
    half = [slice(0, HALF), slice(HALF, MODES)]
    for combo, (px, py) in enumerate(((0, 0), (1, 1), (0, 1), (1, 0))):
        other = ty[half[py], :]
        for m in range(HALF):
            rows = pl.ds((combo * HALF + m) * HALF, HALF)
            at = px * HALF + m
            w_hi[rows, :], w_lo[rows, :] = split2(tx[at : at + 1, :] * other)
    sums = dot_nn(f_hi[...], w_hi[...]) + dot_nn(f_hi[...], w_lo[...]) + dot_nn(f_lo[...], w_hi[...])
    for j in range(FIELDS):
        v_ref[j : j + 1, lanes] = jnp.sum(sums[j * MODES : (j + 1) * MODES, :] * tz, axis=0, keepdims=True)


def spread_field(v, place, z_hot, cells_xy):
    hit = place == lax.broadcasted_iota(jnp.int32, (cells_xy, place.shape[1]), 0).astype(F32)
    v_hi, v_lo = split2(jnp.where(hit, v, 0.0))
    return dot_nt(v_hi, z_hot) + dot_nt(v_lo, z_hot)


def incident_kernel(got_ref, comps_ref, weight_ref, column_ref, out_ref, q_hi, q_lo, p_hi, p_lo, f_ref, f_hi, f_lo, t_ref, w_hi, w_lo, v_ref, z_hot):
    blocks = comps_ref.shape[0]
    wide = 2 * HALF * HALF

    f_ref[...] = jnp.zeros_like(f_ref)

    def one_block(i, carry):
        mode_sums(comps_ref[i], weight_ref[...], column_ref[...], q_hi, q_lo, p_hi, p_lo)
        for which in (0, 1):
            f_ref[:, which * wide : (which + 1) * wide] += mode_products(q_hi, q_lo, p_hi, p_lo, which)
        return carry

    lax.fori_loop(0, blocks, one_block, 0)
    f_hi[...], f_lo[...] = split2(f_ref[...])
    x, y, z, cell = slot_rows(got_ref[...])
    point_modes([x, y, z], t_ref)
    chunk = w_hi.shape[1]

    def one_chunk(i, carry):
        point_sums(t_ref, pl.ds(pl.multiple_of(i * chunk, chunk), chunk), f_hi, f_lo, w_hi, w_lo, v_ref)
        return carry

    lax.fori_loop(0, t_ref.shape[2] // chunk, one_chunk, 0)
    depth = out_ref.shape[2]
    place = jnp.floor((cell - 1.0) * (1.0 / depth))
    along = (cell - 1.0) - place * depth
    z_hot[...] = jnp.where(
        along == lax.broadcasted_iota(jnp.int32, z_hot.shape, 0).astype(F32), 1.0, 0.0
    ).astype(BF16)

    def one_field(j, carry):
        out_ref[j] = spread_field(v_ref[pl.ds(j, 1), :], place, z_hot[...], out_ref.shape[1])
        return carry

    lax.fori_loop(0, FIELDS, one_field, 0)


def with_halo(block, sides, width):
    for axis, dim in sides:
        count = lax.axis_size(axis)
        forward = [(i, i + 1) for i in range(count - 1)]
        backward = [(target, source) for source, target in forward]
        low = lax.ppermute(lax.slice_in_dim(block, block.shape[dim] - width, None, axis=dim), axis, forward)
        high = lax.ppermute(lax.slice_in_dim(block, 0, width, axis=dim), axis, backward)
        block = jnp.concatenate([low, block, high], axis=dim)
    return block


def shifted(padded, axis_pos, offset):
    result = padded
    for dim_pos in (1, 2, 3):
        first_cell = 2 + offset if dim_pos == axis_pos else 2
        result = lax.slice_in_dim(result, first_cell, first_cell + padded.shape[dim_pos] - 4, axis=dim_pos)
    return result


def laplace_four(padded):
    summed = centre_weight * shifted(padded, 0, 0)
    for axis_pos in (1, 2, 3):
        summed = summed + near_weight * (shifted(padded, axis_pos, 1) + shifted(padded, axis_pos, -1))
        summed = summed + far_weight * (shifted(padded, axis_pos, 2) + shifted(padded, axis_pos, -2))
    return summed


def local(current_field, earlier_field, wave_coef, layer_mask, point_xyz, point_owner, cell_offset, wave_vector, frequency, amplitude, phase_index, phase_table):
    devices = lax.axis_size("slab") * lax.axis_size("comp")
    points = point_xyz.shape[1]
    width = frequency.shape[0]
    weight, column = mode_tables()
    send, own = pl.pallas_call(
        pack_kernel,
        out_shape=(
            jax.ShapeDtypeStruct((devices, 4 * SLOTS), F32),
            jax.ShapeDtypeStruct((8, width), F32),
        ),
        compiler_params=pltpu.CompilerParams(vmem_limit_bytes=48 << 20),
    )(
        point_owner.reshape(1, points), point_xyz, cell_offset.reshape(1, points), wave_vector,
        frequency.reshape(1, width), amplitude, phase_index.reshape(1, width), phase_table.reshape(-1, 1),
    )
    got = lax.all_to_all(send, ("slab", "comp"), split_axis=0, concat_axis=0, tiled=True)
    comps = lax.all_gather(own, "comp", axis=0)
    _, nx, ny, nz = current_field.shape
    modes = 4 * HALF * HALF
    slots = devices * SLOTS
    chunk = 256
    forcing = pl.pallas_call(
        incident_kernel,
        out_shape=jax.ShapeDtypeStruct((FIELDS, nx * ny, nz), F32),
        scratch_shapes=[
            pltpu.VMEM((2, FIELDS * MODES, width), BF16),
            pltpu.VMEM((2, FIELDS * MODES, width), BF16),
            pltpu.VMEM((2, modes // 2, width), BF16),
            pltpu.VMEM((2, modes // 2, width), BF16),
            pltpu.VMEM((FIELDS * MODES, modes), F32),
            pltpu.VMEM((FIELDS * MODES, modes), BF16),
            pltpu.VMEM((FIELDS * MODES, modes), BF16),
            pltpu.VMEM((3, MODES, slots), F32),
            pltpu.VMEM((modes, chunk), BF16),
            pltpu.VMEM((modes, chunk), BF16),
            pltpu.VMEM((FIELDS, slots), F32),
            pltpu.VMEM((nz, slots), BF16),
        ],
        compiler_params=pltpu.CompilerParams(vmem_limit_bytes=48 << 20),
    )(got, comps, jnp.asarray(weight), jnp.asarray(column))
    forcing = forcing.reshape(FIELDS, nx, ny, nz)
    sign_field = ((layer_mask == 1).astype(F32) - (layer_mask == 2).astype(F32))[None]
    current = current_field
    earlier = earlier_field
    for step_index in range(STEPS):
        widened = with_halo(current, (("slab", 1), ("comp", 2)), 2)
        padded = jnp.pad(widened, ((0, 0), (0, 0), (0, 0), (2, 2)))
        source = forcing[3 * step_index : 3 * step_index + 3]
        following = 2.0 * current - earlier + wave_coef[None] * laplace_four(padded) + sign_field * source
        earlier = current
        current = following
    return (current, earlier)


def solution(mesh):
    in_specs = (
        P(None, "slab", "comp", None),
        P(None, "slab", "comp", None),
        P("slab", "comp", None),
        P("slab", "comp", None),
        P(None, ("slab", "comp")),
        P(("slab", "comp"), None),
        P(("slab", "comp")),
        P(None, "comp"),
        P("comp"),
        P(None, "comp"),
        P("comp"),
        P(),
    )
    out_specs = (P(None, "slab", "comp", None), P(None, "slab", "comp", None))
    return jax.shard_map(local, mesh=mesh, in_specs=in_specs, out_specs=out_specs, check_vma=False)
```

```python
import functools

import jax
import jax.numpy as jnp
import numpy as np
from jax import lax
from jax.experimental import pallas as pl
from jax.experimental.pallas import tpu as pltpu
from jax.sharding import PartitionSpec as P

STEPS = 3
SLOTS = 16
HALF = 16
MODES = 2 * HALF
FIELDS = 9
F32 = jnp.float32
BF16 = jnp.bfloat16
MESH = pl.DeviceIdType.MESH

step_size = 0.05
near_weight = 4.0 / 3.0
far_weight = -1.0 / 12.0
centre_weight = -7.5


def turn_series(degree):
    fits = []
    for h in (
        lambda s: np.cos(2 * np.pi * np.sqrt(s)),
        lambda s: np.sinc(2 * np.sqrt(s)) * 2 * np.pi,
    ):
        fit = np.polynomial.chebyshev.Chebyshev.interpolate(h, degree, domain=[0, 0.25])
        fits.append([float(c) for c in fit.convert(kind=np.polynomial.Polynomial).coef])
    return fits


COS_SERIES, SIN_SERIES = turn_series(7)


def horner(series, s):
    total = jnp.full_like(s, series[-1])
    for c in series[-2::-1]:
        total = total * s + c
    return total


def cos_sin_turns(u):
    r = u - jnp.round(u)
    s = r * r
    return horner(COS_SERIES, s), r * horner(SIN_SERIES, s)


def mode_tables():
    a = np.arange(HALF)
    angle = (2 * a + 1) * np.pi / (2 * MODES)
    nodes = np.cos(angle)
    weight = np.zeros((6 * HALF, 6 * HALF))
    for dim in range(3):
        for parity in (0, 1):
            m = 2 * np.arange(HALF) + parity
            block = 4.0 / MODES * np.cos(m[:, None] * angle[None, :])
            if parity == 0:
                block[0] *= 0.5
            at = (parity * 3 + dim) * HALF
            weight[at : at + HALF, at : at + HALF] = block
    column = np.tile(nodes, 3)[:, None] * np.ones((1, 128))
    return weight.astype(np.float32), column.astype(np.float32)


def split2(x):
    high = x.astype(BF16)
    return high, (x - high.astype(F32)).astype(BF16)


def dot_nt(a, b):
    return lax.dot_general(a, b, (((1,), (1,)), ((), ())), preferred_element_type=F32)


def dot_nn(a, b):
    return lax.dot_general(a, b, (((1,), (0,)), ((), ())), preferred_element_type=F32)


def mode_sums(block, weight, column, q_hi, q_lo, p_hi, p_lo):
    width = block.shape[1]
    turn = 1.0 / (2.0 * np.pi)
    angles = jnp.concatenate(
        [column[d * HALF : (d + 1) * HALF, 0:1] * (block[d : d + 1, :] * (2.0 * turn)) for d in range(3)], axis=0
    )
    cosine, sine = cos_sin_turns(angles)
    series = lax.dot_general(
        weight, jnp.concatenate([cosine, sine], axis=0), (((1,), (0,)), ((), ())),
        precision=lax.Precision.HIGHEST, preferred_element_type=F32,
    )
    cx, cy, cz, sx, sy, sz = [series[i * HALF : (i + 1) * HALF, :] for i in range(6)]
    centre = (2.0 * turn) * (block[0:1, :] + block[1:2, :] + block[2:3, :]) + turn * block[7:8, :]
    for n in range(STEPS):
        shift_cos, shift_sin = cos_sin_turns(centre - block[3:4, :] * (turn * step_size * (n + 1)))
        for i in range(3):
            b = block[4 + i : 5 + i, :] * shift_cos
            c = -block[4 + i : 5 + i, :] * shift_sin
            at = (3 * n + i) * MODES
            for which, part, value in ((0, 0, b * cz), (0, 1, c * sz), (1, 0, c * cz), (1, 1, -(b * sz))):
                rows = pl.ds(at + part * HALF, HALF)
                q_hi[which, rows, :], q_lo[which, rows, :] = split2(value)
    for m in range(HALF):
        rows_a, rows_b = pl.ds(m * HALF, HALF), pl.ds((HALF + m) * HALF, HALF)
        x_even, x_odd = cx[m : m + 1, :], sx[m : m + 1, :]
        p_hi[0, rows_a, :], p_lo[0, rows_a, :] = split2(x_even * cy)
        p_hi[0, rows_b, :], p_lo[0, rows_b, :] = split2(-(x_odd * sy))
        p_hi[1, rows_a, :], p_lo[1, rows_a, :] = split2(x_even * sy)
        p_hi[1, rows_b, :], p_lo[1, rows_b, :] = split2(x_odd * cy)


def mode_products(q_hi, q_lo, p_hi, p_lo, which):
    return (
        dot_nt(q_hi[which], p_hi[which]) + dot_nt(q_hi[which], p_lo[which]) + dot_nt(q_lo[which], p_hi[which])
    )


def slot_rows(arrived):
    turned = arrived.T
    return [
        jnp.concatenate([turned[c * SLOTS + r : c * SLOTS + r + 1, :] for r in range(SLOTS)], axis=1)
        for c in range(4)
    ]


def point_modes(rows, t_ref):
    tau = jnp.concatenate([(r - 2.0) * 0.5 for r in rows], axis=0)
    older, old = jnp.ones_like(tau), tau
    for m in range(MODES):
        at = (m % 2) * HALF + m // 2
        for d in range(3):
            t_ref[d, at : at + 1, :] = older[d : d + 1, :]
        older, old = old, 2.0 * tau * old - older


def point_sums(t_ref, lanes, f_hi, f_lo, w_hi, w_lo, v_ref):
    tx, ty, tz = t_ref[0, :, lanes], t_ref[1, :, lanes], t_ref[2, :, lanes]
    half = [slice(0, HALF), slice(HALF, MODES)]
    for combo, (px, py) in enumerate(((0, 0), (1, 1), (0, 1), (1, 0))):
        other = ty[half[py], :]
        for m in range(HALF):
            rows = pl.ds((combo * HALF + m) * HALF, HALF)
            at = px * HALF + m
            w_hi[rows, :], w_lo[rows, :] = split2(tx[at : at + 1, :] * other)
    sums = dot_nn(f_hi[...], w_hi[...]) + dot_nn(f_hi[...], w_lo[...]) + dot_nn(f_lo[...], w_hi[...])
    for j in range(FIELDS):
        v_ref[j : j + 1, lanes] = jnp.sum(sums[j * MODES : (j + 1) * MODES, :] * tz, axis=0, keepdims=True)


def spread_field(v, place, z_hot, cells_xy):
    hit = place == lax.broadcasted_iota(jnp.int32, (cells_xy, place.shape[1]), 0).astype(F32)
    v_hi, v_lo = split2(jnp.where(hit, v, 0.0))
    return dot_nt(v_hi, z_hot) + dot_nt(v_lo, z_hot)


def pack_points(owner, xyz, offset, send, split):
    in_row, in_column, in_group = split
    points = owner.shape[1]
    devices = in_row * in_column * in_group
    c = owner & (in_group - 1)
    slab = owner >> (in_group.bit_length() - 1)
    w, y = slab & (in_row - 1), slab >> (in_row.bit_length() - 1)
    place = (w * in_column + y) * in_group + c
    hit = place == lax.broadcasted_iota(jnp.int32, (devices, points), 0)
    match = jnp.where(hit, 1.0, 0.0)
    match16 = match.astype(BF16)
    before = (
        lax.broadcasted_iota(jnp.int32, (points, points), 0)
        < lax.broadcasted_iota(jnp.int32, (points, points), 1)
    )
    count = dot_nn(match16, jnp.where(before, 1.0, 0.0).astype(BF16))
    rank = jnp.sum(count * match, axis=0, keepdims=True)
    slot = rank == lax.broadcasted_iota(jnp.int32, (SLOTS, points), 0).astype(F32)
    values = [xyz[i : i + 1, :] for i in range(3)] + [(offset + 1).astype(F32)]
    spread = jnp.concatenate([jnp.where(slot, v, 0.0) for v in values], axis=0)
    first = spread.astype(BF16)
    second, third = split2(spread - first.astype(F32))
    rows = dot_nt(match16, first) + dot_nt(match16, second) + dot_nt(match16, third)
    for d in range(devices):
        send[d // (in_column * in_group), d // in_group % in_column, d % in_group] = rows[d : d + 1, :]


def wave_kernel(
    split,
    current_in, earlier_in, coef_in, mask_in, owner_in, xyz_in, offset_in, wave_in, freq_in, amp_in, index_in, table_in,
    weight_in, column_in,
    final_ref, prior_ref,
    held, driven, coef, mask, sign, owner, xyz, offset, wave, freq, amp, index, table, weight, column, load_sem,
    comps, comp_send, comp_recv,
    sent, first, second, third, hop_send, hop_recv, hop_own,
    x_in, y_in, y_out, halo_send, halo_recv,
    q_hi, q_lo, p_hi, p_lo, f_ref, f_hi, f_lo, t_ref, w_hi, w_lo, v_ref, z_hot, forcing,
):
    in_row, in_column, in_group = split
    slabs = in_row * in_column
    slab, comp = lax.axis_index("slab"), lax.axis_index("comp")
    y, w = slab // in_row, slab % in_row
    nx, ny, nz = coef.shape
    after, before = lax.rem(slab + 1, slabs), lax.rem(slab + slabs - 1, slabs)
    right, left = lax.rem(comp + 1, in_group), lax.rem(comp + in_group - 1, in_group)

    def row_at(d):
        return lax.rem(w + d, in_row)

    def column_at(d):
        return lax.rem(y + d, in_column)

    def group_at(d):
        return lax.rem(comp + d, in_group)

    barrier = pltpu.get_barrier_semaphore()
    partners = [(y * in_row + row_at(d), comp) for d in range(1, in_row)]
    partners += [(column_at(d) * in_row + w, comp) for d in range(1, in_column)]
    partners += [(slab, group_at(d)) for d in range(1, in_group)]
    partners += [(after, comp), (before, comp)]
    for partner in partners:
        pl.semaphore_signal(barrier, inc=1, device_id=partner, device_id_type=MESH)

    loads = [
        pltpu.make_async_copy(a, b, load_sem.at[i])
        for i, (a, b) in enumerate((
            (owner_in, owner), (xyz_in, xyz), (offset_in, offset),
            (wave_in, wave), (freq_in, freq), (amp_in, amp), (index_in, index), (table_in, table),
            (current_in, held.at[1]), (column_in, column), (weight_in, weight),
            (coef_in, coef), (earlier_in, held.at[0]), (mask_in, mask),
        ))
    ]
    for load in loads:
        load.start()
    for load in loads[:3]:
        load.wait()
    pack_points(owner[...], xyz[...], offset[...], sent, split)
    for load in loads[3:8]:
        load.wait()
    found = index[...] == lax.broadcasted_iota(jnp.int32, (table.shape[1], index.shape[1]), 0)
    phase = lax.dot_general(
        table[...], jnp.where(found, 1.0, 0.0), (((1,), (0,)), ((), ())),
        precision=lax.Precision.HIGHEST, preferred_element_type=F32,
    )
    comps[0, 0:3, :] = wave[...]
    comps[0, 3:4, :] = freq[...]
    comps[0, 4:7, :] = amp[...]
    comps[0, 7:8, :] = phase
    loads[8].wait()

    def halo_copies(e, u):
        faces = (
            (u.at[:, pl.ds(0, 2)], x_in.at[e, 1], (before, comp)),
            (u.at[:, pl.ds(nx - 2, 2)], x_in.at[e, 0], (after, comp)),
            (y_out.at[e, 0], y_in.at[e, 1], (slab, left)),
            (y_out.at[e, 1], y_in.at[e, 0], (slab, right)),
        )
        return [
            pltpu.make_async_remote_copy(
                src_ref=a, dst_ref=b, send_sem=halo_send.at[e, i], recv_sem=halo_recv.at[e, i],
                device_id=target, device_id_type=MESH,
            )
            for i, (a, b, target) in enumerate(faces)
        ]

    def start_halo(e, u):
        y_out[e, 0] = u[:, :, 0:2, :]
        y_out[e, 1] = u[:, :, ny - 2 : ny, :]
        for copy in halo_copies(e, u):
            copy.start()

    def wait_halo(e, u):
        for copy in halo_copies(e, u):
            copy.wait()

    def comp_copy(d):
        return pltpu.make_async_remote_copy(
            src_ref=comps.at[0], dst_ref=comps.at[d], send_sem=comp_send.at[d], recv_sem=comp_recv.at[d],
            device_id=(slab, group_at(d)), device_id_type=MESH,
        )

    def hop_copies(hop):
        if hop == 0:
            moves = [(sent.at[row_at(d)], first.at[w], (y * in_row + row_at(d), comp)) for d in range(in_row)]
        elif hop == 1:
            moves = [
                (first.at[:, column_at(d)], second.at[y], (column_at(d) * in_row + w, comp)) for d in range(in_column)
            ]
        else:
            moves = [(second.at[:, :, group_at(d)], third.at[comp], (slab, group_at(d))) for d in range(in_group)]
        own = pltpu.make_async_copy(moves[0][0], moves[0][1], hop_own.at[hop])
        return [own] + [
            pltpu.make_async_remote_copy(
                src_ref=a, dst_ref=b, send_sem=hop_send.at[hop, d], recv_sem=hop_recv.at[hop, d],
                device_id=target, device_id_type=MESH,
            )
            for d, (a, b, target) in enumerate(moves) if d > 0
        ]

    def start_hop(hop):
        for copy in hop_copies(hop):
            copy.start()

    def wait_hop(hop):
        for copy in hop_copies(hop):
            copy.wait()

    pl.semaphore_wait(barrier, len(partners))
    for d in range(1, in_group):
        comp_copy(d).start()
    start_hop(0)
    start_halo(0, held.at[1])
    for load in loads[9:]:
        load.wait()
    sign[...] = jnp.where(mask[...] == 1, 1.0, 0.0) - jnp.where(mask[...] == 2, 1.0, 0.0)

    lane = lax.broadcasted_iota(jnp.int32, (ny, nz), 1)

    def advance(e, field, i, source):
        def one(c, carry):
            low, high = x_in[e, 0, c], x_in[e, 1, c]
            low, high = jnp.where(slab > 0, low, 0.0), jnp.where(slab < slabs - 1, high, 0.0)
            planes = [low[0], low[1]] + [field[i + 1, c, x] for x in range(nx)] + [high[0], high[1]]
            for x in range(nx):
                u = planes[x + 2]
                back = jnp.where(comp > 0, y_in[e, 0, c, x], 0.0)
                front = jnp.where(comp < in_group - 1, y_in[e, 1, c, x], 0.0)
                tall = jnp.concatenate([back, u, front], axis=0)
                near = planes[x + 1] + planes[x + 3]
                far = planes[x] + planes[x + 4]
                near = near + (tall[1 : ny + 1] + tall[3 : ny + 3])
                far = far + (tall[0:ny] + tall[4 : ny + 4])
                near = near + jnp.where(lane >= 1, pltpu.roll(u, 1, 1), 0.0)
                near = near + jnp.where(lane < nz - 1, pltpu.roll(u, nz - 1, 1), 0.0)
                far = far + jnp.where(lane >= 2, pltpu.roll(u, 2, 1), 0.0)
                far = far + jnp.where(lane < nz - 2, pltpu.roll(u, nz - 2, 1), 0.0)
                curved = centre_weight * u + near_weight * near + far_weight * far
                following = 2.0 * u - field[i, c, x] + coef[x] * curved
                if source is not None:
                    following = following + source(c, x)
                field[i + 2, c, x] = following
            return carry

        lax.fori_loop(0, 3, one, 0)

    wide = 2 * HALF * HALF
    f_ref[...] = jnp.zeros_like(f_ref)

    def one_block(i, carry):
        @pl.when(i > 0)
        def _():
            comp_copy(i).wait()

        mode_sums(comps[i], weight[...], column[...], q_hi, q_lo, p_hi, p_lo)
        for which in (0, 1):
            f_ref[:, which * wide : (which + 1) * wide] += mode_products(q_hi, q_lo, p_hi, p_lo, which)

        for hop in (0, 1):
            @pl.when(i == hop)
            def _(hop=hop):
                wait_hop(hop)
                start_hop(hop + 1)

        @pl.when(i < STEPS)
        def _():
            wait_halo(i, held.at[i + 1])
            advance(i, held, i, None)

            @pl.when(i < STEPS - 1)
            def _():
                start_halo(i + 1, held.at[i + 2])

        return carry

    lax.fori_loop(0, in_group, one_block, 0)
    f_hi[...], f_lo[...] = split2(f_ref[...])
    wait_hop(2)
    px, py, pz, cell = slot_rows(third[...].reshape(in_group * slabs, 4 * SLOTS))
    point_modes([px, py, pz], t_ref)
    chunk = w_hi.shape[1]

    def one_chunk(i, carry):
        point_sums(t_ref, pl.ds(pl.multiple_of(i * chunk, chunk), chunk), f_hi, f_lo, w_hi, w_lo, v_ref)
        return carry

    lax.fori_loop(0, t_ref.shape[2] // chunk, one_chunk, 0)
    place = jnp.floor((cell - 1.0) * (1.0 / nz))
    along = (cell - 1.0) - place * nz
    z_hot[...] = jnp.where(
        along == lax.broadcasted_iota(jnp.int32, z_hot.shape, 0).astype(F32), 1.0, 0.0
    ).astype(BF16)
    driven[0] = jnp.zeros_like(driven[0])

    def one_step(n, carry):
        def one_field(i, inner):
            j = 3 * n + i
            forcing[i] = spread_field(v_ref[pl.ds(j, 1), :], place, z_hot[...], nx * ny)
            return inner

        lax.fori_loop(0, 3, one_field, 0)

        def source(c, x):
            return sign[x] * forcing[c, x * ny : (x + 1) * ny, :]

        @pl.when(n == 0)
        def _():
            def one(c, inner):
                for x in range(nx):
                    driven[1, c, x] = source(c, x)
                return inner

            lax.fori_loop(0, 3, one, 0)

        @pl.when(n > 0)
        def _():
            wait_halo(STEPS + n - 1, driven.at[n])
            advance(STEPS + n - 1, driven, n - 1, source)

        @pl.when(n < STEPS - 1)
        def _():
            start_halo(STEPS + n, driven.at[n + 1])

        return carry

    lax.fori_loop(0, STEPS, one_step, 0)
    prior_ref[...] = held[STEPS] + driven[STEPS - 1]
    final_ref[...] = held[STEPS + 1] + driven[STEPS]


def local(current_field, earlier_field, wave_coef, layer_mask, point_xyz, point_owner, cell_offset, wave_vector, frequency, amplitude, phase_index, phase_table):
    slabs, in_group = lax.axis_size("slab"), lax.axis_size("comp")
    in_row = min(8, slabs // 2)
    in_column = slabs // in_row
    devices = slabs * in_group
    points = point_xyz.shape[1]
    width = frequency.shape[0]
    _, nx, ny, nz = current_field.shape
    modes = 4 * HALF * HALF
    slots = devices * SLOTS
    chunk = 256
    weight, column = mode_tables()
    field = jax.ShapeDtypeStruct(current_field.shape, F32)
    operands = (
        current_field, earlier_field, wave_coef, layer_mask, point_owner.reshape(1, points), point_xyz,
        cell_offset.reshape(1, points), wave_vector, frequency.reshape(1, width), amplitude,
        phase_index.reshape(1, width), phase_table.reshape(1, -1), jnp.asarray(weight), jnp.asarray(column),
    )
    like = [pltpu.VMEM(a.shape, a.dtype) for a in operands]
    dma = pltpu.SemaphoreType.DMA
    exchanges = 2 * STEPS - 1
    final_field, prior_field = pl.pallas_call(
        functools.partial(wave_kernel, (in_row, in_column, in_group)),
        out_shape=(field, field),
        in_specs=[pl.BlockSpec(memory_space=pl.ANY)] * len(operands),
        out_specs=[pl.BlockSpec(memory_space=pltpu.VMEM)] * 2,
        scratch_shapes=[
            pltpu.VMEM((STEPS + 2, 3, nx, ny, nz), F32),
            pltpu.VMEM((STEPS + 1, 3, nx, ny, nz), F32),
            like[2], like[3], pltpu.VMEM((nx, ny, nz), F32), *like[4:], dma((len(operands),)),
            pltpu.VMEM((in_group, 8, width), F32), dma((in_group,)), dma((in_group,)),
            pltpu.VMEM((in_row, in_column, in_group, 1, 4 * SLOTS), F32),
            pltpu.VMEM((in_row, in_column, in_group, 1, 4 * SLOTS), F32),
            pltpu.VMEM((in_column, in_row, in_group, 1, 4 * SLOTS), F32),
            pltpu.VMEM((in_group, in_column, in_row, 1, 4 * SLOTS), F32),
            dma((3, in_row)), dma((3, in_row)), dma((3,)),
            pltpu.VMEM((exchanges, 2, 3, 2, ny, nz), F32),
            pltpu.VMEM((exchanges, 2, 3, nx, 2, nz), F32),
            pltpu.VMEM((exchanges, 2, 3, nx, 2, nz), F32),
            dma((exchanges, 4)), dma((exchanges, 4)),
            pltpu.VMEM((2, FIELDS * MODES, width), BF16),
            pltpu.VMEM((2, FIELDS * MODES, width), BF16),
            pltpu.VMEM((2, modes // 2, width), BF16),
            pltpu.VMEM((2, modes // 2, width), BF16),
            pltpu.VMEM((FIELDS * MODES, modes), F32),
            pltpu.VMEM((FIELDS * MODES, modes), BF16),
            pltpu.VMEM((FIELDS * MODES, modes), BF16),
            pltpu.VMEM((3, MODES, slots), F32),
            pltpu.VMEM((modes, chunk), BF16),
            pltpu.VMEM((modes, chunk), BF16),
            pltpu.VMEM((FIELDS, slots), F32),
            pltpu.VMEM((nz, slots), BF16),
            pltpu.VMEM((3, nx * ny, nz), F32),
        ],
        compiler_params=pltpu.CompilerParams(
            collective_id=0, has_side_effects=True, vmem_limit_bytes=60 << 20
        ),
    )(*operands)
    return final_field, prior_field


def solution(mesh):
    in_specs = (
        P(None, "slab", "comp", None),
        P(None, "slab", "comp", None),
        P("slab", "comp", None),
        P("slab", "comp", None),
        P(None, ("slab", "comp")),
        P(("slab", "comp"), None),
        P(("slab", "comp")),
        P(None, "comp"),
        P("comp"),
        P(None, "comp"),
        P("comp"),
        P(),
    )
    out_specs = (P(None, "slab", "comp", None), P(None, "slab", "comp", None))
    return jax.shard_map(local, mesh=mesh, in_specs=in_specs, out_specs=out_specs, check_vma=False)
```

```python
import functools

import jax
import jax.numpy as jnp
import numpy as np
from jax import lax
from jax.experimental import pallas as pl
from jax.experimental.pallas import tpu as pltpu
from jax.sharding import PartitionSpec as P

STEPS = 3
SLOTS = 16
HALF = 16
MODES = 2 * HALF
FIELDS = 9
F32 = jnp.float32
BF16 = jnp.bfloat16
MESH = pl.DeviceIdType.MESH

step_size = 0.05
near_weight = 4.0 / 3.0
far_weight = -1.0 / 12.0
centre_weight = -7.5


def turn_series(degree):
    fits = []
    for h in (
        lambda s: np.cos(2 * np.pi * np.sqrt(s)),
        lambda s: np.sinc(2 * np.sqrt(s)) * 2 * np.pi,
    ):
        fit = np.polynomial.chebyshev.Chebyshev.interpolate(h, degree, domain=[0, 0.25])
        fits.append([float(c) for c in fit.convert(kind=np.polynomial.Polynomial).coef])
    return fits


COS_SERIES, SIN_SERIES = turn_series(7)


def horner(series, s):
    total = jnp.full_like(s, series[-1])
    for c in series[-2::-1]:
        total = total * s + c
    return total


def cos_sin_turns(u):
    r = u - jnp.round(u)
    s = r * r
    return horner(COS_SERIES, s), r * horner(SIN_SERIES, s)


def mode_tables():
    a = np.arange(HALF)
    angle = (2 * a + 1) * np.pi / (2 * MODES)
    nodes = np.cos(angle)
    weight = np.zeros((6 * HALF, 6 * HALF))
    for dim in range(3):
        for parity in (0, 1):
            m = 2 * np.arange(HALF) + parity
            block = 4.0 / MODES * np.cos(m[:, None] * angle[None, :])
            if parity == 0:
                block[0] *= 0.5
            at = (parity * 3 + dim) * HALF
            weight[at : at + HALF, at : at + HALF] = block
    column = np.tile(nodes, 3)[:, None] * np.ones((1, 128))
    return weight.astype(np.float32), column.astype(np.float32)


def split2(x):
    high = x.astype(BF16)
    return high, (x - high.astype(F32)).astype(BF16)


def dot_nt(a, b):
    return lax.dot_general(a, b, (((1,), (1,)), ((), ())), preferred_element_type=F32)


def dot_nn(a, b):
    return lax.dot_general(a, b, (((1,), (0,)), ((), ())), preferred_element_type=F32)


def mode_sums(block, weight, column, odd, q, p_hi, p_lo):
    turn = 1.0 / (2.0 * np.pi)
    rows = FIELDS * MODES
    angles = jnp.concatenate(
        [column[d * HALF : (d + 1) * HALF, 0:1] * (block[d : d + 1, :] * (2.0 * turn)) for d in range(3)], axis=0
    )
    cosine, sine = cos_sin_turns(angles)
    series = lax.dot_general(
        weight, jnp.concatenate([cosine, sine], axis=0), (((1,), (0,)), ((), ())),
        precision=lax.Precision.HIGHEST, preferred_element_type=F32,
    )
    cx, cy, cz, sx, sy, sz = [series[i * HALF : (i + 1) * HALF, :] for i in range(6)]
    centre = (2.0 * turn) * (block[0:1, :] + block[1:2, :] + block[2:3, :]) + turn * block[7:8, :]
    for n in range(STEPS):
        shift_cos, shift_sin = cos_sin_turns(centre - block[3:4, :] * (turn * step_size * (n + 1)))
        outer = jnp.where(odd, -shift_sin, shift_cos)
        inner = jnp.where(odd, -shift_cos, -shift_sin)
        for i in range(3):
            amp = block[4 + i : 5 + i, :]
            at = (3 * n + i) * MODES
            for part, value in ((0, (amp * outer) * cz), (1, (amp * inner) * sz)):
                low = at + part * HALF
                q[low : low + HALF, :], q[rows + low : rows + low + HALF, :] = split2(value)
    even_y = jnp.where(odd, sy, cy)
    odd_y = jnp.where(odd, cy, -sy)
    for m in range(HALF):
        rows_a, rows_b = pl.ds(m * HALF, HALF), pl.ds((HALF + m) * HALF, HALF)
        p_hi[rows_a, :], p_lo[rows_a, :] = split2(cx[m : m + 1, :] * even_y)
        p_hi[rows_b, :], p_lo[rows_b, :] = split2(sx[m : m + 1, :] * odd_y)


def mode_products(q, p_hi, p_lo):
    rows = FIELDS * MODES
    both = dot_nt(q[...], p_hi[...])
    return both[:rows] + both[rows:] + dot_nt(q[:rows, :], p_lo[...])


def slot_rows(arrived):
    turned = arrived.T
    return [
        jnp.concatenate([turned[c * SLOTS + r : c * SLOTS + r + 1, :] for r in range(SLOTS)], axis=1)
        for c in range(4)
    ]


def point_modes(rows, t_ref):
    tau = jnp.concatenate([(r - 2.0) * 0.5 for r in rows], axis=0)
    older, old = jnp.ones_like(tau), tau
    for m in range(MODES):
        at = (m % 2) * HALF + m // 2
        for d in range(3):
            t_ref[d, at : at + 1, :] = older[d : d + 1, :]
        older, old = old, 2.0 * tau * old - older


def point_sums(t_ref, lanes, f, w_hi, w_lo, v_ref):
    tx, ty, tz = t_ref[0, :, lanes], t_ref[1, :, lanes], t_ref[2, :, lanes]
    half = [slice(0, HALF), slice(HALF, MODES)]
    for combo, (px, py) in enumerate(((0, 0), (1, 1), (0, 1), (1, 0))):
        other = ty[half[py], :]
        for m in range(HALF):
            rows = pl.ds((combo * HALF + m) * HALF, HALF)
            at = px * HALF + m
            w_hi[rows, :], w_lo[rows, :] = split2(tx[at : at + 1, :] * other)
    count = FIELDS * MODES
    both = dot_nn(f[...], w_hi[...])
    sums = both[:count] + both[count:] + dot_nn(f[:count, :], w_lo[...])
    for j in range(FIELDS):
        v_ref[j // 3, j % 3 : j % 3 + 1, lanes] = jnp.sum(sums[j * MODES : (j + 1) * MODES, :] * tz, axis=0, keepdims=True)


def hot_rows(arrived, cell, xy_hot, z_hot):
    depth = z_hot.shape[1]
    place = jnp.floor((cell - 1.0) * (1.0 / depth))
    xy_hot[...] = jnp.where(
        place == lax.broadcasted_iota(jnp.int32, xy_hot.shape, 0).astype(F32), 1.0, 0.0
    ).astype(BF16)
    sources = arrived.shape[0]
    lane = lax.broadcasted_iota(jnp.int32, (sources, depth), 1).astype(F32)
    for r in range(SLOTS):
        one = arrived[:, 3 * SLOTS + r : 3 * SLOTS + r + 1] - 1.0
        along = one - jnp.floor(one * (1.0 / depth)) * depth
        z_hot[r * sources : (r + 1) * sources, :] = jnp.where(along == lane, 1.0, 0.0).astype(BF16)


def spread_fields(v, xy_hot, z_hot, spread, forcing):
    cells = xy_hot.shape[0]
    v_hi, v_lo = split2(v)
    for i in range(3):
        spread[2 * i * cells : (2 * i + 1) * cells, :] = xy_hot[...] * v_hi[i : i + 1, :]
        spread[(2 * i + 1) * cells : (2 * i + 2) * cells, :] = xy_hot[...] * v_lo[i : i + 1, :]
    total = dot_nn(spread[...], z_hot[...])
    for i in range(3):
        forcing[i] = total[2 * i * cells : (2 * i + 1) * cells] + total[(2 * i + 1) * cells : (2 * i + 2) * cells]


def pack_points(owner, xyz, offset, send, split):
    in_row, in_column, in_group = split
    points = owner.shape[1]
    devices = in_row * in_column * in_group
    c = owner & (in_group - 1)
    slab = owner >> (in_group.bit_length() - 1)
    w, y = slab & (in_row - 1), slab >> (in_row.bit_length() - 1)
    place = (w * in_column + y) * in_group + c
    hit = place == lax.broadcasted_iota(jnp.int32, (devices, points), 0)
    match = jnp.where(hit, 1.0, 0.0)
    match16 = match.astype(BF16)
    before = (
        lax.broadcasted_iota(jnp.int32, (points, points), 0)
        < lax.broadcasted_iota(jnp.int32, (points, points), 1)
    )
    count = dot_nn(match16, jnp.where(before, 1.0, 0.0).astype(BF16))
    rank = jnp.sum(count * match, axis=0, keepdims=True)
    slot = rank == lax.broadcasted_iota(jnp.int32, (SLOTS, points), 0).astype(F32)
    values = [xyz[i : i + 1, :] for i in range(3)] + [(offset + 1).astype(F32)]
    spread = jnp.concatenate([jnp.where(slot, v, 0.0) for v in values], axis=0)
    first = spread.astype(BF16)
    second, third = split2(spread - first.astype(F32))
    rows = dot_nt(match16, first) + dot_nt(match16, second) + dot_nt(match16, third)
    for d in range(devices):
        send[d // (in_column * in_group), d // in_group % in_column, d % in_group] = rows[d : d + 1, :]


def wave_kernel(
    split,
    current_in, earlier_in, coef_in, mask_in, owner_in, xyz_in, offset_in, wave_in, freq_in, amp_in, index_in, table_in,
    weight_in, column_in,
    held_out, driven_out,
    held, driven, coef, mask, sign, owner, xyz, offset, wave, freq, amp, index, table, weight, column, load_sem,
    comps, comp_send, comp_recv,
    sent, first, second, third, hop_send, hop_recv, hop_own,
    x_in, y_in, y_out, halo_send, halo_recv,
    q, p_hi, p_lo, f_ref, f_send, f_recv, f, t_ref, w_hi, w_lo, v_ref, xy_hot, z_hot, spread, forcing, store_sem,
):
    in_row, in_column, in_group = split
    slabs = in_row * in_column
    slab, comp = lax.axis_index("slab"), lax.axis_index("comp")
    y, w = slab // in_row, slab % in_row
    nx, ny, nz = coef.shape
    after, before = lax.rem(slab + 1, slabs), lax.rem(slab + slabs - 1, slabs)
    right, left = lax.rem(comp + 1, in_group), lax.rem(comp + in_group - 1, in_group)

    def row_at(d):
        return lax.rem(w + d, in_row)

    def column_at(d):
        return lax.rem(y + d, in_column)

    def group_at(d):
        return lax.rem(comp + d, in_group)

    barrier = pltpu.get_barrier_semaphore()
    partners = [(y * in_row + row_at(d), comp) for d in range(1, in_row)]
    partners += [(column_at(d) * in_row + w, comp) for d in range(1, in_column)]
    partners += [(slab, group_at(d)) for d in range(1, in_group)]
    partners += [(after, comp), (before, comp)]
    for partner in partners:
        pl.semaphore_signal(barrier, inc=1, device_id=partner, device_id_type=MESH)

    loads = [
        pltpu.make_async_copy(a, b, load_sem.at[i])
        for i, (a, b) in enumerate((
            (owner_in, owner), (xyz_in, xyz), (offset_in, offset),
            (wave_in, wave), (freq_in, freq), (amp_in, amp), (index_in, index), (table_in, table),
            (current_in, held.at[1]), (column_in, column), (weight_in, weight),
            (coef_in, coef), (earlier_in, held.at[0]), (mask_in, mask),
        ))
    ]
    for load in loads:
        load.start()
    for load in loads[:3]:
        load.wait()
    pack_points(owner[...], xyz[...], offset[...], sent, split)
    for load in loads[3:8]:
        load.wait()
    found = index[...] == lax.broadcasted_iota(jnp.int32, (table.shape[1], index.shape[1]), 0)
    phase = lax.dot_general(
        table[...], jnp.where(found, 1.0, 0.0), (((1,), (0,)), ((), ())),
        precision=lax.Precision.HIGHEST, preferred_element_type=F32,
    )
    comps[0, 0:3, :] = wave[...]
    comps[0, 3:4, :] = freq[...]
    comps[0, 4:7, :] = amp[...]
    comps[0, 7:8, :] = phase
    loads[8].wait()

    def halo_copies(e, u):
        faces = (
            (u.at[:, pl.ds(0, 2)], x_in.at[e, 1], (before, comp)),
            (u.at[:, pl.ds(nx - 2, 2)], x_in.at[e, 0], (after, comp)),
            (y_out.at[e, 0], y_in.at[e, 1], (slab, left)),
            (y_out.at[e, 1], y_in.at[e, 0], (slab, right)),
        )
        return [
            pltpu.make_async_remote_copy(
                src_ref=a, dst_ref=b, send_sem=halo_send.at[e, i], recv_sem=halo_recv.at[e, i],
                device_id=target, device_id_type=MESH,
            )
            for i, (a, b, target) in enumerate(faces)
        ]

    def start_halo(e, u):
        y_out[e, 0] = u[:, :, 0:2, :]
        y_out[e, 1] = u[:, :, ny - 2 : ny, :]
        for copy in halo_copies(e, u):
            copy.start()

    def wait_halo(e, u):
        for copy in halo_copies(e, u):
            copy.wait()

    def comp_copy(d):
        return pltpu.make_async_remote_copy(
            src_ref=comps.at[0], dst_ref=comps.at[d], send_sem=comp_send.at[d], recv_sem=comp_recv.at[d],
            device_id=(slab, group_at(d)), device_id_type=MESH,
        )

    def hop_copies(hop):
        if hop == 0:
            moves = [(sent.at[row_at(d)], first.at[w], (y * in_row + row_at(d), comp)) for d in range(in_row)]
        elif hop == 1:
            moves = [
                (first.at[:, column_at(d)], second.at[y], (column_at(d) * in_row + w, comp)) for d in range(in_column)
            ]
        else:
            moves = [(second.at[:, :, group_at(d)], third.at[comp], (slab, group_at(d))) for d in range(in_group)]
        own = pltpu.make_async_copy(moves[0][0], moves[0][1], hop_own.at[hop])
        return [own] + [
            pltpu.make_async_remote_copy(
                src_ref=a, dst_ref=b, send_sem=hop_send.at[hop, d], recv_sem=hop_recv.at[hop, d],
                device_id=target, device_id_type=MESH,
            )
            for d, (a, b, target) in enumerate(moves) if d > 0
        ]

    def start_hop(hop):
        for copy in hop_copies(hop):
            copy.start()

    def wait_hop(hop):
        for copy in hop_copies(hop):
            copy.wait()

    pl.semaphore_wait(barrier, len(partners))
    for d in range(1, in_group):
        comp_copy(d).start()
    start_hop(0)
    start_halo(0, held.at[1])
    for load in loads[9:]:
        load.wait()
    sign[...] = jnp.where(mask[...] == 1, 1.0, 0.0) - jnp.where(mask[...] == 2, 1.0, 0.0)

    lane = lax.broadcasted_iota(jnp.int32, (ny, nz), 1)

    def advance(e, field, i, source):
        def one(c, carry):
            low, high = x_in[e, 0, c], x_in[e, 1, c]
            low, high = jnp.where(slab > 0, low, 0.0), jnp.where(slab < slabs - 1, high, 0.0)
            planes = [low[0], low[1]] + [field[i + 1, c, x] for x in range(nx)] + [high[0], high[1]]
            for x in range(nx):
                u = planes[x + 2]
                back = jnp.where(comp > 0, y_in[e, 0, c, x], 0.0)
                front = jnp.where(comp < in_group - 1, y_in[e, 1, c, x], 0.0)
                tall = jnp.concatenate([back, u, front], axis=0)
                near = planes[x + 1] + planes[x + 3]
                far = planes[x] + planes[x + 4]
                near = near + (tall[1 : ny + 1] + tall[3 : ny + 3])
                far = far + (tall[0:ny] + tall[4 : ny + 4])
                near = near + jnp.where(lane >= 1, pltpu.roll(u, 1, 1), 0.0)
                near = near + jnp.where(lane < nz - 1, pltpu.roll(u, nz - 1, 1), 0.0)
                far = far + jnp.where(lane >= 2, pltpu.roll(u, 2, 1), 0.0)
                far = far + jnp.where(lane < nz - 2, pltpu.roll(u, nz - 2, 1), 0.0)
                curved = centre_weight * u + near_weight * near + far_weight * far
                following = 2.0 * u - field[i, c, x] + coef[x] * curved
                if source is not None:
                    following = following + source(c, x)
                field[i + 2, c, x] = following
            return carry

        lax.fori_loop(0, 3, one, 0)

    wide = 2 * HALF * HALF
    core = lax.rem(comp, 2)
    odd = core == 1
    stores = [
        pltpu.make_async_copy(a, b, store_sem.at[i])
        for i, (a, b) in enumerate((
            (held.at[pl.ds(STEPS, 2)], held_out),
            (driven.at[STEPS - 1], driven_out.at[0]),
            (driven.at[STEPS], driven_out.at[1]),
        ))
    ]
    f_ref[core] = jnp.zeros((FIELDS * MODES, wide), F32)

    def one_block(i, carry):
        @pl.when(i > 0)
        def _():
            comp_copy(i).wait()

        mode_sums(comps[i], weight[...], column[...], odd, q, p_hi, p_lo)
        f_ref[core] += mode_products(q, p_hi, p_lo)

        for hop in (0, 1):
            @pl.when(i == hop)
            def _(hop=hop):
                wait_hop(hop)
                start_hop(hop + 1)

        @pl.when(i < STEPS)
        def _():
            wait_halo(i, held.at[i + 1])
            advance(i, held, i, None)

            @pl.when(i < STEPS - 1)
            def _():
                start_halo(i + 1, held.at[i + 2])

        return carry

    lax.fori_loop(0, in_group, one_block, 0)
    half_copy = pltpu.make_async_remote_copy(
        src_ref=f_ref.at[core], dst_ref=f_ref.at[core], send_sem=f_send, recv_sem=f_recv,
        device_id=(slab, comp + 1 - 2 * core), device_id_type=MESH,
    )
    half_copy.start()
    stores[0].start()
    wait_hop(2)
    arrived = third[...].reshape(in_group * slabs, 4 * SLOTS)
    px, py, pz, cell = slot_rows(arrived)
    point_modes([px, py, pz], t_ref)
    hot_rows(arrived, cell, xy_hot, z_hot)
    half_copy.wait()
    rows = FIELDS * MODES
    for which in (0, 1):
        lanes = pl.ds(which * wide, wide)
        f[:rows, lanes], f[rows:, lanes] = split2(f_ref[which])
    chunk = w_hi.shape[1]

    def one_chunk(i, carry):
        point_sums(t_ref, pl.ds(pl.multiple_of(i * chunk, chunk), chunk), f, w_hi, w_lo, v_ref)
        return carry

    lax.fori_loop(0, t_ref.shape[2] // chunk, one_chunk, 0)
    driven[0] = jnp.zeros_like(driven[0])

    def one_step(n, carry):
        @pl.when(n == STEPS - 1)
        def _():
            stores[1].start()

        spread_fields(v_ref[n], xy_hot, z_hot, spread, forcing)

        def source(c, x):
            return sign[x] * forcing[c, x * ny : (x + 1) * ny, :]

        @pl.when(n == 0)
        def _():
            def one(c, inner):
                for x in range(nx):
                    driven[1, c, x] = source(c, x)
                return inner

            lax.fori_loop(0, 3, one, 0)

        @pl.when(n > 0)
        def _():
            wait_halo(STEPS + n - 1, driven.at[n])
            advance(STEPS + n - 1, driven, n - 1, source)

        @pl.when(n < STEPS - 1)
        def _():
            start_halo(STEPS + n, driven.at[n + 1])

        return carry

    lax.fori_loop(0, STEPS, one_step, 0)
    stores[2].start()
    for store in stores:
        store.wait()


def local(current_field, earlier_field, wave_coef, layer_mask, point_xyz, point_owner, cell_offset, wave_vector, frequency, amplitude, phase_index, phase_table):
    slabs, in_group = lax.axis_size("slab"), lax.axis_size("comp")
    in_row = min(8, slabs // 2)
    in_column = slabs // in_row
    devices = slabs * in_group
    points = point_xyz.shape[1]
    width = frequency.shape[0]
    _, nx, ny, nz = current_field.shape
    modes = 4 * HALF * HALF
    slots = devices * SLOTS
    chunk = 256
    weight, column = mode_tables()
    pair = jax.ShapeDtypeStruct((2, *current_field.shape), F32)
    operands = (
        current_field, earlier_field, wave_coef, layer_mask, point_owner.reshape(1, points), point_xyz,
        cell_offset.reshape(1, points), wave_vector, frequency.reshape(1, width), amplitude,
        phase_index.reshape(1, width), phase_table.reshape(1, -1), jnp.asarray(weight), jnp.asarray(column),
    )
    like = [pltpu.VMEM(a.shape, a.dtype) for a in operands]
    dma = pltpu.SemaphoreType.DMA
    exchanges = 2 * STEPS - 1
    held, driven = pl.pallas_call(
        functools.partial(wave_kernel, (in_row, in_column, in_group)),
        out_shape=(pair, pair),
        in_specs=[pl.BlockSpec(memory_space=pl.ANY)] * len(operands),
        out_specs=[pl.BlockSpec(memory_space=pl.ANY)] * 2,
        scratch_shapes=[
            pltpu.VMEM((STEPS + 2, 3, nx, ny, nz), F32),
            pltpu.VMEM((STEPS + 1, 3, nx, ny, nz), F32),
            like[2], like[3], pltpu.VMEM((nx, ny, nz), F32), *like[4:], dma((len(operands),)),
            pltpu.VMEM((in_group, 8, width), F32), dma((in_group,)), dma((in_group,)),
            pltpu.VMEM((in_row, in_column, in_group, 1, 4 * SLOTS), F32),
            pltpu.VMEM((in_row, in_column, in_group, 1, 4 * SLOTS), F32),
            pltpu.VMEM((in_column, in_row, in_group, 1, 4 * SLOTS), F32),
            pltpu.VMEM((in_group, in_column, in_row, 1, 4 * SLOTS), F32),
            dma((3, in_row)), dma((3, in_row)), dma((3,)),
            pltpu.VMEM((exchanges, 2, 3, 2, ny, nz), F32),
            pltpu.VMEM((exchanges, 2, 3, nx, 2, nz), F32),
            pltpu.VMEM((exchanges, 2, 3, nx, 2, nz), F32),
            dma((exchanges, 4)), dma((exchanges, 4)),
            pltpu.VMEM((2 * FIELDS * MODES, width), BF16),
            pltpu.VMEM((modes // 2, width), BF16),
            pltpu.VMEM((modes // 2, width), BF16),
            pltpu.VMEM((2, FIELDS * MODES, modes // 2), F32), dma, dma,
            pltpu.VMEM((2 * FIELDS * MODES, modes), BF16),
            pltpu.VMEM((3, MODES, slots), F32),
            pltpu.VMEM((modes, chunk), BF16),
            pltpu.VMEM((modes, chunk), BF16),
            pltpu.VMEM((STEPS, 3, slots), F32),
            pltpu.VMEM((nx * ny, slots), BF16),
            pltpu.VMEM((slots, nz), BF16),
            pltpu.VMEM((6 * nx * ny, slots), BF16),
            pltpu.VMEM((3, nx * ny, nz), F32), dma((3,)),
        ],
        compiler_params=pltpu.CompilerParams(
            collective_id=0, has_side_effects=True, vmem_limit_bytes=60 << 20
        ),
    )(*operands)
    return held[1] + driven[1], held[0] + driven[0]


def solution(mesh):
    in_specs = (
        P(None, "slab", "comp", None),
        P(None, "slab", "comp", None),
        P("slab", "comp", None),
        P("slab", "comp", None),
        P(None, ("slab", "comp")),
        P(("slab", "comp"), None),
        P(("slab", "comp")),
        P(None, "comp"),
        P("comp"),
        P(None, "comp"),
        P("comp"),
        P(),
    )
    out_specs = (P(None, "slab", "comp", None), P(None, "slab", "comp", None))
    return jax.shard_map(local, mesh=mesh, in_specs=in_specs, out_specs=out_specs, check_vma=False)
```

```python
import functools

import jax
import jax.numpy as jnp
import numpy as np
from jax import lax
from jax.experimental import pallas as pl
from jax.experimental.pallas import tpu as pltpu
from jax.sharding import PartitionSpec as P

STEPS = 3
SLOTS = 16
HALF = 16
MODES = 2 * HALF
FIELDS = 9
F32 = jnp.float32
BF16 = jnp.bfloat16
MESH = pl.DeviceIdType.MESH

step_size = 0.05
near_weight = 4.0 / 3.0
far_weight = -1.0 / 12.0
centre_weight = -7.5


def turn_series(degree):
    fits = []
    for h in (
        lambda s: np.cos(2 * np.pi * np.sqrt(s)),
        lambda s: np.sinc(2 * np.sqrt(s)) * 2 * np.pi,
    ):
        fit = np.polynomial.chebyshev.Chebyshev.interpolate(h, degree, domain=[0, 0.25])
        fits.append([float(c) for c in fit.convert(kind=np.polynomial.Polynomial).coef])
    return fits


COS_SERIES, SIN_SERIES = turn_series(7)


def horner(series, s):
    total = jnp.full_like(s, series[-1])
    for c in series[-2::-1]:
        total = total * s + c
    return total


def cos_sin_turns(u):
    r = u - jnp.round(u)
    s = r * r
    return horner(COS_SERIES, s), r * horner(SIN_SERIES, s)


def mode_tables():
    a = np.arange(HALF)
    angle = (2 * a + 1) * np.pi / (2 * MODES)
    nodes = np.cos(angle)
    weight = np.zeros((6 * HALF, 6 * HALF))
    for dim in range(3):
        for parity in (0, 1):
            m = 2 * np.arange(HALF) + parity
            block = 4.0 / MODES * np.cos(m[:, None] * angle[None, :])
            if parity == 0:
                block[0] *= 0.5
            at = (parity * 3 + dim) * HALF
            weight[at : at + HALF, at : at + HALF] = block
    column = np.tile(nodes, 3)[:, None] * np.ones((1, 128))
    return weight.astype(np.float32), column.astype(np.float32)


def split2(x):
    high = x.astype(BF16)
    return high, (x - high.astype(F32)).astype(BF16)


def dot_nt(a, b):
    return lax.dot_general(a, b, (((1,), (1,)), ((), ())), preferred_element_type=F32)


def dot_nn(a, b):
    return lax.dot_general(a, b, (((1,), (0,)), ((), ())), preferred_element_type=F32)


def mode_sums(block, weight, column, odd, q, p_hi, p_lo):
    turn = 1.0 / (2.0 * np.pi)
    rows = FIELDS * MODES
    angles = jnp.concatenate(
        [column[d * HALF : (d + 1) * HALF, 0:1] * (block[d : d + 1, :] * (2.0 * turn)) for d in range(3)], axis=0
    )
    cosine, sine = cos_sin_turns(angles)
    series = lax.dot_general(
        weight, jnp.concatenate([cosine, sine], axis=0), (((1,), (0,)), ((), ())),
        precision=lax.Precision.HIGHEST, preferred_element_type=F32,
    )
    cx, cy, cz, sx, sy, sz = [series[i * HALF : (i + 1) * HALF, :] for i in range(6)]
    centre = (2.0 * turn) * (block[0:1, :] + block[1:2, :] + block[2:3, :]) + turn * block[7:8, :]
    for n in range(STEPS):
        shift_cos, shift_sin = cos_sin_turns(centre - block[3:4, :] * (turn * step_size * (n + 1)))
        outer = jnp.where(odd, -shift_sin, shift_cos)
        inner = jnp.where(odd, -shift_cos, -shift_sin)
        for i in range(3):
            amp = block[4 + i : 5 + i, :]
            at = (3 * n + i) * MODES
            for part, value in ((0, (amp * outer) * cz), (1, (amp * inner) * sz)):
                low = at + part * HALF
                q[low : low + HALF, :], q[rows + low : rows + low + HALF, :] = split2(value)
    even_y = jnp.where(odd, sy, cy)
    odd_y = jnp.where(odd, cy, -sy)
    for m in range(HALF):
        rows_a, rows_b = pl.ds(m * HALF, HALF), pl.ds((HALF + m) * HALF, HALF)
        p_hi[rows_a, :], p_lo[rows_a, :] = split2(cx[m : m + 1, :] * even_y)
        p_hi[rows_b, :], p_lo[rows_b, :] = split2(sx[m : m + 1, :] * odd_y)


def mode_products(q, p_hi, p_lo):
    rows = FIELDS * MODES
    both = dot_nt(q[...], p_hi[...])
    return both[:rows] + both[rows:] + dot_nt(q[:rows, :], p_lo[...])


def slot_rows(arrived):
    turned = arrived.T
    return [
        jnp.concatenate([turned[c * SLOTS + r : c * SLOTS + r + 1, :] for r in range(SLOTS)], axis=1)
        for c in range(4)
    ]


def point_modes(rows, t_ref):
    tau = jnp.concatenate([(r - 2.0) * 0.5 for r in rows], axis=0)
    older, old = jnp.ones_like(tau), tau
    for m in range(MODES):
        at = (m % 2) * HALF + m // 2
        for d in range(3):
            t_ref[d, at : at + 1, :] = older[d : d + 1, :]
        older, old = old, 2.0 * tau * old - older


def point_sums(t_ref, lanes, f, w_hi, w_lo, v_ref):
    tx, ty, tz = t_ref[0, :, lanes], t_ref[1, :, lanes], t_ref[2, :, lanes]
    half = [slice(0, HALF), slice(HALF, MODES)]
    for combo, (px, py) in enumerate(((0, 0), (1, 1), (0, 1), (1, 0))):
        other = ty[half[py], :]
        for m in range(HALF):
            rows = pl.ds((combo * HALF + m) * HALF, HALF)
            at = px * HALF + m
            w_hi[rows, :], w_lo[rows, :] = split2(tx[at : at + 1, :] * other)
    count = FIELDS * MODES
    both = dot_nn(f[...], w_hi[...])
    sums = both[:count] + both[count:] + dot_nn(f[:count, :], w_lo[...])
    for j in range(FIELDS):
        v_ref[j // 3, j % 3 : j % 3 + 1, lanes] = jnp.sum(sums[j * MODES : (j + 1) * MODES, :] * tz, axis=0, keepdims=True)


def hot_rows(arrived, cell, xy_hot, z_hot):
    depth = z_hot.shape[1]
    place = jnp.floor((cell - 1.0) * (1.0 / depth))
    xy_hot[...] = jnp.where(
        place == lax.broadcasted_iota(jnp.int32, xy_hot.shape, 0).astype(F32), 1.0, 0.0
    ).astype(BF16)
    sources = arrived.shape[0]
    lane = lax.broadcasted_iota(jnp.int32, (sources, depth), 1).astype(F32)
    for r in range(SLOTS):
        one = arrived[:, 3 * SLOTS + r : 3 * SLOTS + r + 1] - 1.0
        along = one - jnp.floor(one * (1.0 / depth)) * depth
        z_hot[r * sources : (r + 1) * sources, :] = jnp.where(along == lane, 1.0, 0.0).astype(BF16)


def spread_fields(v, xy_hot, z_hot, spread, forcing):
    cells = xy_hot.shape[0]
    v_hi, v_lo = split2(v)
    for i in range(3):
        spread[2 * i * cells : (2 * i + 1) * cells, :] = xy_hot[...] * v_hi[i : i + 1, :]
        spread[(2 * i + 1) * cells : (2 * i + 2) * cells, :] = xy_hot[...] * v_lo[i : i + 1, :]
    total = dot_nn(spread[...], z_hot[...])
    for i in range(3):
        forcing[i] = total[2 * i * cells : (2 * i + 1) * cells] + total[(2 * i + 1) * cells : (2 * i + 2) * cells]


def pack_points(owner, xyz, offset, send, split):
    in_row, in_column, in_group = split
    points = owner.shape[1]
    devices = in_row * in_column * in_group
    c = owner & (in_group - 1)
    slab = owner >> (in_group.bit_length() - 1)
    w, y = slab & (in_row - 1), slab >> (in_row.bit_length() - 1)
    place = (w * in_column + y) * in_group + c
    hit = place == lax.broadcasted_iota(jnp.int32, (devices, points), 0)
    match = jnp.where(hit, 1.0, 0.0)
    match16 = match.astype(BF16)
    before = (
        lax.broadcasted_iota(jnp.int32, (points, points), 0)
        < lax.broadcasted_iota(jnp.int32, (points, points), 1)
    )
    count = dot_nn(match16, jnp.where(before, 1.0, 0.0).astype(BF16))
    rank = jnp.sum(count * match, axis=0, keepdims=True)
    slot = rank == lax.broadcasted_iota(jnp.int32, (SLOTS, points), 0).astype(F32)
    values = [xyz[i : i + 1, :] for i in range(3)] + [(offset + 1).astype(F32)]
    spread = jnp.concatenate([jnp.where(slot, v, 0.0) for v in values], axis=0)
    first = spread.astype(BF16)
    second, third = split2(spread - first.astype(F32))
    rows = dot_nt(match16, first) + dot_nt(match16, second) + dot_nt(match16, third)
    for d in range(devices):
        send[d // (in_column * in_group), d // in_group % in_column, d % in_group] = rows[d : d + 1, :]


def wave_kernel(
    split,
    current_in, earlier_in, coef_in, mask_in, owner_in, xyz_in, offset_in, wave_in, freq_in, amp_in, index_in, table_in,
    weight_in, column_in,
    final_ref, prior_ref,
    held, driven, coef, mask, sign, owner, xyz, offset, wave, freq, amp, index, table, weight, column, load_sem,
    comps, comp_send, comp_recv,
    sent, first, second, third, hop_send, hop_recv, hop_own,
    x_in, y_in, y_out, halo_send, halo_recv,
    q, p_hi, p_lo, f_ref, f_send, f_recv, f, t_ref, w_hi, w_lo, v_ref, xy_hot, z_hot, spread, forcing,
):
    in_row, in_column, in_group = split
    slabs = in_row * in_column
    slab, comp = lax.axis_index("slab"), lax.axis_index("comp")
    y, w = slab // in_row, slab % in_row
    nx, ny, nz = coef.shape
    after, before = lax.rem(slab + 1, slabs), lax.rem(slab + slabs - 1, slabs)
    right, left = lax.rem(comp + 1, in_group), lax.rem(comp + in_group - 1, in_group)

    def row_at(d):
        return lax.rem(w + d, in_row)

    def column_at(d):
        return lax.rem(y + d, in_column)

    def group_at(d):
        return lax.rem(comp + d, in_group)

    barrier = pltpu.get_barrier_semaphore()
    partners = [(y * in_row + row_at(d), comp) for d in range(1, in_row)]
    partners += [(column_at(d) * in_row + w, comp) for d in range(1, in_column)]
    partners += [(slab, group_at(d)) for d in range(1, in_group)]
    partners += [(after, comp), (before, comp)]
    for partner in partners:
        pl.semaphore_signal(barrier, inc=1, device_id=partner, device_id_type=MESH)

    loads = [
        pltpu.make_async_copy(a, b, load_sem.at[i])
        for i, (a, b) in enumerate((
            (owner_in, owner), (xyz_in, xyz), (offset_in, offset),
            (wave_in, wave), (freq_in, freq), (amp_in, amp), (index_in, index), (table_in, table),
            (current_in, held.at[1]), (column_in, column), (weight_in, weight),
            (coef_in, coef), (earlier_in, held.at[0]), (mask_in, mask),
        ))
    ]
    for load in loads:
        load.start()
    for load in loads[:3]:
        load.wait()
    pack_points(owner[...], xyz[...], offset[...], sent, split)
    for load in loads[3:8]:
        load.wait()
    found = index[...] == lax.broadcasted_iota(jnp.int32, (table.shape[1], index.shape[1]), 0)
    phase = lax.dot_general(
        table[...], jnp.where(found, 1.0, 0.0), (((1,), (0,)), ((), ())),
        precision=lax.Precision.HIGHEST, preferred_element_type=F32,
    )
    comps[0, 0:3, :] = wave[...]
    comps[0, 3:4, :] = freq[...]
    comps[0, 4:7, :] = amp[...]
    comps[0, 7:8, :] = phase
    loads[8].wait()

    def halo_copies(e, u):
        faces = (
            (u.at[:, pl.ds(0, 2)], x_in.at[e, 1], (before, comp)),
            (u.at[:, pl.ds(nx - 2, 2)], x_in.at[e, 0], (after, comp)),
            (y_out.at[e, 0], y_in.at[e, 1], (slab, left)),
            (y_out.at[e, 1], y_in.at[e, 0], (slab, right)),
        )
        return [
            pltpu.make_async_remote_copy(
                src_ref=a, dst_ref=b, send_sem=halo_send.at[e, i], recv_sem=halo_recv.at[e, i],
                device_id=target, device_id_type=MESH,
            )
            for i, (a, b, target) in enumerate(faces)
        ]

    def start_halo(e, u):
        y_out[e, 0] = u[:, :, 0:2, :]
        y_out[e, 1] = u[:, :, ny - 2 : ny, :]
        for copy in halo_copies(e, u):
            copy.start()

    def wait_halo(e, u):
        for copy in halo_copies(e, u):
            copy.wait()

    def comp_copy(d):
        return pltpu.make_async_remote_copy(
            src_ref=comps.at[0], dst_ref=comps.at[d], send_sem=comp_send.at[d], recv_sem=comp_recv.at[d],
            device_id=(slab, group_at(d)), device_id_type=MESH,
        )

    def hop_copies(hop):
        if hop == 0:
            moves = [(sent.at[row_at(d)], first.at[w], (y * in_row + row_at(d), comp)) for d in range(in_row)]
        elif hop == 1:
            moves = [
                (first.at[:, column_at(d)], second.at[y], (column_at(d) * in_row + w, comp)) for d in range(in_column)
            ]
        else:
            moves = [(second.at[:, :, group_at(d)], third.at[comp], (slab, group_at(d))) for d in range(in_group)]
        own = pltpu.make_async_copy(moves[0][0], moves[0][1], hop_own.at[hop])
        return [own] + [
            pltpu.make_async_remote_copy(
                src_ref=a, dst_ref=b, send_sem=hop_send.at[hop, d], recv_sem=hop_recv.at[hop, d],
                device_id=target, device_id_type=MESH,
            )
            for d, (a, b, target) in enumerate(moves) if d > 0
        ]

    def start_hop(hop):
        for copy in hop_copies(hop):
            copy.start()

    def wait_hop(hop):
        for copy in hop_copies(hop):
            copy.wait()

    pl.semaphore_wait(barrier, len(partners))
    for d in range(1, in_group):
        comp_copy(d).start()
    start_hop(0)
    start_halo(0, held.at[1])
    for load in loads[9:]:
        load.wait()
    sign[...] = jnp.where(mask[...] == 1, 1.0, 0.0) - jnp.where(mask[...] == 2, 1.0, 0.0)

    lane = lax.broadcasted_iota(jnp.int32, (ny, nz), 1)

    def advance(e, field, i, source):
        def one(c, carry):
            low, high = x_in[e, 0, c], x_in[e, 1, c]
            low, high = jnp.where(slab > 0, low, 0.0), jnp.where(slab < slabs - 1, high, 0.0)
            planes = [low[0], low[1]] + [field[i + 1, c, x] for x in range(nx)] + [high[0], high[1]]
            for x in range(nx):
                u = planes[x + 2]
                back = jnp.where(comp > 0, y_in[e, 0, c, x], 0.0)
                front = jnp.where(comp < in_group - 1, y_in[e, 1, c, x], 0.0)
                tall = jnp.concatenate([back, u, front], axis=0)
                near = planes[x + 1] + planes[x + 3]
                far = planes[x] + planes[x + 4]
                near = near + (tall[1 : ny + 1] + tall[3 : ny + 3])
                far = far + (tall[0:ny] + tall[4 : ny + 4])
                near = near + jnp.where(lane >= 1, pltpu.roll(u, 1, 1), 0.0)
                near = near + jnp.where(lane < nz - 1, pltpu.roll(u, nz - 1, 1), 0.0)
                far = far + jnp.where(lane >= 2, pltpu.roll(u, 2, 1), 0.0)
                far = far + jnp.where(lane < nz - 2, pltpu.roll(u, nz - 2, 1), 0.0)
                curved = centre_weight * u + near_weight * near + far_weight * far
                following = 2.0 * u - field[i, c, x] + coef[x] * curved
                if source is not None:
                    following = following + source(c, x)
                field[i + 2, c, x] = following
            return carry

        lax.fori_loop(0, 3, one, 0)

    wide = 2 * HALF * HALF
    core = lax.rem(comp, 2)
    odd = core == 1
    f_ref[core] = jnp.zeros((FIELDS * MODES, wide), F32)

    def one_block(i, carry):
        @pl.when(i > 0)
        def _():
            comp_copy(i).wait()

        mode_sums(comps[i], weight[...], column[...], odd, q, p_hi, p_lo)
        f_ref[core] += mode_products(q, p_hi, p_lo)

        for hop in (0, 1):
            @pl.when(i == 2 * hop + 1)
            def _(hop=hop):
                wait_hop(hop)
                start_hop(hop + 1)

        @pl.when(i == 2)
        def _():
            wait_halo(0, held.at[1])
            advance(0, held, 0, None)
            start_halo(1, held.at[2])

        return carry

    lax.fori_loop(0, in_group, one_block, 0)
    half_copy = pltpu.make_async_remote_copy(
        src_ref=f_ref.at[core], dst_ref=f_ref.at[core], send_sem=f_send, recv_sem=f_recv,
        device_id=(slab, comp + 1 - 2 * core), device_id_type=MESH,
    )
    half_copy.start()
    wait_hop(2)
    arrived = third[...].reshape(in_group * slabs, 4 * SLOTS)
    px, py, pz, cell = slot_rows(arrived)
    point_modes([px, py, pz], t_ref)
    hot_rows(arrived, cell, xy_hot, z_hot)
    half_copy.wait()
    rows = FIELDS * MODES
    for which in (0, 1):
        lanes = pl.ds(which * wide, wide)
        f[:rows, lanes], f[rows:, lanes] = split2(f_ref[which])
    chunk = w_hi.shape[1]

    def one_chunk(i, carry):
        point_sums(t_ref, pl.ds(pl.multiple_of(i * chunk, chunk), chunk), f, w_hi, w_lo, v_ref)
        return carry

    lax.fori_loop(0, t_ref.shape[2] // chunk, one_chunk, 0)
    driven[0] = jnp.zeros_like(driven[0])

    def one_step(n, carry):
        @pl.when(n == STEPS - 1)
        def _():
            prior_ref[...] = held[STEPS] + driven[STEPS - 1]

        spread_fields(v_ref[n], xy_hot, z_hot, spread, forcing)

        def source(c, x):
            return sign[x] * forcing[c, x * ny : (x + 1) * ny, :]

        @pl.when(n == 0)
        def _():
            def one(c, inner):
                for x in range(nx):
                    driven[1, c, x] = source(c, x)
                return inner

            lax.fori_loop(0, 3, one, 0)

        @pl.when(n > 0)
        def _():
            wait_halo(STEPS + n - 1, driven.at[n])
            advance(STEPS + n - 1, driven, n - 1, source)

        @pl.when(n < STEPS - 1)
        def _():
            start_halo(STEPS + n, driven.at[n + 1])
            wait_halo(n + 1, held.at[n + 2])
            advance(n + 1, held, n + 1, None)

            @pl.when(n < STEPS - 2)
            def _():
                start_halo(n + 2, held.at[n + 3])

        return carry

    lax.fori_loop(0, STEPS, one_step, 0)
    final_ref[...] = held[STEPS + 1] + driven[STEPS]


def local(current_field, earlier_field, wave_coef, layer_mask, point_xyz, point_owner, cell_offset, wave_vector, frequency, amplitude, phase_index, phase_table):
    slabs, in_group = lax.axis_size("slab"), lax.axis_size("comp")
    in_row = min(8, slabs // 2)
    in_column = slabs // in_row
    devices = slabs * in_group
    points = point_xyz.shape[1]
    width = frequency.shape[0]
    _, nx, ny, nz = current_field.shape
    modes = 4 * HALF * HALF
    slots = devices * SLOTS
    chunk = 256
    weight, column = mode_tables()
    field = pltpu.VMEM(current_field.shape, F32)
    operands = (
        current_field, earlier_field, wave_coef, layer_mask, point_owner.reshape(1, points), point_xyz,
        cell_offset.reshape(1, points), wave_vector, frequency.reshape(1, width), amplitude,
        phase_index.reshape(1, width), phase_table.reshape(1, -1), jnp.asarray(weight), jnp.asarray(column),
    )
    like = [pltpu.VMEM(a.shape, a.dtype) for a in operands]
    dma = pltpu.SemaphoreType.DMA
    exchanges = 2 * STEPS - 1
    final_field, prior_field = pl.pallas_call(
        functools.partial(wave_kernel, (in_row, in_column, in_group)),
        out_shape=(field, field),
        in_specs=[pl.BlockSpec(memory_space=pl.ANY)] * len(operands),
        out_specs=[pl.BlockSpec(memory_space=pltpu.VMEM)] * 2,
        scratch_shapes=[
            pltpu.VMEM((STEPS + 2, 3, nx, ny, nz), F32),
            pltpu.VMEM((STEPS + 1, 3, nx, ny, nz), F32),
            like[2], like[3], pltpu.VMEM((nx, ny, nz), F32), *like[4:], dma((len(operands),)),
            pltpu.VMEM((in_group, 8, width), F32), dma((in_group,)), dma((in_group,)),
            pltpu.VMEM((in_row, in_column, in_group, 1, 4 * SLOTS), F32),
            pltpu.VMEM((in_row, in_column, in_group, 1, 4 * SLOTS), F32),
            pltpu.VMEM((in_column, in_row, in_group, 1, 4 * SLOTS), F32),
            pltpu.VMEM((in_group, in_column, in_row, 1, 4 * SLOTS), F32),
            dma((3, in_row)), dma((3, in_row)), dma((3,)),
            pltpu.VMEM((exchanges, 2, 3, 2, ny, nz), F32),
            pltpu.VMEM((exchanges, 2, 3, nx, 2, nz), F32),
            pltpu.VMEM((exchanges, 2, 3, nx, 2, nz), F32),
            dma((exchanges, 4)), dma((exchanges, 4)),
            pltpu.VMEM((2 * FIELDS * MODES, width), BF16),
            pltpu.VMEM((modes // 2, width), BF16),
            pltpu.VMEM((modes // 2, width), BF16),
            pltpu.VMEM((2, FIELDS * MODES, modes // 2), F32), dma, dma,
            pltpu.VMEM((2 * FIELDS * MODES, modes), BF16),
            pltpu.VMEM((3, MODES, slots), F32),
            pltpu.VMEM((modes, chunk), BF16),
            pltpu.VMEM((modes, chunk), BF16),
            pltpu.VMEM((STEPS, 3, slots), F32),
            pltpu.VMEM((nx * ny, slots), BF16),
            pltpu.VMEM((slots, nz), BF16),
            pltpu.VMEM((6 * nx * ny, slots), BF16),
            pltpu.VMEM((3, nx * ny, nz), F32),
        ],
        compiler_params=pltpu.CompilerParams(
            collective_id=0, has_side_effects=True, vmem_limit_bytes=60400 << 10
        ),
    )(*operands)
    return final_field, prior_field


def solution(mesh):
    in_specs = (
        P(None, "slab", "comp", None),
        P(None, "slab", "comp", None),
        P("slab", "comp", None),
        P("slab", "comp", None),
        P(None, ("slab", "comp")),
        P(("slab", "comp"), None),
        P(("slab", "comp")),
        P(None, "comp"),
        P("comp"),
        P(None, "comp"),
        P("comp"),
        P(),
    )
    out_specs = (P(None, "slab", "comp", None), P(None, "slab", "comp", None))
    return jax.shard_map(local, mesh=mesh, in_specs=in_specs, out_specs=out_specs, check_vma=False)
```

```python
import functools

import jax
import jax.numpy as jnp
import numpy as np
from jax import lax
from jax.experimental import pallas as pl
from jax.experimental.pallas import tpu as pltpu
from jax.sharding import PartitionSpec as P

STEPS = 3
SLOTS = 16
HALF = 16
MODES = 2 * HALF
FIELDS = 9
F32 = jnp.float32
BF16 = jnp.bfloat16
MESH = pl.DeviceIdType.MESH

step_size = 0.05
near_weight = 4.0 / 3.0
far_weight = -1.0 / 12.0
centre_weight = -7.5


def turn_series(degree):
    fits = []
    for h in (
        lambda s: np.cos(2 * np.pi * np.sqrt(s)),
        lambda s: np.sinc(2 * np.sqrt(s)) * 2 * np.pi,
    ):
        fit = np.polynomial.chebyshev.Chebyshev.interpolate(h, degree, domain=[0, 0.25])
        fits.append([float(c) for c in fit.convert(kind=np.polynomial.Polynomial).coef])
    return fits


COS_SERIES, SIN_SERIES = turn_series(7)


def horner(series, s):
    total = jnp.full_like(s, series[-1])
    for c in series[-2::-1]:
        total = total * s + c
    return total


def cos_sin_turns(u):
    r = u - jnp.round(u)
    s = r * r
    return horner(COS_SERIES, s), r * horner(SIN_SERIES, s)


def mode_tables():
    a = np.arange(HALF)
    angle = (2 * a + 1) * np.pi / (2 * MODES)
    nodes = np.cos(angle)
    weight = np.zeros((6 * HALF, 6 * HALF))
    for dim in range(3):
        for parity in (0, 1):
            m = 2 * np.arange(HALF) + parity
            block = 4.0 / MODES * np.cos(m[:, None] * angle[None, :])
            if parity == 0:
                block[0] *= 0.5
            at = (parity * 3 + dim) * HALF
            weight[at : at + HALF, at : at + HALF] = block
    column = np.tile(nodes, 3)[:, None] * np.ones((1, 128))
    return weight.astype(np.float32), column.astype(np.float32)


def split2(x):
    high = x.astype(BF16)
    return high, (x - high.astype(F32)).astype(BF16)


def dot_nt(a, b):
    return lax.dot_general(a, b, (((1,), (1,)), ((), ())), preferred_element_type=F32)


def dot_nn(a, b):
    return lax.dot_general(a, b, (((1,), (0,)), ((), ())), preferred_element_type=F32)


def mode_sums(block, weight, column, odd, q, p_hi, p_lo):
    turn = 1.0 / (2.0 * np.pi)
    rows = FIELDS * MODES
    angles = jnp.concatenate(
        [column[d * HALF : (d + 1) * HALF, 0:1] * (block[d : d + 1, :] * (2.0 * turn)) for d in range(3)], axis=0
    )
    cosine, sine = cos_sin_turns(angles)
    series = lax.dot_general(
        weight, jnp.concatenate([cosine, sine], axis=0), (((1,), (0,)), ((), ())),
        precision=lax.Precision.HIGHEST, preferred_element_type=F32,
    )
    cx, cy, cz, sx, sy, sz = [series[i * HALF : (i + 1) * HALF, :] for i in range(6)]
    centre = (2.0 * turn) * (block[0:1, :] + block[1:2, :] + block[2:3, :]) + turn * block[7:8, :]
    for n in range(STEPS):
        shift_cos, shift_sin = cos_sin_turns(centre - block[3:4, :] * (turn * step_size * (n + 1)))
        outer = jnp.where(odd, -shift_sin, shift_cos)
        inner = jnp.where(odd, -shift_cos, -shift_sin)
        for i in range(3):
            amp = block[4 + i : 5 + i, :]
            at = (3 * n + i) * MODES
            for part, value in ((0, (amp * outer) * cz), (1, (amp * inner) * sz)):
                low = at + part * HALF
                q[low : low + HALF, :], q[rows + low : rows + low + HALF, :] = split2(value)
    even_y = jnp.where(odd, sy, cy)
    odd_y = jnp.where(odd, cy, -sy)
    for m in range(HALF):
        rows_a, rows_b = pl.ds(m * HALF, HALF), pl.ds((HALF + m) * HALF, HALF)
        p_hi[rows_a, :], p_lo[rows_a, :] = split2(cx[m : m + 1, :] * even_y)
        p_hi[rows_b, :], p_lo[rows_b, :] = split2(sx[m : m + 1, :] * odd_y)


def mode_products(q, p_hi, p_lo):
    rows = FIELDS * MODES
    both = dot_nt(q[...], p_hi[...])
    return both[:rows] + both[rows:] + dot_nt(q[:rows, :], p_lo[...])


def slot_rows(arrived):
    turned = arrived.T
    return [
        jnp.concatenate([turned[c * SLOTS + r : c * SLOTS + r + 1, :] for r in range(SLOTS)], axis=1)
        for c in range(4)
    ]


def point_modes(rows, t_ref):
    tau = jnp.concatenate([(r - 2.0) * 0.5 for r in rows], axis=0)
    older, old = jnp.ones_like(tau), tau
    for m in range(MODES):
        at = (m % 2) * HALF + m // 2
        for d in range(3):
            t_ref[d, at : at + 1, :] = older[d : d + 1, :]
        older, old = old, 2.0 * tau * old - older


def point_products(t_ref, lanes, w_hi, w_lo):
    tx, ty = t_ref[0, :, lanes], t_ref[1, :, lanes]
    half = [slice(0, HALF), slice(HALF, MODES)]
    for combo, (px, py) in enumerate(((0, 0), (1, 1), (0, 1), (1, 0))):
        other = ty[half[py], :]
        for m in range(HALF):
            rows = pl.ds((combo * HALF + m) * HALF, HALF)
            at = px * HALF + m
            w_hi[rows, lanes], w_lo[rows, lanes] = split2(tx[at : at + 1, :] * other)


def point_sums(n, t_ref, lanes, f, w_hi, w_lo, v_ref):
    tz = t_ref[2, :, lanes]
    count = 3 * MODES
    both = dot_nn(f[n], w_hi[:, lanes])
    sums = both[:count] + both[count:] + dot_nn(f[n, :count, :], w_lo[:, lanes])
    for i in range(3):
        v_ref[n, i : i + 1, lanes] = jnp.sum(sums[i * MODES : (i + 1) * MODES, :] * tz, axis=0, keepdims=True)


def hot_rows(arrived, cell, xy_hot, z_hot):
    depth = z_hot.shape[1]
    place = jnp.floor((cell - 1.0) * (1.0 / depth))
    xy_hot[...] = jnp.where(
        place == lax.broadcasted_iota(jnp.int32, xy_hot.shape, 0).astype(F32), 1.0, 0.0
    ).astype(BF16)
    sources = arrived.shape[0]
    lane = lax.broadcasted_iota(jnp.int32, (sources, depth), 1).astype(F32)
    for r in range(SLOTS):
        one = arrived[:, 3 * SLOTS + r : 3 * SLOTS + r + 1] - 1.0
        along = one - jnp.floor(one * (1.0 / depth)) * depth
        z_hot[r * sources : (r + 1) * sources, :] = jnp.where(along == lane, 1.0, 0.0).astype(BF16)


def spread_fields(v, xy_hot, z_hot, spread, forcing):
    cells = xy_hot.shape[0]
    v_hi, v_lo = split2(v)
    for i in range(3):
        spread[2 * i * cells : (2 * i + 1) * cells, :] = xy_hot[...] * v_hi[i : i + 1, :]
        spread[(2 * i + 1) * cells : (2 * i + 2) * cells, :] = xy_hot[...] * v_lo[i : i + 1, :]
    total = dot_nn(spread[...], z_hot[...])
    for i in range(3):
        forcing[i] = total[2 * i * cells : (2 * i + 1) * cells] + total[(2 * i + 1) * cells : (2 * i + 2) * cells]


def pack_points(owner, xyz, offset, send, split):
    in_x, in_z, in_y, in_group = split
    points = owner.shape[1]
    devices = in_x * in_z * in_y * in_group
    bits = [n.bit_length() - 1 for n in (in_group, in_x, in_z)]
    c = owner & (in_group - 1)
    x = (owner >> bits[0]) & (in_x - 1)
    z = (owner >> (bits[0] + bits[1])) & (in_z - 1)
    y = owner >> (bits[0] + bits[1] + bits[2])
    place = ((y * in_x + x) * in_z + z) * in_group + c
    hit = place == lax.broadcasted_iota(jnp.int32, (devices, points), 0)
    match = jnp.where(hit, 1.0, 0.0)
    match16 = match.astype(BF16)
    run = min(points, 128)
    rows, columns = (lax.broadcasted_iota(jnp.int32, (run, 2 * run), d) for d in (0, 1))
    before = jnp.where((rows < columns) | (columns >= run), 1.0, 0.0).astype(BF16)
    offset_in = jnp.zeros((devices, run), F32)
    ranks = []
    for at in range(0, points, run):
        sums = dot_nn(match16[:, at : at + run], before)
        ranks.append(jnp.sum((sums[:, :run] + offset_in) * match[:, at : at + run], axis=0, keepdims=True))
        offset_in = offset_in + sums[:, run:]
    rank = jnp.concatenate(ranks, axis=1)
    slot = rank == lax.broadcasted_iota(jnp.int32, (SLOTS, points), 0).astype(F32)
    values = [xyz[i : i + 1, :] for i in range(3)] + [(offset + 1).astype(F32)]
    spread = jnp.concatenate([jnp.where(slot, v, 0.0) for v in values], axis=0)
    first = spread.astype(BF16)
    second, third = split2(spread - first.astype(F32))
    rows = dot_nt(match16, first) + dot_nt(match16, second) + dot_nt(match16, third)
    inner = in_z * in_group
    for d in range(devices):
        send[d // inner, d % inner] = rows[d : d + 1, :]


def wave_kernel(
    split,
    current_in, earlier_in, coef_in, mask_in, owner_in, xyz_in, offset_in, wave_in, freq_in, amp_in, index_in, table_in,
    weight_in, column_in,
    held, driven,
    coef, mask, sign, owner, xyz, offset, wave, freq, amp, index, table, weight, column, load_sem,
    comps, comp_send, comp_recv,
    sent, first, second, hop_send, hop_recv, hop_own,
    x_in, y_in, y_out, halo_send, halo_recv,
    q, p_hi, p_lo, f_ref, f_send, f_recv, f, t_ref, w_hi, w_lo, v_ref, xy_hot, z_hot, spread, forcing,
):
    in_x, in_z, in_y, in_group = split
    slabs = in_x * in_z * in_y
    slab, comp = lax.axis_index("slab"), lax.axis_index("comp")
    x, z, y = slab % in_x, slab // in_x % in_z, slab // (in_x * in_z)
    nx, ny, nz = coef.shape
    after, before = lax.rem(slab + 1, slabs), lax.rem(slab + slabs - 1, slabs)
    right, left = lax.rem(comp + 1, in_group), lax.rem(comp + in_group - 1, in_group)
    outer, inner = y * in_x + x, z * in_group + comp
    outers, inners = in_y * in_x, in_z * in_group

    def outer_at(d):
        there = lax.rem(outer + d, outers)
        return there, ((there // in_x * in_z + z) * in_x + there % in_x, comp)

    def inner_at(d):
        there = lax.rem(inner + d, inners)
        return there, ((y * in_z + there // in_group) * in_x + x, there % in_group)

    def group_at(d):
        return lax.rem(comp + d, in_group)

    barrier = pltpu.get_barrier_semaphore()
    partners = [outer_at(d)[1] for d in range(1, outers)]
    partners += [inner_at(d)[1] for d in range(1, inners)]
    partners += [(after, comp), (before, comp)]
    for partner in partners:
        pl.semaphore_signal(barrier, inc=1, device_id=partner, device_id_type=MESH)

    loads = [
        pltpu.make_async_copy(a, b, load_sem.at[i])
        for i, (a, b) in enumerate((
            (owner_in, owner), (xyz_in, xyz), (offset_in, offset),
            (wave_in, wave), (freq_in, freq), (amp_in, amp), (index_in, index), (table_in, table),
            (current_in, held.at[1]), (column_in, column), (weight_in, weight),
            (coef_in, coef), (earlier_in, held.at[0]), (mask_in, mask),
        ))
    ]
    for load in loads:
        load.start()
    for load in loads[:3]:
        load.wait()
    pack_points(owner[...], xyz[...], offset[...], sent, split)
    for load in loads[3:8]:
        load.wait()
    found = index[...] == lax.broadcasted_iota(jnp.int32, (table.shape[1], index.shape[1]), 0)
    phase = lax.dot_general(
        table[...], jnp.where(found, 1.0, 0.0), (((1,), (0,)), ((), ())),
        precision=lax.Precision.HIGHEST, preferred_element_type=F32,
    )
    comps[0, 0:3, :] = wave[...]
    comps[0, 3:4, :] = freq[...]
    comps[0, 4:7, :] = amp[...]
    comps[0, 7:8, :] = phase
    loads[8].wait()

    def halo_copies(e, u):
        faces = (
            (u.at[:, pl.ds(0, 2)], x_in.at[e, 1], (before, comp)),
            (u.at[:, pl.ds(nx - 2, 2)], x_in.at[e, 0], (after, comp)),
            (y_out.at[e, 0], y_in.at[e, 1], (slab, left)),
            (y_out.at[e, 1], y_in.at[e, 0], (slab, right)),
        )
        return [
            pltpu.make_async_remote_copy(
                src_ref=a, dst_ref=b, send_sem=halo_send.at[e, i], recv_sem=halo_recv.at[e, i],
                device_id=target, device_id_type=MESH,
            )
            for i, (a, b, target) in enumerate(faces)
        ]

    def start_halo(e, u):
        y_out[e, 0] = u[:, :, 0:2, :]
        y_out[e, 1] = u[:, :, ny - 2 : ny, :]
        for copy in halo_copies(e, u):
            copy.start()

    def wait_halo(e, u):
        for copy in halo_copies(e, u):
            copy.wait()

    def comp_copy(d):
        return pltpu.make_async_remote_copy(
            src_ref=comps.at[0], dst_ref=comps.at[d], send_sem=comp_send.at[d], recv_sem=comp_recv.at[d],
            device_id=(slab, group_at(d)), device_id_type=MESH,
        )

    def hop_copies(hop):
        if hop == 0:
            moves = [(sent.at[outer_at(d)[0]], first.at[outer], outer_at(d)[1]) for d in range(outers)]
        else:
            moves = [(first.at[:, inner_at(d)[0]], second.at[inner], inner_at(d)[1]) for d in range(inners)]
        own = pltpu.make_async_copy(moves[0][0], moves[0][1], hop_own.at[hop])
        return [own] + [
            pltpu.make_async_remote_copy(
                src_ref=a, dst_ref=b, send_sem=hop_send.at[hop, d], recv_sem=hop_recv.at[hop, d],
                device_id=target, device_id_type=MESH,
            )
            for d, (a, b, target) in enumerate(moves) if d > 0
        ]

    def start_hop(hop):
        for copy in hop_copies(hop):
            copy.start()

    def wait_hop(hop):
        for copy in hop_copies(hop):
            copy.wait()

    pl.semaphore_wait(barrier, len(partners))
    start_hop(0)
    for d in range(1, in_group):
        comp_copy(d).start()
    start_halo(0, held.at[1])
    for load in loads[9:]:
        load.wait()
    sign[...] = jnp.where(mask[...] == 1, 1.0, 0.0) - jnp.where(mask[...] == 2, 1.0, 0.0)

    lane = lax.broadcasted_iota(jnp.int32, (ny, nz), 1)

    def advance(e, field, i, source):
        def one(c, carry):
            low, high = x_in[e, 0, c], x_in[e, 1, c]
            low, high = jnp.where(slab > 0, low, 0.0), jnp.where(slab < slabs - 1, high, 0.0)
            planes = [low[0], low[1]] + [field[i + 1, c, x] for x in range(nx)] + [high[0], high[1]]
            for x in range(nx):
                u = planes[x + 2]
                back = jnp.where(comp > 0, y_in[e, 0, c, x], 0.0)
                front = jnp.where(comp < in_group - 1, y_in[e, 1, c, x], 0.0)
                tall = jnp.concatenate([back, u, front], axis=0)
                near = planes[x + 1] + planes[x + 3]
                far = planes[x] + planes[x + 4]
                near = near + (tall[1 : ny + 1] + tall[3 : ny + 3])
                far = far + (tall[0:ny] + tall[4 : ny + 4])
                near = near + jnp.where(lane >= 1, pltpu.roll(u, 1, 1), 0.0)
                near = near + jnp.where(lane < nz - 1, pltpu.roll(u, nz - 1, 1), 0.0)
                far = far + jnp.where(lane >= 2, pltpu.roll(u, 2, 1), 0.0)
                far = far + jnp.where(lane < nz - 2, pltpu.roll(u, nz - 2, 1), 0.0)
                curved = centre_weight * u + near_weight * near + far_weight * far
                following = 2.0 * u - field[i, c, x] + coef[x] * curved
                if source is not None:
                    following = following + source(c, x)
                field[i + 2, c, x] = following
            return carry

        lax.fori_loop(0, 3, one, 0)

    wide = 2 * HALF * HALF
    core = lax.rem(comp, 2)
    odd = core == 1
    f_ref[core] = jnp.zeros((FIELDS * MODES, wide), F32)

    def one_block(i, carry):
        @pl.when(i > 0)
        def _():
            comp_copy(i).wait()

        mode_sums(comps[i], weight[...], column[...], odd, q, p_hi, p_lo)
        f_ref[core] += mode_products(q, p_hi, p_lo)

        @pl.when(i == 1)
        def _():
            wait_hop(0)
            start_hop(1)

        return carry

    lax.fori_loop(0, in_group, one_block, 0)
    half_copy = pltpu.make_async_remote_copy(
        src_ref=f_ref.at[core], dst_ref=f_ref.at[core], send_sem=f_send, recv_sem=f_recv,
        device_id=(slab, comp + 1 - 2 * core), device_id_type=MESH,
    )
    half_copy.start()
    wait_halo(0, held.at[1])
    advance(0, held, 0, None)
    start_halo(1, held.at[2])
    wait_hop(1)
    arrived = second[...].reshape(slabs * in_group, 4 * SLOTS)
    px, py, pz, cell = slot_rows(arrived)
    point_modes([px, py, pz], t_ref)
    hot_rows(arrived, cell, xy_hot, z_hot)
    chunk = 256

    def lanes_of(i):
        return pl.ds(pl.multiple_of(i * chunk, chunk), chunk)

    def one_product(i, carry):
        point_products(t_ref, lanes_of(i), w_hi, w_lo)
        return carry

    chunks = t_ref.shape[2] // chunk
    lax.fori_loop(0, chunks, one_product, 0)
    half_copy.wait()
    rows = 3 * MODES
    for which in (0, 1):
        lanes = pl.ds(which * wide, wide)
        for n in range(STEPS):
            f[n, :rows, lanes], f[n, rows:, lanes] = split2(f_ref[which, n * rows : (n + 1) * rows, :])
    driven[0] = jnp.zeros_like(driven[0])

    def one_step(n, carry):
        @pl.when(n > 0)
        def _():
            wait_halo(n, held.at[n + 1])
            advance(n, held, n, None)

        @pl.when((n > 0) & (n < STEPS - 1))
        def _():
            start_halo(n + 1, held.at[n + 2])

        def one_chunk(i, inner):
            point_sums(n, t_ref, lanes_of(i), f, w_hi, w_lo, v_ref)
            return inner

        lax.fori_loop(0, chunks, one_chunk, 0)
        spread_fields(v_ref[n], xy_hot, z_hot, spread, forcing)

        def source(c, x):
            return sign[x] * forcing[c, x * ny : (x + 1) * ny, :]

        @pl.when(n == 0)
        def _():
            def one(c, inner):
                for x in range(nx):
                    driven[1, c, x] = source(c, x)
                return inner

            lax.fori_loop(0, 3, one, 0)

        @pl.when(n > 0)
        def _():
            wait_halo(STEPS + n - 1, driven.at[n])
            advance(STEPS + n - 1, driven, n - 1, source)

        @pl.when(n < STEPS - 1)
        def _():
            start_halo(STEPS + n, driven.at[n + 1])

        return carry

    lax.fori_loop(0, STEPS, one_step, 0)

def local(current_field, earlier_field, wave_coef, layer_mask, point_xyz, point_owner, cell_offset, wave_vector, frequency, amplitude, phase_index, phase_table):
    slabs, in_group = lax.axis_size("slab"), lax.axis_size("comp")
    in_x, in_z = 4, 2
    in_y = slabs // (in_x * in_z)
    devices = slabs * in_group
    points = point_xyz.shape[1]
    width = frequency.shape[0]
    _, nx, ny, nz = current_field.shape
    modes = 4 * HALF * HALF
    slots = devices * SLOTS
    weight, column = mode_tables()
    operands = (
        current_field, earlier_field, wave_coef, layer_mask, point_owner.reshape(1, points), point_xyz,
        cell_offset.reshape(1, points), wave_vector, frequency.reshape(1, width), amplitude,
        phase_index.reshape(1, width), phase_table.reshape(1, -1), jnp.asarray(weight), jnp.asarray(column),
    )
    like = [pltpu.VMEM(a.shape, a.dtype) for a in operands]
    dma = pltpu.SemaphoreType.DMA
    exchanges = 2 * STEPS - 1
    held, driven = pl.pallas_call(
        functools.partial(wave_kernel, (in_x, in_z, in_y, in_group)),
        out_shape=(
            pltpu.VMEM((STEPS + 2, 3, nx, ny, nz), F32),
            pltpu.VMEM((STEPS + 1, 3, nx, ny, nz), F32),
        ),
        in_specs=[pl.BlockSpec(memory_space=pl.ANY)] * len(operands),
        out_specs=[pl.BlockSpec(memory_space=pltpu.VMEM)] * 2,
        scratch_shapes=[
            like[2], like[3], pltpu.VMEM((nx, ny, nz), F32), *like[4:], dma((len(operands),)),
            pltpu.VMEM((in_group, 8, width), F32), dma((in_group,)), dma((in_group,)),
            pltpu.VMEM((in_y * in_x, in_z * in_group, 1, 4 * SLOTS), F32),
            pltpu.VMEM((in_y * in_x, in_z * in_group, 1, 4 * SLOTS), F32),
            pltpu.VMEM((in_z * in_group, in_y * in_x, 1, 4 * SLOTS), F32),
            dma((2, in_y * in_x)), dma((2, in_y * in_x)), dma((2,)),
            pltpu.VMEM((exchanges, 2, 3, 2, ny, nz), F32),
            pltpu.VMEM((exchanges, 2, 3, nx, 2, nz), F32),
            pltpu.VMEM((exchanges, 2, 3, nx, 2, nz), F32),
            dma((exchanges, 4)), dma((exchanges, 4)),
            pltpu.VMEM((2 * FIELDS * MODES, width), BF16),
            pltpu.VMEM((modes // 2, width), BF16),
            pltpu.VMEM((modes // 2, width), BF16),
            pltpu.VMEM((2, FIELDS * MODES, modes // 2), F32), dma, dma,
            pltpu.VMEM((STEPS, 6 * MODES, modes), BF16),
            pltpu.VMEM((3, MODES, slots), F32),
            pltpu.VMEM((modes, slots), BF16),
            pltpu.VMEM((modes, slots), BF16),
            pltpu.VMEM((STEPS, 3, slots), F32),
            pltpu.VMEM((nx * ny, slots), BF16),
            pltpu.VMEM((slots, nz), BF16),
            pltpu.VMEM((6 * nx * ny, slots), BF16),
            pltpu.VMEM((3, nx * ny, nz), F32),
        ],
        compiler_params=pltpu.CompilerParams(
            collective_id=0, has_side_effects=True, vmem_limit_bytes=57600 << 10
        ),
    )(*operands)
    return held[STEPS + 1] + driven[STEPS], held[STEPS] + driven[STEPS - 1]


def solution(mesh):
    in_specs = (
        P(None, "slab", "comp", None),
        P(None, "slab", "comp", None),
        P("slab", "comp", None),
        P("slab", "comp", None),
        P(None, ("slab", "comp")),
        P(("slab", "comp"), None),
        P(("slab", "comp")),
        P(None, "comp"),
        P("comp"),
        P(None, "comp"),
        P("comp"),
        P(),
    )
    out_specs = (P(None, "slab", "comp", None), P(None, "slab", "comp", None))
    return jax.shard_map(local, mesh=mesh, in_specs=in_specs, out_specs=out_specs, check_vma=False)
```

```python
import functools

import jax
import jax.numpy as jnp
import numpy as np
from jax import lax
from jax.experimental import pallas as pl
from jax.experimental.pallas import tpu as pltpu
from jax.sharding import PartitionSpec as P

STEPS = 3
SLOTS = 16
HALF = 16
MODES = 2 * HALF
FIELDS = 9
F32 = jnp.float32
BF16 = jnp.bfloat16
MESH = pl.DeviceIdType.MESH

step_size = 0.05
near_weight = 4.0 / 3.0
far_weight = -1.0 / 12.0
centre_weight = -7.5


def turn_series(degree):
    fits = []
    for h in (
        lambda s: np.cos(2 * np.pi * np.sqrt(s)),
        lambda s: np.sinc(2 * np.sqrt(s)) * 2 * np.pi,
    ):
        fit = np.polynomial.chebyshev.Chebyshev.interpolate(h, degree, domain=[0, 0.25])
        fits.append([float(c) for c in fit.convert(kind=np.polynomial.Polynomial).coef])
    return fits


COS_SERIES, SIN_SERIES = turn_series(7)


def horner(series, s):
    total = jnp.full_like(s, series[-1])
    for c in series[-2::-1]:
        total = total * s + c
    return total


def cos_sin_turns(u):
    r = u - jnp.round(u)
    s = r * r
    return horner(COS_SERIES, s), r * horner(SIN_SERIES, s)


def mode_tables():
    a = np.arange(HALF)
    angle = (2 * a + 1) * np.pi / (2 * MODES)
    nodes = np.cos(angle)
    weight = np.zeros((6 * HALF, 6 * HALF))
    for dim in range(3):
        for parity in (0, 1):
            m = 2 * np.arange(HALF) + parity
            block = 4.0 / MODES * np.cos(m[:, None] * angle[None, :])
            if parity == 0:
                block[0] *= 0.5
            at = (parity * 3 + dim) * HALF
            weight[at : at + HALF, at : at + HALF] = block
    column = np.tile(nodes, 3)[:, None] * np.ones((1, 128))
    return weight.astype(np.float32), column.astype(np.float32)


def split2(x):
    high = x.astype(BF16)
    return high, (x - high.astype(F32)).astype(BF16)


def dot_nt(a, b):
    return lax.dot_general(a, b, (((1,), (1,)), ((), ())), preferred_element_type=F32)


def dot_nn(a, b):
    return lax.dot_general(a, b, (((1,), (0,)), ((), ())), preferred_element_type=F32)


def mode_sums(block, weight, column, odd, q, p_hi, p_lo):
    turn = 1.0 / (2.0 * np.pi)
    rows = FIELDS * MODES
    angles = jnp.concatenate(
        [column[d * HALF : (d + 1) * HALF, 0:1] * (block[d : d + 1, :] * (2.0 * turn)) for d in range(3)], axis=0
    )
    cosine, sine = cos_sin_turns(angles)
    series = lax.dot_general(
        weight, jnp.concatenate([cosine, sine], axis=0), (((1,), (0,)), ((), ())),
        precision=lax.Precision.HIGHEST, preferred_element_type=F32,
    )
    cx, cy, cz, sx, sy, sz = [series[i * HALF : (i + 1) * HALF, :] for i in range(6)]
    centre = (2.0 * turn) * (block[0:1, :] + block[1:2, :] + block[2:3, :]) + turn * block[7:8, :]
    for n in range(STEPS):
        shift_cos, shift_sin = cos_sin_turns(centre - block[3:4, :] * (turn * step_size * (n + 1)))
        outer = jnp.where(odd, -shift_sin, shift_cos)
        inner = jnp.where(odd, -shift_cos, -shift_sin)
        for i in range(3):
            amp = block[4 + i : 5 + i, :]
            at = (3 * n + i) * MODES
            for part, value in ((0, (amp * outer) * cz), (1, (amp * inner) * sz)):
                low = at + part * HALF
                q[low : low + HALF, :], q[rows + low : rows + low + HALF, :] = split2(value)
    even_y = jnp.where(odd, sy, cy)
    odd_y = jnp.where(odd, cy, -sy)
    for m in range(HALF):
        rows_a, rows_b = pl.ds(m * HALF, HALF), pl.ds((HALF + m) * HALF, HALF)
        p_hi[rows_a, :], p_lo[rows_a, :] = split2(cx[m : m + 1, :] * even_y)
        p_hi[rows_b, :], p_lo[rows_b, :] = split2(sx[m : m + 1, :] * odd_y)


def mode_products(q, p_hi, p_lo):
    rows = FIELDS * MODES
    both = dot_nt(q[...], p_hi[...])
    return both[:rows] + both[rows:] + dot_nt(q[:rows, :], p_lo[...])


def slot_rows(arrived):
    turned = arrived.T
    return [
        jnp.concatenate([turned[c * SLOTS + r : c * SLOTS + r + 1, :] for r in range(SLOTS)], axis=1)
        for c in range(4)
    ]


def point_modes(rows, t_ref):
    tau = jnp.concatenate([(r - 2.0) * 0.5 for r in rows], axis=0)
    older, old = jnp.ones_like(tau), tau
    for m in range(MODES):
        at = (m % 2) * HALF + m // 2
        for d in range(3):
            t_ref[d, at : at + 1, :] = older[d : d + 1, :]
        older, old = old, 2.0 * tau * old - older


def point_products(t_ref, lanes, w_hi, w_lo):
    tx, ty = t_ref[0, :, lanes], t_ref[1, :, lanes]
    half = [slice(0, HALF), slice(HALF, MODES)]
    for combo, (px, py) in enumerate(((0, 0), (1, 1), (0, 1), (1, 0))):
        other = ty[half[py], :]
        for m in range(HALF):
            rows = pl.ds((combo * HALF + m) * HALF, HALF)
            at = px * HALF + m
            w_hi[rows, lanes], w_lo[rows, lanes] = split2(tx[at : at + 1, :] * other)


def point_sums(n, t_ref, lanes, f, w_hi, w_lo, v_ref):
    tz = t_ref[2, :, lanes]
    count = 3 * MODES
    both = dot_nn(f[n], w_hi[:, lanes])
    sums = both[:count] + both[count:] + dot_nn(f[n, :count, :], w_lo[:, lanes])
    for i in range(3):
        v_ref[n, i : i + 1, lanes] = jnp.sum(sums[i * MODES : (i + 1) * MODES, :] * tz, axis=0, keepdims=True)


def hot_rows(arrived, cell, xy_hot, z_hot):
    depth = z_hot.shape[1]
    place = jnp.floor((cell - 1.0) * (1.0 / depth))
    xy_hot[...] = jnp.where(
        place == lax.broadcasted_iota(jnp.int32, xy_hot.shape, 0).astype(F32), 1.0, 0.0
    ).astype(BF16)
    sources = arrived.shape[0]
    lane = lax.broadcasted_iota(jnp.int32, (sources, depth), 1).astype(F32)
    for r in range(SLOTS):
        one = arrived[:, 3 * SLOTS + r : 3 * SLOTS + r + 1] - 1.0
        along = one - jnp.floor(one * (1.0 / depth)) * depth
        z_hot[r * sources : (r + 1) * sources, :] = jnp.where(along == lane, 1.0, 0.0).astype(BF16)


def spread_fields(v, xy_hot, z_hot, spread, forcing):
    cells = xy_hot.shape[0]
    v_hi, v_lo = split2(v)
    for i in range(3):
        spread[2 * i * cells : (2 * i + 1) * cells, :] = xy_hot[...] * v_hi[i : i + 1, :]
        spread[(2 * i + 1) * cells : (2 * i + 2) * cells, :] = xy_hot[...] * v_lo[i : i + 1, :]
    total = dot_nn(spread[...], z_hot[...])
    for i in range(3):
        forcing[i] = total[2 * i * cells : (2 * i + 1) * cells] + total[(2 * i + 1) * cells : (2 * i + 2) * cells]


def pack_points(owner, xyz, offset, send, split):
    in_x, in_z, in_y, in_group = split
    points = owner.shape[1]
    devices = in_x * in_z * in_y * in_group
    bits = [n.bit_length() - 1 for n in (in_group, in_x, in_z)]
    c = owner & (in_group - 1)
    x = (owner >> bits[0]) & (in_x - 1)
    z = (owner >> (bits[0] + bits[1])) & (in_z - 1)
    y = owner >> (bits[0] + bits[1] + bits[2])
    place = ((y * in_x + x) * in_z + z) * in_group + c
    hit = place == lax.broadcasted_iota(jnp.int32, (devices, points), 0)
    match = jnp.where(hit, 1.0, 0.0)
    match16 = match.astype(BF16)
    run = min(points, 128)
    rows, columns = (lax.broadcasted_iota(jnp.int32, (run, 2 * run), d) for d in (0, 1))
    before = jnp.where((rows < columns) | (columns >= run), 1.0, 0.0).astype(BF16)
    offset_in = jnp.zeros((devices, run), F32)
    ranks = []
    for at in range(0, points, run):
        sums = dot_nn(match16[:, at : at + run], before)
        ranks.append(jnp.sum((sums[:, :run] + offset_in) * match[:, at : at + run], axis=0, keepdims=True))
        offset_in = offset_in + sums[:, run:]
    rank = jnp.concatenate(ranks, axis=1)
    slot = rank == lax.broadcasted_iota(jnp.int32, (SLOTS, points), 0).astype(F32)
    values = [xyz[i : i + 1, :] for i in range(3)] + [(offset + 1).astype(F32)]
    spread = jnp.concatenate([jnp.where(slot, v, 0.0) for v in values], axis=0)
    first = spread.astype(BF16)
    second, third = split2(spread - first.astype(F32))
    rows = dot_nt(match16, first) + dot_nt(match16, second) + dot_nt(match16, third)
    inner = in_z * in_group
    for d in range(devices):
        send[d // inner, d % inner] = rows[d : d + 1, :]


def wave_kernel(
    split,
    current_in, earlier_in, coef_in, mask_in, owner_in, xyz_in, offset_in, wave_in, freq_in, amp_in, index_in, table_in,
    weight_in, column_in,
    held,
    coef, mask, sign, owner, xyz, offset, wave, freq, amp, index, table, weight, column, load_sem,
    comps, comp_send, comp_recv,
    sent, first, second, hop_send, hop_recv, hop_own,
    x_in, y_in, y_out, halo_send, halo_recv,
    q, p_hi, p_lo, f_ref, f_send, f_recv, f, t_ref, w_hi, w_lo, v_ref, xy_hot, z_hot, spread, forcing,
):
    in_x, in_z, in_y, in_group = split
    slabs = in_x * in_z * in_y
    slab, comp = lax.axis_index("slab"), lax.axis_index("comp")
    x, z, y = slab % in_x, slab // in_x % in_z, slab // (in_x * in_z)
    nx, ny, nz = coef.shape
    after, before = lax.rem(slab + 1, slabs), lax.rem(slab + slabs - 1, slabs)
    right, left = lax.rem(comp + 1, in_group), lax.rem(comp + in_group - 1, in_group)
    outer, inner = y * in_x + x, z * in_group + comp
    outers, inners = in_y * in_x, in_z * in_group

    def outer_at(d):
        there = lax.rem(outer + d, outers)
        return there, ((there // in_x * in_z + z) * in_x + there % in_x, comp)

    def inner_at(d):
        there = lax.rem(inner + d, inners)
        return there, ((y * in_z + there // in_group) * in_x + x, there % in_group)

    def group_at(d):
        return lax.rem(comp + d, in_group)

    barrier = pltpu.get_barrier_semaphore()
    partners = [outer_at(d)[1] for d in range(1, outers)]
    partners += [inner_at(d)[1] for d in range(1, inners)]
    partners += [(after, comp), (before, comp)]
    loads = [
        pltpu.make_async_copy(a, b, load_sem.at[i])
        for i, (a, b) in enumerate((
            (owner_in, owner), (xyz_in, xyz), (offset_in, offset),
            (wave_in, wave), (freq_in, freq), (amp_in, amp), (index_in, index), (table_in, table),
            (current_in, held.at[1]), (column_in, column), (weight_in, weight),
            (coef_in, coef), (earlier_in, held.at[0]), (mask_in, mask),
        ))
    ]
    for load in loads[:3]:
        load.start()
    for partner in partners:
        pl.semaphore_signal(barrier, inc=1, device_id=partner, device_id_type=MESH)
    for load in loads[3:]:
        load.start()
    for load in loads[:3]:
        load.wait()
    pack_points(owner[...], xyz[...], offset[...], sent, split)
    for load in loads[3:8]:
        load.wait()
    found = index[...] == lax.broadcasted_iota(jnp.int32, (table.shape[1], index.shape[1]), 0)
    phase = lax.dot_general(
        table[...], jnp.where(found, 1.0, 0.0), (((1,), (0,)), ((), ())),
        precision=lax.Precision.HIGHEST, preferred_element_type=F32,
    )
    comps[0, 0:3, :] = wave[...]
    comps[0, 3:4, :] = freq[...]
    comps[0, 4:7, :] = amp[...]
    comps[0, 7:8, :] = phase
    loads[8].wait()

    def halo_copies(e, u, c):
        faces = (
            (u.at[c, pl.ds(0, 2)], x_in.at[e, 1, c], (before, comp)),
            (u.at[c, pl.ds(nx - 2, 2)], x_in.at[e, 0, c], (after, comp)),
            (y_out.at[e, 0, c], y_in.at[e, 1, c], (slab, left)),
            (y_out.at[e, 1, c], y_in.at[e, 0, c], (slab, right)),
        )
        return [
            pltpu.make_async_remote_copy(
                src_ref=a, dst_ref=b, send_sem=halo_send.at[e, c, i], recv_sem=halo_recv.at[e, c, i],
                device_id=target, device_id_type=MESH,
            )
            for i, (a, b, target) in enumerate(faces)
        ]

    def start_halo(e, u, c):
        copies = halo_copies(e, u, c)
        for copy in copies[:2]:
            copy.start()
        y_out[e, 0, c] = u[c, :, 0:2, :]
        y_out[e, 1, c] = u[c, :, ny - 2 : ny, :]
        for copy in copies[2:]:
            copy.start()

    def wait_halo(e, u, c):
        for copy in halo_copies(e, u, c):
            copy.wait()

    def comp_copy(d):
        return pltpu.make_async_remote_copy(
            src_ref=comps.at[0], dst_ref=comps.at[d], send_sem=comp_send.at[d], recv_sem=comp_recv.at[d],
            device_id=(slab, group_at(d)), device_id_type=MESH,
        )

    def hop_copies(hop):
        if hop == 0:
            moves = [(sent.at[outer_at(d)[0]], first.at[outer], outer_at(d)[1]) for d in range(outers)]
        else:
            moves = [(first.at[:, inner_at(d)[0]], second.at[inner], inner_at(d)[1]) for d in range(inners)]
        own = pltpu.make_async_copy(moves[0][0], moves[0][1], hop_own.at[hop])
        return [own] + [
            pltpu.make_async_remote_copy(
                src_ref=a, dst_ref=b, send_sem=hop_send.at[hop, d], recv_sem=hop_recv.at[hop, d],
                device_id=target, device_id_type=MESH,
            )
            for d, (a, b, target) in enumerate(moves) if d > 0
        ]

    def start_hop(hop):
        for copy in hop_copies(hop):
            copy.start()

    def wait_hop(hop):
        for copy in hop_copies(hop):
            copy.wait()

    pl.semaphore_wait(barrier, len(partners))
    start_hop(0)
    for d in range(1, in_group):
        comp_copy(d).start()
    for c in range(3):
        start_halo(0, held.at[1], c)
    for load in loads[9:]:
        load.wait()
    sign[...] = jnp.where(mask[...] == 1, 1.0, 0.0) - jnp.where(mask[...] == 2, 1.0, 0.0)

    lane = lax.broadcasted_iota(jnp.int32, (ny, nz), 1)

    def advance(i, source, send):
        def one(c, carry):
            wait_halo(i, held.at[i + 1], c)
            low, high = x_in[i, 0, c], x_in[i, 1, c]
            low, high = jnp.where(slab > 0, low, 0.0), jnp.where(slab < slabs - 1, high, 0.0)
            planes = [low[0], low[1]] + [held[i + 1, c, x] for x in range(nx)] + [high[0], high[1]]
            for x in range(nx):
                u = planes[x + 2]
                back = jnp.where(comp > 0, y_in[i, 0, c, x], 0.0)
                front = jnp.where(comp < in_group - 1, y_in[i, 1, c, x], 0.0)
                tall = jnp.concatenate([back, u, front], axis=0)
                near = planes[x + 1] + planes[x + 3]
                far = planes[x] + planes[x + 4]
                near = near + (tall[1 : ny + 1] + tall[3 : ny + 3])
                far = far + (tall[0:ny] + tall[4 : ny + 4])
                near = near + jnp.where(lane >= 1, pltpu.roll(u, 1, 1), 0.0)
                near = near + jnp.where(lane < nz - 1, pltpu.roll(u, nz - 1, 1), 0.0)
                far = far + jnp.where(lane >= 2, pltpu.roll(u, 2, 1), 0.0)
                far = far + jnp.where(lane < nz - 2, pltpu.roll(u, nz - 2, 1), 0.0)
                curved = centre_weight * u + near_weight * near + far_weight * far
                following = 2.0 * u - held[i, c, x] + coef[x] * curved
                if source is not None:
                    following = following + source(c, x)
                held[i + 2, c, x] = following
            if send is not None:
                @pl.when(send)
                def _():
                    start_halo(i + 1, held.at[i + 2], c)

            return carry

        lax.fori_loop(0, 3, one, 0)

    wide = 2 * HALF * HALF
    core = lax.rem(comp, 2)
    odd = core == 1
    f_ref[core] = jnp.zeros((FIELDS * MODES, wide), F32)

    def one_block(i, carry):
        @pl.when(i > 0)
        def _():
            comp_copy(i).wait()

        mode_sums(comps[i], weight[...], column[...], odd, q, p_hi, p_lo)
        f_ref[core] += mode_products(q, p_hi, p_lo)

        @pl.when(i == 1)
        def _():
            wait_hop(0)
            start_hop(1)

        return carry

    lax.fori_loop(0, in_group, one_block, 0)
    half_copies = [
        pltpu.make_async_remote_copy(
            src_ref=f_ref.at[core, pl.ds(n * 3 * MODES, 3 * MODES)],
            dst_ref=f_ref.at[core, pl.ds(n * 3 * MODES, 3 * MODES)],
            send_sem=f_send.at[n], recv_sem=f_recv.at[n],
            device_id=(slab, comp + 1 - 2 * core), device_id_type=MESH,
        )
        for n in range(STEPS)
    ]
    for copy in half_copies:
        copy.start()
    advance(0, None, None)
    wait_hop(1)
    arrived = second[...].reshape(slabs * in_group, 4 * SLOTS)
    px, py, pz, cell = slot_rows(arrived)
    point_modes([px, py, pz], t_ref)
    hot_rows(arrived, cell, xy_hot, z_hot)
    def lanes_of(i, chunk):
        return pl.ds(pl.multiple_of(i * chunk, chunk), chunk)

    def one_product(i, carry):
        point_products(t_ref, lanes_of(i, narrow), w_hi, w_lo)
        return carry

    slots = t_ref.shape[2]
    narrow, broad = min(slots, 256), min(slots, 1024)
    lax.fori_loop(0, slots // narrow, one_product, 0)
    rows = 3 * MODES

    def take_half(n):
        half_copies[n].wait()
        for which in (0, 1):
            lanes = pl.ds(which * wide, wide)
            f[n, :rows, lanes], f[n, rows:, lanes] = split2(f_ref[which, n * rows : (n + 1) * rows, :])

    def one_step(n, carry):
        for step in range(STEPS):
            @pl.when(n == step)
            def _(step=step):
                take_half(step)

        def one_chunk(i, inner):
            point_sums(n, t_ref, lanes_of(i, broad), f, w_hi, w_lo, v_ref)
            return inner

        lax.fori_loop(0, slots // broad, one_chunk, 0)
        spread_fields(v_ref[n], xy_hot, z_hot, spread, forcing)

        def source(c, x):
            return sign[x] * forcing[c, x * ny : (x + 1) * ny, :]

        @pl.when(n == 0)
        def _():
            def one(c, inner):
                for x in range(nx):
                    held[2, c, x] += source(c, x)
                start_halo(1, held.at[2], c)
                return inner

            lax.fori_loop(0, 3, one, 0)

        @pl.when(n > 0)
        def _():
            advance(n, source, n < STEPS - 1)

        return carry

    lax.fori_loop(0, STEPS, one_step, 0)

def local(current_field, earlier_field, wave_coef, layer_mask, point_xyz, point_owner, cell_offset, wave_vector, frequency, amplitude, phase_index, phase_table):
    slabs, in_group = lax.axis_size("slab"), lax.axis_size("comp")
    in_x, in_z = 4, 2
    in_y = slabs // (in_x * in_z)
    devices = slabs * in_group
    points = point_xyz.shape[1]
    width = frequency.shape[0]
    _, nx, ny, nz = current_field.shape
    modes = 4 * HALF * HALF
    slots = devices * SLOTS
    weight, column = mode_tables()
    operands = (
        current_field, earlier_field, wave_coef, layer_mask, point_owner.reshape(1, points), point_xyz,
        cell_offset.reshape(1, points), wave_vector, frequency.reshape(1, width), amplitude,
        phase_index.reshape(1, width), phase_table.reshape(1, -1), jnp.asarray(weight), jnp.asarray(column),
    )
    like = [pltpu.VMEM(a.shape, a.dtype) for a in operands]
    dma = pltpu.SemaphoreType.DMA
    exchanges = STEPS
    held = pl.pallas_call(
        functools.partial(wave_kernel, (in_x, in_z, in_y, in_group)),
        out_shape=pltpu.VMEM((STEPS + 2, 3, nx, ny, nz), F32),
        in_specs=[pl.BlockSpec(memory_space=pl.ANY)] * len(operands),
        out_specs=pl.BlockSpec(memory_space=pltpu.VMEM),
        scratch_shapes=[
            like[2], like[3], pltpu.VMEM((nx, ny, nz), F32), *like[4:], dma((len(operands),)),
            pltpu.VMEM((in_group, 8, width), F32), dma((in_group,)), dma((in_group,)),
            pltpu.VMEM((in_y * in_x, in_z * in_group, 1, 4 * SLOTS), F32),
            pltpu.VMEM((in_y * in_x, in_z * in_group, 1, 4 * SLOTS), F32),
            pltpu.VMEM((in_z * in_group, in_y * in_x, 1, 4 * SLOTS), F32),
            dma((2, in_y * in_x)), dma((2, in_y * in_x)), dma((2,)),
            pltpu.VMEM((exchanges, 2, 3, 2, ny, nz), F32),
            pltpu.VMEM((exchanges, 2, 3, nx, 2, nz), F32),
            pltpu.VMEM((exchanges, 2, 3, nx, 2, nz), F32),
            dma((exchanges, 3, 4)), dma((exchanges, 3, 4)),
            pltpu.VMEM((2 * FIELDS * MODES, width), BF16),
            pltpu.VMEM((modes // 2, width), BF16),
            pltpu.VMEM((modes // 2, width), BF16),
            pltpu.VMEM((2, FIELDS * MODES, modes // 2), F32), dma((STEPS,)), dma((STEPS,)),
            pltpu.VMEM((STEPS, 6 * MODES, modes), BF16),
            pltpu.VMEM((3, MODES, slots), F32),
            pltpu.VMEM((modes, slots), BF16),
            pltpu.VMEM((modes, slots), BF16),
            pltpu.VMEM((STEPS, 3, slots), F32),
            pltpu.VMEM((nx * ny, slots), BF16),
            pltpu.VMEM((slots, nz), BF16),
            pltpu.VMEM((6 * nx * ny, slots), BF16),
            pltpu.VMEM((3, nx * ny, nz), F32),
        ],
        compiler_params=pltpu.CompilerParams(
            collective_id=0, has_side_effects=True, vmem_limit_bytes=59200 << 10
        ),
    )(*operands)
    return held[STEPS + 1], held[STEPS]


def solution(mesh):
    in_specs = (
        P(None, "slab", "comp", None),
        P(None, "slab", "comp", None),
        P("slab", "comp", None),
        P("slab", "comp", None),
        P(None, ("slab", "comp")),
        P(("slab", "comp"), None),
        P(("slab", "comp")),
        P(None, "comp"),
        P("comp"),
        P(None, "comp"),
        P("comp"),
        P(),
    )
    out_specs = (P(None, "slab", "comp", None), P(None, "slab", "comp", None))
    return jax.shard_map(local, mesh=mesh, in_specs=in_specs, out_specs=out_specs, check_vma=False)
```

```python
import functools

import jax
import jax.numpy as jnp
import numpy as np
from jax import lax
from jax.experimental import pallas as pl
from jax.experimental.pallas import tpu as pltpu
from jax.sharding import PartitionSpec as P

STEPS = 3
SLOTS = 16
HALF = 16
MODES = 2 * HALF
FIELDS = 9
F32 = jnp.float32
BF16 = jnp.bfloat16
MESH = pl.DeviceIdType.MESH

step_size = 0.05
near_weight = 4.0 / 3.0
far_weight = -1.0 / 12.0
centre_weight = -7.5


def turn_series(degree):
    fits = []
    for h in (
        lambda s: np.cos(2 * np.pi * np.sqrt(s)),
        lambda s: np.sinc(2 * np.sqrt(s)) * 2 * np.pi,
    ):
        fit = np.polynomial.chebyshev.Chebyshev.interpolate(h, degree, domain=[0, 0.25])
        fits.append([float(c) for c in fit.convert(kind=np.polynomial.Polynomial).coef])
    return fits


COS_SERIES, SIN_SERIES = turn_series(7)


def horner(series, s):
    total = jnp.full_like(s, series[-1])
    for c in series[-2::-1]:
        total = total * s + c
    return total


def cos_sin_turns(u):
    r = u - jnp.round(u)
    s = r * r
    return horner(COS_SERIES, s), r * horner(SIN_SERIES, s)


def mode_tables():
    a = np.arange(HALF)
    angle = (2 * a + 1) * np.pi / (2 * MODES)
    nodes = np.cos(angle)
    weight = np.zeros((6 * HALF, 6 * HALF))
    for dim in range(3):
        for parity in (0, 1):
            m = 2 * np.arange(HALF) + parity
            block = 4.0 / MODES * np.cos(m[:, None] * angle[None, :])
            if parity == 0:
                block[0] *= 0.5
            at = (parity * 3 + dim) * HALF
            weight[at : at + HALF, at : at + HALF] = block
    column = np.tile(nodes, 3)[:, None] * np.ones((1, 128))
    return weight.astype(np.float32), column.astype(np.float32)


def split2(x):
    high = x.astype(BF16)
    return high, (x - high.astype(F32)).astype(BF16)


def dot_nt(a, b):
    return lax.dot_general(a, b, (((1,), (1,)), ((), ())), preferred_element_type=F32)


def dot_nn(a, b):
    return lax.dot_general(a, b, (((1,), (0,)), ((), ())), preferred_element_type=F32)


def mode_sums(block, weight, column, odd, q, p_hi, p_lo):
    turn = 1.0 / (2.0 * np.pi)
    rows = FIELDS * MODES
    angles = jnp.concatenate(
        [column[d * HALF : (d + 1) * HALF, 0:1] * (block[d : d + 1, :] * (2.0 * turn)) for d in range(3)], axis=0
    )
    cosine, sine = cos_sin_turns(angles)
    series = lax.dot_general(
        weight, jnp.concatenate([cosine, sine], axis=0), (((1,), (0,)), ((), ())),
        precision=lax.Precision.HIGHEST, preferred_element_type=F32,
    )
    cx, cy, cz, sx, sy, sz = [series[i * HALF : (i + 1) * HALF, :] for i in range(6)]
    centre = (2.0 * turn) * (block[0:1, :] + block[1:2, :] + block[2:3, :]) + turn * block[7:8, :]
    for n in range(STEPS):
        shift_cos, shift_sin = cos_sin_turns(centre - block[3:4, :] * (turn * step_size * (n + 1)))
        outer = jnp.where(odd, -shift_sin, shift_cos)
        inner = jnp.where(odd, -shift_cos, -shift_sin)
        for i in range(3):
            amp = block[4 + i : 5 + i, :]
            at = (3 * n + i) * MODES
            for part, value in ((0, (amp * outer) * cz), (1, (amp * inner) * sz)):
                low = at + part * HALF
                q[low : low + HALF, :], q[rows + low : rows + low + HALF, :] = split2(value)
    even_y = jnp.where(odd, sy, cy)
    odd_y = jnp.where(odd, cy, -sy)
    for m in range(HALF):
        rows_a, rows_b = pl.ds(m * HALF, HALF), pl.ds((HALF + m) * HALF, HALF)
        p_hi[rows_a, :], p_lo[rows_a, :] = split2(cx[m : m + 1, :] * even_y)
        p_hi[rows_b, :], p_lo[rows_b, :] = split2(sx[m : m + 1, :] * odd_y)


def mode_products(q, p_hi, p_lo):
    rows = FIELDS * MODES
    both = dot_nt(q[...], p_hi[...])
    return both[:rows] + both[rows:] + dot_nt(q[:rows, :], p_lo[...])


def slot_rows(arrived):
    turned = arrived.T
    return [
        jnp.concatenate([turned[c * SLOTS + r : c * SLOTS + r + 1, :] for r in range(SLOTS)], axis=1)
        for c in range(4)
    ]


def point_modes(rows, t_ref):
    tau = jnp.concatenate([(r - 2.0) * 0.5 for r in rows], axis=0)
    older, old = jnp.ones_like(tau), tau
    for m in range(MODES):
        at = (m % 2) * HALF + m // 2
        for d in range(3):
            t_ref[d, at : at + 1, :] = older[d : d + 1, :]
        older, old = old, 2.0 * tau * old - older


def point_products(t_ref, lanes, w_hi, w_lo):
    tx, ty = t_ref[0, :, lanes], t_ref[1, :, lanes]
    half = [slice(0, HALF), slice(HALF, MODES)]
    for combo, (px, py) in enumerate(((0, 0), (1, 1), (0, 1), (1, 0))):
        other = ty[half[py], :]
        for m in range(HALF):
            rows = pl.ds((combo * HALF + m) * HALF, HALF)
            at = px * HALF + m
            w_hi[rows, lanes], w_lo[rows, lanes] = split2(tx[at : at + 1, :] * other)


def point_sums(n, t_ref, lanes, f, w_hi, w_lo, v_ref):
    tz = t_ref[2, :, lanes]
    count = 3 * MODES
    both = dot_nn(f[n], w_hi[:, lanes])
    sums = both[:count] + both[count:] + dot_nn(f[n, :count, :], w_lo[:, lanes])
    for i in range(3):
        v_ref[n, i : i + 1, lanes] = jnp.sum(sums[i * MODES : (i + 1) * MODES, :] * tz, axis=0, keepdims=True)


def hot_rows(cell, xy_hot, depth):
    place = jnp.floor((cell - 1.0) * (1.0 / depth))
    xy_hot[...] = jnp.where(
        place == lax.broadcasted_iota(jnp.int32, xy_hot.shape, 0).astype(F32), 1.0, 0.0
    ).astype(BF16)


def hot_columns(along, first, last, z_hot):
    depth = z_hot.shape[1]
    sources = along.shape[0]
    lane = lax.broadcasted_iota(jnp.int32, (sources, depth), 1).astype(F32)
    for r in range(first, last):
        z_hot[r * sources : (r + 1) * sources, :] = jnp.where(along[:, r : r + 1] == lane, 1.0, 0.0).astype(BF16)


def spread_fields(v, xy_hot, z_hot, spread, forcing):
    cells = xy_hot.shape[0]
    v_hi, v_lo = split2(v)
    for i in range(3):
        spread[2 * i * cells : (2 * i + 1) * cells, :] = xy_hot[...] * v_hi[i : i + 1, :]
        spread[(2 * i + 1) * cells : (2 * i + 2) * cells, :] = xy_hot[...] * v_lo[i : i + 1, :]
    total = dot_nn(spread[...], z_hot[...])
    for i in range(3):
        forcing[i] = total[2 * i * cells : (2 * i + 1) * cells] + total[(2 * i + 1) * cells : (2 * i + 2) * cells]


def pack_points(owner, xyz, offset, send, split):
    in_x, in_z, in_y, in_group = split
    points = owner.shape[1]
    devices = in_x * in_z * in_y * in_group
    bits = [n.bit_length() - 1 for n in (in_group, in_x, in_z)]
    c = owner & (in_group - 1)
    x = (owner >> bits[0]) & (in_x - 1)
    z = (owner >> (bits[0] + bits[1])) & (in_z - 1)
    y = owner >> (bits[0] + bits[1] + bits[2])
    place = ((y * in_x + x) * in_z + z) * in_group + c
    hit = place == lax.broadcasted_iota(jnp.int32, (devices, points), 0)
    match = jnp.where(hit, 1.0, 0.0)
    match16 = match.astype(BF16)
    run = min(points, 128)
    rows, columns = (lax.broadcasted_iota(jnp.int32, (run, 2 * run), d) for d in (0, 1))
    before = jnp.where((rows < columns) | (columns >= run), 1.0, 0.0).astype(BF16)
    offset_in = jnp.zeros((devices, run), F32)
    ranks = []
    for at in range(0, points, run):
        sums = dot_nn(match16[:, at : at + run], before)
        ranks.append(jnp.sum((sums[:, :run] + offset_in) * match[:, at : at + run], axis=0, keepdims=True))
        offset_in = offset_in + sums[:, run:]
    rank = jnp.concatenate(ranks, axis=1)
    slot = rank == lax.broadcasted_iota(jnp.int32, (SLOTS, points), 0).astype(F32)
    values = [xyz[i : i + 1, :] for i in range(3)] + [(offset + 1).astype(F32)]
    spread = jnp.concatenate([jnp.where(slot, v, 0.0) for v in values], axis=0)
    first = spread.astype(BF16)
    second, third = split2(spread - first.astype(F32))
    rows = dot_nt(match16, first) + dot_nt(match16, second) + dot_nt(match16, third)
    inner = in_z * in_group
    for d in range(devices):
        send[d // inner, d % inner] = rows[d : d + 1, :]


def wave_kernel(
    split,
    current_in, earlier_in, coef_in, mask_in, owner_in, xyz_in, offset_in, wave_in, freq_in, amp_in, index_in, table_in,
    weight_in, column_in,
    held,
    coef, mask, sign, owner, xyz, offset, wave, freq, amp, index, table, weight, column, load_sem,
    comps, comp_send, comp_recv,
    sent, first, second, hop_send, hop_recv, hop_own,
    x_in, y_in, y_out, halo_send, halo_recv,
    q, p_hi, p_lo, f_ref, f_send, f_recv, f, t_ref, w_hi, w_lo, v_ref, xy_hot, z_hot, spread, forcing,
):
    in_x, in_z, in_y, in_group = split
    slabs = in_x * in_z * in_y
    slab, comp = lax.axis_index("slab"), lax.axis_index("comp")
    x, z, y = slab % in_x, slab // in_x % in_z, slab // (in_x * in_z)
    nx, ny, nz = coef.shape
    after, before = lax.rem(slab + 1, slabs), lax.rem(slab + slabs - 1, slabs)
    right, left = lax.rem(comp + 1, in_group), lax.rem(comp + in_group - 1, in_group)
    outer, inner = y * in_x + x, z * in_group + comp
    outers, inners = in_y * in_x, in_z * in_group

    def outer_at(d):
        there = lax.rem(outer + d, outers)
        return there, ((there // in_x * in_z + z) * in_x + there % in_x, comp)

    def inner_at(d):
        there = lax.rem(inner + d, inners)
        return there, ((y * in_z + there // in_group) * in_x + x, there % in_group)

    def group_at(d):
        return lax.rem(comp + d, in_group)

    barrier = pltpu.get_barrier_semaphore()
    partners = [outer_at(d)[1] for d in range(1, outers)]
    partners += [inner_at(d)[1] for d in range(1, inners)]
    partners += [(after, comp), (before, comp)]
    loads = [
        pltpu.make_async_copy(a, b, load_sem.at[i])
        for i, (a, b) in enumerate((
            (owner_in, owner), (xyz_in, xyz), (offset_in, offset),
            (wave_in, wave), (freq_in, freq), (amp_in, amp), (index_in, index), (table_in, table),
            (current_in, held.at[1]), (column_in, column), (weight_in, weight),
            (coef_in, coef), (earlier_in, held.at[0]), (mask_in, mask),
        ))
    ]
    for load in loads[:3]:
        load.start()
    for partner in partners:
        pl.semaphore_signal(barrier, inc=1, device_id=partner, device_id_type=MESH)
    for load in loads[3:]:
        load.start()
    for load in loads[:3]:
        load.wait()
    pack_points(owner[...], xyz[...], offset[...], sent, split)
    for load in loads[3:8]:
        load.wait()
    found = index[...] == lax.broadcasted_iota(jnp.int32, (table.shape[1], index.shape[1]), 0)
    phase = lax.dot_general(
        table[...], jnp.where(found, 1.0, 0.0), (((1,), (0,)), ((), ())),
        precision=lax.Precision.HIGHEST, preferred_element_type=F32,
    )
    comps[0, 0:3, :] = wave[...]
    comps[0, 3:4, :] = freq[...]
    comps[0, 4:7, :] = amp[...]
    comps[0, 7:8, :] = phase
    loads[8].wait()

    def halo_copies(e, u, c):
        faces = (
            (u.at[c, pl.ds(0, 2)], x_in.at[e, 1, c], (before, comp)),
            (u.at[c, pl.ds(nx - 2, 2)], x_in.at[e, 0, c], (after, comp)),
            (y_out.at[e, 0, c], y_in.at[e, 1, c], (slab, left)),
            (y_out.at[e, 1, c], y_in.at[e, 0, c], (slab, right)),
        )
        return [
            pltpu.make_async_remote_copy(
                src_ref=a, dst_ref=b, send_sem=halo_send.at[e, c, i], recv_sem=halo_recv.at[e, c, i],
                device_id=target, device_id_type=MESH,
            )
            for i, (a, b, target) in enumerate(faces)
        ]

    def start_halo(e, u, c):
        copies = halo_copies(e, u, c)
        for copy in copies[:2]:
            copy.start()
        y_out[e, 0, c] = u[c, :, 0:2, :]
        y_out[e, 1, c] = u[c, :, ny - 2 : ny, :]
        for copy in copies[2:]:
            copy.start()

    def wait_halo(e, u, c):
        for copy in halo_copies(e, u, c):
            copy.wait()

    def comp_copy(d):
        return pltpu.make_async_remote_copy(
            src_ref=comps.at[0], dst_ref=comps.at[d], send_sem=comp_send.at[d], recv_sem=comp_recv.at[d],
            device_id=(slab, group_at(d)), device_id_type=MESH,
        )

    def hop_copies(hop):
        if hop == 0:
            moves = [(sent.at[outer_at(d)[0]], first.at[outer], outer_at(d)[1]) for d in range(outers)]
        else:
            moves = [(first.at[:, inner_at(d)[0]], second.at[inner], inner_at(d)[1]) for d in range(inners)]
        own = pltpu.make_async_copy(moves[0][0], moves[0][1], hop_own.at[hop])
        return [own] + [
            pltpu.make_async_remote_copy(
                src_ref=a, dst_ref=b, send_sem=hop_send.at[hop, d], recv_sem=hop_recv.at[hop, d],
                device_id=target, device_id_type=MESH,
            )
            for d, (a, b, target) in enumerate(moves) if d > 0
        ]

    def start_hop(hop):
        for copy in hop_copies(hop):
            copy.start()

    def wait_hop(hop):
        for copy in hop_copies(hop):
            copy.wait()

    pl.semaphore_wait(barrier, len(partners))
    start_hop(0)
    for d in range(1, in_group):
        comp_copy(d).start()
    for c in range(3):
        start_halo(0, held.at[1], c)
    for load in loads[9:]:
        load.wait()
    sign[...] = jnp.where(mask[...] == 1, 1.0, 0.0) - jnp.where(mask[...] == 2, 1.0, 0.0)

    lane = lax.broadcasted_iota(jnp.int32, (ny, nz), 1)

    def advance(i, source, send):
        def one(c, carry):
            wait_halo(i, held.at[i + 1], c)
            low, high = x_in[i, 0, c], x_in[i, 1, c]
            low, high = jnp.where(slab > 0, low, 0.0), jnp.where(slab < slabs - 1, high, 0.0)
            planes = [low[0], low[1]] + [held[i + 1, c, x] for x in range(nx)] + [high[0], high[1]]
            for x in range(nx):
                u = planes[x + 2]
                back = jnp.where(comp > 0, y_in[i, 0, c, x], 0.0)
                front = jnp.where(comp < in_group - 1, y_in[i, 1, c, x], 0.0)
                tall = jnp.concatenate([back, u, front], axis=0)
                near = planes[x + 1] + planes[x + 3]
                far = planes[x] + planes[x + 4]
                near = near + (tall[1 : ny + 1] + tall[3 : ny + 3])
                far = far + (tall[0:ny] + tall[4 : ny + 4])
                near = near + jnp.where(lane >= 1, pltpu.roll(u, 1, 1), 0.0)
                near = near + jnp.where(lane < nz - 1, pltpu.roll(u, nz - 1, 1), 0.0)
                far = far + jnp.where(lane >= 2, pltpu.roll(u, 2, 1), 0.0)
                far = far + jnp.where(lane < nz - 2, pltpu.roll(u, nz - 2, 1), 0.0)
                curved = centre_weight * u + near_weight * near + far_weight * far
                following = 2.0 * u - held[i, c, x] + coef[x] * curved
                if source is not None:
                    following = following + source(c, x)
                held[i + 2, c, x] = following
            if send is not None:
                @pl.when(send)
                def _():
                    start_halo(i + 1, held.at[i + 2], c)

            return carry

        lax.fori_loop(0, 3, one, 0)

    wide = 2 * HALF * HALF
    core = lax.rem(comp, 2)
    odd = core == 1
    f_ref[core] = jnp.zeros((FIELDS * MODES, wide), F32)

    def one_block(i, carry):
        @pl.when(i > 0)
        def _():
            comp_copy(i).wait()

        mode_sums(comps[i], weight[...], column[...], odd, q, p_hi, p_lo)
        f_ref[core] += mode_products(q, p_hi, p_lo)

        @pl.when(i == 1)
        def _():
            wait_hop(0)
            start_hop(1)

        return carry

    lax.fori_loop(0, in_group, one_block, 0)
    half_copies = [
        pltpu.make_async_remote_copy(
            src_ref=f_ref.at[core, pl.ds(n * 3 * MODES, 3 * MODES)],
            dst_ref=f_ref.at[core, pl.ds(n * 3 * MODES, 3 * MODES)],
            send_sem=f_send.at[n], recv_sem=f_recv.at[n],
            device_id=(slab, comp + 1 - 2 * core), device_id_type=MESH,
        )
        for n in range(STEPS)
    ]
    for copy in half_copies:
        copy.start()
    advance(0, None, None)
    wait_hop(1)
    arrived = second[...].reshape(slabs * in_group, 4 * SLOTS)
    px, py, pz, cell = slot_rows(arrived)
    point_modes([px, py, pz], t_ref)
    cells = arrived[:, 3 * SLOTS :] - 1.0
    along = cells - jnp.floor(cells * (1.0 / nz)) * nz
    def lanes_of(i, chunk):
        return pl.ds(pl.multiple_of(i * chunk, chunk), chunk)

    slots = t_ref.shape[2]
    narrow, broad = slots // 4, min(slots, 1024)
    point_products(t_ref, pl.ds(0, narrow), w_hi, w_lo)
    rows = 3 * MODES

    def take_half(n):
        half_copies[n].wait()
        for which in (0, 1):
            lanes = pl.ds(which * wide, wide)
            f[n, :rows, lanes], f[n, rows:, lanes] = split2(f_ref[which, n * rows : (n + 1) * rows, :])

    take_half(0)
    for i in range(4):
        point_sums(0, t_ref, pl.ds(i * narrow, narrow), f, w_hi, w_lo, v_ref)
        if i < 3:
            point_products(t_ref, pl.ds((i + 1) * narrow, narrow), w_hi, w_lo)
            hot_columns(along, i * SLOTS // 4, (i + 1) * SLOTS // 4, z_hot)
        else:
            hot_columns(along, i * SLOTS // 4, SLOTS, z_hot)
            hot_rows(cell, xy_hot, nz)
    spread_fields(v_ref[0], xy_hot, z_hot, spread, forcing)

    def source(c, x):
        return sign[x] * forcing[c, x * ny : (x + 1) * ny, :]

    def first_step(c, carry):
        for x in range(nx):
            held[2, c, x] += source(c, x)
        start_halo(1, held.at[2], c)
        return carry

    lax.fori_loop(0, 3, first_step, 0)

    def one_step(n, carry):
        for step in range(1, STEPS):
            @pl.when(n == step)
            def _(step=step):
                take_half(step)

        def one_chunk(i, inner):
            point_sums(n, t_ref, lanes_of(i, broad), f, w_hi, w_lo, v_ref)
            return inner

        lax.fori_loop(0, slots // broad, one_chunk, 0)
        spread_fields(v_ref[n], xy_hot, z_hot, spread, forcing)

        advance(n, source, n < STEPS - 1)
        return carry

    lax.fori_loop(1, STEPS, one_step, 0)

def local(current_field, earlier_field, wave_coef, layer_mask, point_xyz, point_owner, cell_offset, wave_vector, frequency, amplitude, phase_index, phase_table):
    slabs, in_group = lax.axis_size("slab"), lax.axis_size("comp")
    in_x, in_z = 4, 2
    in_y = slabs // (in_x * in_z)
    devices = slabs * in_group
    points = point_xyz.shape[1]
    width = frequency.shape[0]
    _, nx, ny, nz = current_field.shape
    modes = 4 * HALF * HALF
    slots = devices * SLOTS
    weight, column = mode_tables()
    operands = (
        current_field, earlier_field, wave_coef, layer_mask, point_owner.reshape(1, points), point_xyz,
        cell_offset.reshape(1, points), wave_vector, frequency.reshape(1, width), amplitude,
        phase_index.reshape(1, width), phase_table.reshape(1, -1), jnp.asarray(weight), jnp.asarray(column),
    )
    like = [pltpu.VMEM(a.shape, a.dtype) for a in operands]
    dma = pltpu.SemaphoreType.DMA
    exchanges = STEPS
    held = pl.pallas_call(
        functools.partial(wave_kernel, (in_x, in_z, in_y, in_group)),
        out_shape=pltpu.VMEM((STEPS + 2, 3, nx, ny, nz), F32),
        in_specs=[pl.BlockSpec(memory_space=pl.ANY)] * len(operands),
        out_specs=pl.BlockSpec(memory_space=pltpu.VMEM),
        scratch_shapes=[
            like[2], like[3], pltpu.VMEM((nx, ny, nz), F32), *like[4:], dma((len(operands),)),
            pltpu.VMEM((in_group, 8, width), F32), dma((in_group,)), dma((in_group,)),
            pltpu.VMEM((in_y * in_x, in_z * in_group, 1, 4 * SLOTS), F32),
            pltpu.VMEM((in_y * in_x, in_z * in_group, 1, 4 * SLOTS), F32),
            pltpu.VMEM((in_z * in_group, in_y * in_x, 1, 4 * SLOTS), F32),
            dma((2, in_y * in_x)), dma((2, in_y * in_x)), dma((2,)),
            pltpu.VMEM((exchanges, 2, 3, 2, ny, nz), F32),
            pltpu.VMEM((exchanges, 2, 3, nx, 2, nz), F32),
            pltpu.VMEM((exchanges, 2, 3, nx, 2, nz), F32),
            dma((exchanges, 3, 4)), dma((exchanges, 3, 4)),
            pltpu.VMEM((2 * FIELDS * MODES, width), BF16),
            pltpu.VMEM((modes // 2, width), BF16),
            pltpu.VMEM((modes // 2, width), BF16),
            pltpu.VMEM((2, FIELDS * MODES, modes // 2), F32), dma((STEPS,)), dma((STEPS,)),
            pltpu.VMEM((STEPS, 6 * MODES, modes), BF16),
            pltpu.VMEM((3, MODES, slots), F32),
            pltpu.VMEM((modes, slots), BF16),
            pltpu.VMEM((modes, slots), BF16),
            pltpu.VMEM((STEPS, 3, slots), F32),
            pltpu.VMEM((nx * ny, slots), BF16),
            pltpu.VMEM((slots, nz), BF16),
            pltpu.VMEM((6 * nx * ny, slots), BF16),
            pltpu.VMEM((3, nx * ny, nz), F32),
        ],
        compiler_params=pltpu.CompilerParams(
            collective_id=0, has_side_effects=True, vmem_limit_bytes=59200 << 10
        ),
    )(*operands)
    return held[STEPS + 1], held[STEPS]


def solution(mesh):
    in_specs = (
        P(None, "slab", "comp", None),
        P(None, "slab", "comp", None),
        P("slab", "comp", None),
        P("slab", "comp", None),
        P(None, ("slab", "comp")),
        P(("slab", "comp"), None),
        P(("slab", "comp")),
        P(None, "comp"),
        P("comp"),
        P(None, "comp"),
        P("comp"),
        P(),
    )
    out_specs = (P(None, "slab", "comp", None), P(None, "slab", "comp", None))
    return jax.shard_map(local, mesh=mesh, in_specs=in_specs, out_specs=out_specs, check_vma=False)
```

```python
import functools

import jax
import jax.numpy as jnp
import numpy as np
from jax import lax
from jax.experimental import pallas as pl
from jax.experimental.pallas import tpu as pltpu
from jax.sharding import PartitionSpec as P

STEPS = 3
SLOTS = 16
HALF = 16
MODES = 2 * HALF
FIELDS = 9
F32 = jnp.float32
BF16 = jnp.bfloat16
MESH = pl.DeviceIdType.MESH

step_size = 0.05
near_weight = 4.0 / 3.0
far_weight = -1.0 / 12.0
centre_weight = -7.5


def turn_series(degree):
    fits = []
    for h in (
        lambda s: np.cos(2 * np.pi * np.sqrt(s)),
        lambda s: np.sinc(2 * np.sqrt(s)) * 2 * np.pi,
    ):
        fit = np.polynomial.chebyshev.Chebyshev.interpolate(h, degree, domain=[0, 0.25])
        fits.append([float(c) for c in fit.convert(kind=np.polynomial.Polynomial).coef])
    return fits


COS_SERIES, SIN_SERIES = turn_series(7)


def horner(series, s):
    total = jnp.full_like(s, series[-1])
    for c in series[-2::-1]:
        total = total * s + c
    return total


def cos_sin_turns(u):
    r = u - jnp.round(u)
    s = r * r
    return horner(COS_SERIES, s), r * horner(SIN_SERIES, s)


def mode_tables():
    a = np.arange(HALF)
    angle = (2 * a + 1) * np.pi / (2 * MODES)
    nodes = np.cos(angle)
    weight = np.zeros((6 * HALF, 6 * HALF))
    for dim in range(3):
        for parity in (0, 1):
            m = 2 * np.arange(HALF) + parity
            block = 4.0 / MODES * np.cos(m[:, None] * angle[None, :])
            if parity == 0:
                block[0] *= 0.5
            at = (parity * 3 + dim) * HALF
            weight[at : at + HALF, at : at + HALF] = block
    column = np.tile(nodes, 3)[:, None] * np.ones((1, 128))
    return weight.astype(np.float32), column.astype(np.float32)


def split2(x):
    high = x.astype(BF16)
    return high, (x - high.astype(F32)).astype(BF16)


def dot_nt(a, b):
    return lax.dot_general(a, b, (((1,), (1,)), ((), ())), preferred_element_type=F32)


def dot_nn(a, b):
    return lax.dot_general(a, b, (((1,), (0,)), ((), ())), preferred_element_type=F32)


def mode_sums(block, weight, column, odd, q, p_hi, p_lo):
    turn = 1.0 / (2.0 * np.pi)
    rows = FIELDS * MODES
    angles = jnp.concatenate(
        [column[d * HALF : (d + 1) * HALF, 0:1] * (block[d : d + 1, :] * (2.0 * turn)) for d in range(3)], axis=0
    )
    cosine, sine = cos_sin_turns(angles)
    series = lax.dot_general(
        weight, jnp.concatenate([cosine, sine], axis=0), (((1,), (0,)), ((), ())),
        precision=lax.Precision.HIGHEST, preferred_element_type=F32,
    )
    cx, cy, cz, sx, sy, sz = [series[i * HALF : (i + 1) * HALF, :] for i in range(6)]
    centre = (2.0 * turn) * (block[0:1, :] + block[1:2, :] + block[2:3, :]) + turn * block[7:8, :]
    for n in range(STEPS):
        shift_cos, shift_sin = cos_sin_turns(centre - block[3:4, :] * (turn * step_size * (n + 1)))
        outer = jnp.where(odd, -shift_sin, shift_cos)
        inner = jnp.where(odd, -shift_cos, -shift_sin)
        for i in range(3):
            amp = block[4 + i : 5 + i, :]
            at = (3 * n + i) * MODES
            for part, value in ((0, (amp * outer) * cz), (1, (amp * inner) * sz)):
                low = at + part * HALF
                q[low : low + HALF, :], q[rows + low : rows + low + HALF, :] = split2(value)
    even_y = jnp.where(odd, sy, cy)
    odd_y = jnp.where(odd, cy, -sy)
    for m in range(HALF):
        rows_a, rows_b = pl.ds(m * HALF, HALF), pl.ds((HALF + m) * HALF, HALF)
        p_hi[rows_a, :], p_lo[rows_a, :] = split2(cx[m : m + 1, :] * even_y)
        p_hi[rows_b, :], p_lo[rows_b, :] = split2(sx[m : m + 1, :] * odd_y)


def mode_products(q, p_hi, p_lo):
    rows = FIELDS * MODES
    both = dot_nt(q[...], p_hi[...])
    return both[:rows] + both[rows:] + dot_nt(q[:rows, :], p_lo[...])


def slot_rows(arrived):
    turned = arrived.T
    return [
        jnp.concatenate([turned[c * SLOTS + r : c * SLOTS + r + 1, :] for r in range(SLOTS)], axis=1)
        for c in range(4)
    ]


def point_modes(rows, t_ref):
    tau = jnp.concatenate([(r - 2.0) * 0.5 for r in rows], axis=0)
    older, old = jnp.ones_like(tau), tau
    for m in range(MODES):
        at = (m % 2) * HALF + m // 2
        for d in range(3):
            t_ref[d, at : at + 1, :] = older[d : d + 1, :]
        older, old = old, 2.0 * tau * old - older


def point_products(t_ref, lanes, w_hi, w_lo):
    tx, ty = t_ref[0, :, lanes], t_ref[1, :, lanes]
    half = [slice(0, HALF), slice(HALF, MODES)]
    for combo, (px, py) in enumerate(((0, 0), (1, 1), (0, 1), (1, 0))):
        other = ty[half[py], :]
        for m in range(HALF):
            rows = pl.ds((combo * HALF + m) * HALF, HALF)
            at = px * HALF + m
            w_hi[rows, lanes], w_lo[rows, lanes] = split2(tx[at : at + 1, :] * other)


def point_sums(n, t_ref, lanes, f, w_hi, w_lo, v_ref):
    tz = t_ref[2, :, lanes]
    count = 3 * MODES
    both = dot_nn(f[n], w_hi[:, lanes])
    sums = both[:count] + both[count:] + dot_nn(f[n, :count, :], w_lo[:, lanes])
    for i in range(3):
        v_ref[n, i : i + 1, lanes] = jnp.sum(sums[i * MODES : (i + 1) * MODES, :] * tz, axis=0, keepdims=True)


def hot_rows(cell, xy_hot, depth):
    place = jnp.floor((cell - 1.0) * (1.0 / depth))
    xy_hot[...] = jnp.where(
        place == lax.broadcasted_iota(jnp.int32, xy_hot.shape, 0).astype(F32), 1.0, 0.0
    ).astype(BF16)


def hot_columns(along, first, last, z_hot):
    depth = z_hot.shape[1]
    sources = along.shape[0]
    lane = lax.broadcasted_iota(jnp.int32, (sources, depth), 1).astype(F32)
    for r in range(first, last):
        z_hot[r * sources : (r + 1) * sources, :] = jnp.where(along[:, r : r + 1] == lane, 1.0, 0.0).astype(BF16)


def spread_fields(v, xy_hot, z_hot, spread, forcing):
    cells = xy_hot.shape[0]
    v_hi, v_lo = split2(v)
    for i in range(3):
        spread[2 * i * cells : (2 * i + 1) * cells, :] = xy_hot[...] * v_hi[i : i + 1, :]
        spread[(2 * i + 1) * cells : (2 * i + 2) * cells, :] = xy_hot[...] * v_lo[i : i + 1, :]
    total = dot_nn(spread[...], z_hot[...])
    for i in range(3):
        forcing[i] = total[2 * i * cells : (2 * i + 1) * cells] + total[(2 * i + 1) * cells : (2 * i + 2) * cells]


def pack_points(owner, xyz, offset, send, split):
    in_x, in_z, in_y, in_group = split
    points = owner.shape[1]
    devices = in_x * in_z * in_y * in_group
    bits = [n.bit_length() - 1 for n in (in_group, in_x, in_z)]
    c = owner & (in_group - 1)
    x = (owner >> bits[0]) & (in_x - 1)
    z = (owner >> (bits[0] + bits[1])) & (in_z - 1)
    y = owner >> (bits[0] + bits[1] + bits[2])
    place = ((y * in_x + x) * in_z + z) * in_group + c
    hit = place == lax.broadcasted_iota(jnp.int32, (devices, points), 0)
    match = jnp.where(hit, 1.0, 0.0)
    match16 = match.astype(BF16)
    run = min(points, 128)
    rows, columns = (lax.broadcasted_iota(jnp.int32, (run, 2 * run), d) for d in (0, 1))
    before = jnp.where((rows < columns) | (columns >= run), 1.0, 0.0).astype(BF16)
    offset_in = jnp.zeros((devices, run), F32)
    ranks = []
    for at in range(0, points, run):
        sums = dot_nn(match16[:, at : at + run], before)
        ranks.append(jnp.sum((sums[:, :run] + offset_in) * match[:, at : at + run], axis=0, keepdims=True))
        offset_in = offset_in + sums[:, run:]
    rank = jnp.concatenate(ranks, axis=1)
    slot = rank == lax.broadcasted_iota(jnp.int32, (SLOTS, points), 0).astype(F32)
    values = [xyz[i : i + 1, :] for i in range(3)] + [(offset + 1).astype(F32)]
    spread = jnp.concatenate([jnp.where(slot, v, 0.0) for v in values], axis=0)
    first = spread.astype(BF16)
    second, third = split2(spread - first.astype(F32))
    rows = dot_nt(match16, first) + dot_nt(match16, second) + dot_nt(match16, third)
    inner = in_z * in_group
    for d in range(devices):
        send[d // inner, d % inner] = rows[d : d + 1, :]


def wave_kernel(
    split,
    current_in, earlier_in, coef_in, mask_in, owner_in, xyz_in, offset_in, wave_in, freq_in, amp_in, index_in, table_in,
    weight_in, column_in,
    held,
    coef, mask, sign, owner, xyz, offset, wave, freq, amp, index, table, weight, column, load_sem,
    comps, comp_send, comp_recv,
    sent, first, second, hop_send, hop_recv, hop_own,
    x_in, y_in, y_out, halo_send, halo_recv,
    q, p_hi, p_lo, f_ref, f_send, f_recv, f, t_ref, w_hi, w_lo, v_ref, xy_hot, z_hot, spread, forcing,
):
    in_x, in_z, in_y, in_group = split
    slabs = in_x * in_z * in_y
    slab, comp = lax.axis_index("slab"), lax.axis_index("comp")
    x, z, y = slab % in_x, slab // in_x % in_z, slab // (in_x * in_z)
    nx, ny, nz = coef.shape
    after, before = lax.rem(slab + 1, slabs), lax.rem(slab + slabs - 1, slabs)
    right, left = lax.rem(comp + 1, in_group), lax.rem(comp + in_group - 1, in_group)
    outer, inner = y * in_x + x, z * in_group + comp
    outers, inners = in_y * in_x, in_z * in_group

    def outer_at(d):
        there = lax.rem(outer + d, outers)
        return there, ((there // in_x * in_z + z) * in_x + there % in_x, comp)

    def inner_at(d):
        there = lax.rem(inner + d, inners)
        return there, ((y * in_z + there // in_group) * in_x + x, there % in_group)

    def group_at(d):
        return comp + lax.rem(d, 2) * (1 - 2 * lax.rem(comp, 2)) + (d // 2) * (2 - 4 * (comp // 2))

    barrier = pltpu.get_barrier_semaphore()
    partners = [outer_at(d)[1] for d in range(1, outers)]
    partners += [inner_at(d)[1] for d in range(1, inners)]
    partners += [(after, comp), (before, comp)]
    loads = [
        pltpu.make_async_copy(a, b, load_sem.at[i])
        for i, (a, b) in enumerate((
            (owner_in, owner), (xyz_in, xyz), (offset_in, offset),
            (wave_in, wave), (freq_in, freq), (amp_in, amp), (index_in, index), (table_in, table),
            (current_in, held.at[1]), (column_in, column), (weight_in, weight),
            (coef_in, coef), (earlier_in, held.at[0]), (mask_in, mask),
        ))
    ]
    for load in loads[:3]:
        load.start()
    for partner in partners:
        pl.semaphore_signal(barrier, inc=1, device_id=partner, device_id_type=MESH)
    for load in loads[3:]:
        load.start()
    for load in loads[:3]:
        load.wait()
    pack_points(owner[...], xyz[...], offset[...], sent, split)
    for load in loads[3:8]:
        load.wait()
    found = index[...] == lax.broadcasted_iota(jnp.int32, (table.shape[1], index.shape[1]), 0)
    phase = lax.dot_general(
        table[...], jnp.where(found, 1.0, 0.0), (((1,), (0,)), ((), ())),
        precision=lax.Precision.HIGHEST, preferred_element_type=F32,
    )
    comps[0, 0:3, :] = wave[...]
    comps[0, 3:4, :] = freq[...]
    comps[0, 4:7, :] = amp[...]
    comps[0, 7:8, :] = phase
    loads[8].wait()

    def halo_copies(e, u, c):
        faces = (
            (u.at[c, pl.ds(0, 2)], x_in.at[e, 1, c], (before, comp)),
            (u.at[c, pl.ds(nx - 2, 2)], x_in.at[e, 0, c], (after, comp)),
            (y_out.at[e, 0, c], y_in.at[e, 1, c], (slab, left)),
            (y_out.at[e, 1, c], y_in.at[e, 0, c], (slab, right)),
        )
        return [
            pltpu.make_async_remote_copy(
                src_ref=a, dst_ref=b, send_sem=halo_send.at[e, c, i], recv_sem=halo_recv.at[e, c, i],
                device_id=target, device_id_type=MESH,
            )
            for i, (a, b, target) in enumerate(faces)
        ]

    def start_x(e, u, c):
        for copy in halo_copies(e, u, c)[:2]:
            copy.start()

    def start_y(e, u, c):
        y_out[e, 0, c] = u[c, :, 0:2, :]
        y_out[e, 1, c] = u[c, :, ny - 2 : ny, :]
        for copy in halo_copies(e, u, c)[2:]:
            copy.start()

    def start_halo(e, u, c):
        start_x(e, u, c)
        start_y(e, u, c)

    def wait_halo(e, u, c):
        for copy in halo_copies(e, u, c):
            copy.wait()

    def comp_copy(d):
        return pltpu.make_async_remote_copy(
            src_ref=comps.at[0], dst_ref=comps.at[d], send_sem=comp_send.at[d], recv_sem=comp_recv.at[d],
            device_id=(slab, group_at(d)), device_id_type=MESH,
        )

    def hop_copies(hop):
        if hop == 0:
            moves = [(sent.at[outer_at(d)[0]], first.at[outer], outer_at(d)[1]) for d in range(outers)]
        else:
            moves = [(first.at[:, inner_at(d)[0]], second.at[inner], inner_at(d)[1]) for d in range(inners)]
        own = pltpu.make_async_copy(moves[0][0], moves[0][1], hop_own.at[hop])
        return [own] + [
            pltpu.make_async_remote_copy(
                src_ref=a, dst_ref=b, send_sem=hop_send.at[hop, d], recv_sem=hop_recv.at[hop, d],
                device_id=target, device_id_type=MESH,
            )
            for d, (a, b, target) in enumerate(moves) if d > 0
        ]

    def start_hop(hop):
        for copy in hop_copies(hop):
            copy.start()

    def wait_hop(hop):
        for copy in hop_copies(hop):
            copy.wait()

    pl.semaphore_wait(barrier, len(partners))
    start_hop(0)
    for d in range(1, in_group):
        comp_copy(d).start()
    for c in range(3):
        start_halo(0, held.at[1], c)
    for load in loads[9:]:
        load.wait()
    sign[...] = jnp.where(mask[...] == 1, 1.0, 0.0) - jnp.where(mask[...] == 2, 1.0, 0.0)

    lane = lax.broadcasted_iota(jnp.int32, (ny, nz), 1)
    outside = [0, 1, nx - 2, nx - 1]
    inside = list(range(2, nx - 2))

    def advance(i, source, send):
        def one(c, carry):
            wait_halo(i, held.at[i + 1], c)
            low, high = x_in[i, 0, c], x_in[i, 1, c]
            low, high = jnp.where(slab > 0, low, 0.0), jnp.where(slab < slabs - 1, high, 0.0)
            planes = [low[0], low[1]] + [held[i + 1, c, x] for x in range(nx)] + [high[0], high[1]]
            for x in outside + inside:
                if x == inside[0] and send is not None:
                    @pl.when(send)
                    def _():
                        start_x(i + 1, held.at[i + 2], c)

                u = planes[x + 2]
                back = jnp.where(comp > 0, y_in[i, 0, c, x], 0.0)
                front = jnp.where(comp < in_group - 1, y_in[i, 1, c, x], 0.0)
                tall = jnp.concatenate([back, u, front], axis=0)
                near = planes[x + 1] + planes[x + 3]
                far = planes[x] + planes[x + 4]
                near = near + (tall[1 : ny + 1] + tall[3 : ny + 3])
                far = far + (tall[0:ny] + tall[4 : ny + 4])
                near = near + jnp.where(lane >= 1, pltpu.roll(u, 1, 1), 0.0)
                near = near + jnp.where(lane < nz - 1, pltpu.roll(u, nz - 1, 1), 0.0)
                far = far + jnp.where(lane >= 2, pltpu.roll(u, 2, 1), 0.0)
                far = far + jnp.where(lane < nz - 2, pltpu.roll(u, nz - 2, 1), 0.0)
                curved = centre_weight * u + near_weight * near + far_weight * far
                following = 2.0 * u - held[i, c, x] + coef[x] * curved
                if source is not None:
                    following = following + source(c, x)
                held[i + 2, c, x] = following
            if send is not None:
                @pl.when(send)
                def _():
                    start_y(i + 1, held.at[i + 2], c)

            return carry

        lax.fori_loop(0, 3, one, 0)

    wide = 2 * HALF * HALF
    core = lax.rem(comp, 2)
    odd = core == 1
    f_ref[core] = jnp.zeros((FIELDS * MODES, wide), F32)

    def one_block(i, carry):
        @pl.when(i > 0)
        def _():
            comp_copy(i).wait()

        mode_sums(comps[i], weight[...], column[...], odd, q, p_hi, p_lo)
        f_ref[core] += mode_products(q, p_hi, p_lo)

        @pl.when(i == 2)
        def _():
            wait_hop(0)
            start_hop(1)

        return carry

    lax.fori_loop(0, in_group, one_block, 0)
    half_copies = [
        pltpu.make_async_remote_copy(
            src_ref=f_ref.at[core, pl.ds(n * 3 * MODES, 3 * MODES)],
            dst_ref=f_ref.at[core, pl.ds(n * 3 * MODES, 3 * MODES)],
            send_sem=f_send.at[n], recv_sem=f_recv.at[n],
            device_id=(slab, comp + 1 - 2 * core), device_id_type=MESH,
        )
        for n in range(STEPS)
    ]
    for copy in half_copies:
        copy.start()
    advance(0, None, None)
    wait_hop(1)
    arrived = second[...].reshape(slabs * in_group, 4 * SLOTS)
    px, py, pz, cell = slot_rows(arrived)
    point_modes([px, py, pz], t_ref)
    cells = arrived[:, 3 * SLOTS :] - 1.0
    along = cells - jnp.floor(cells * (1.0 / nz)) * nz
    def lanes_of(i, chunk):
        return pl.ds(pl.multiple_of(i * chunk, chunk), chunk)

    slots = t_ref.shape[2]
    narrow, broad = slots // 4, min(slots, 1024)
    point_products(t_ref, pl.ds(0, narrow), w_hi, w_lo)
    rows = 3 * MODES

    def take_half(n):
        half_copies[n].wait()
        for which in (0, 1):
            lanes = pl.ds(which * wide, wide)
            f[n, :rows, lanes], f[n, rows:, lanes] = split2(f_ref[which, n * rows : (n + 1) * rows, :])

    take_half(0)
    for i in range(4):
        point_sums(0, t_ref, pl.ds(i * narrow, narrow), f, w_hi, w_lo, v_ref)
        if i < 3:
            point_products(t_ref, pl.ds((i + 1) * narrow, narrow), w_hi, w_lo)
            hot_columns(along, i * SLOTS // 4, (i + 1) * SLOTS // 4, z_hot)
        else:
            hot_columns(along, i * SLOTS // 4, SLOTS, z_hot)
            hot_rows(cell, xy_hot, nz)
    spread_fields(v_ref[0], xy_hot, z_hot, spread, forcing)

    def source(c, x):
        return sign[x] * forcing[c, x * ny : (x + 1) * ny, :]

    def first_outside(c, carry):
        for x in outside:
            held[2, c, x] += source(c, x)
        start_x(1, held.at[2], c)
        return carry

    def first_inside(c, carry):
        for x in inside:
            held[2, c, x] += source(c, x)
        start_y(1, held.at[2], c)
        return carry

    lax.fori_loop(0, 3, first_outside, 0)
    lax.fori_loop(0, 3, first_inside, 0)

    def one_step(n, carry):
        for step in range(1, STEPS):
            @pl.when(n == step)
            def _(step=step):
                take_half(step)

        def one_chunk(i, inner):
            point_sums(n, t_ref, lanes_of(i, broad), f, w_hi, w_lo, v_ref)
            return inner

        lax.fori_loop(0, slots // broad, one_chunk, 0)
        spread_fields(v_ref[n], xy_hot, z_hot, spread, forcing)

        advance(n, source, n < STEPS - 1)
        return carry

    lax.fori_loop(1, STEPS, one_step, 0)

def local(current_field, earlier_field, wave_coef, layer_mask, point_xyz, point_owner, cell_offset, wave_vector, frequency, amplitude, phase_index, phase_table):
    slabs, in_group = lax.axis_size("slab"), lax.axis_size("comp")
    in_x, in_z = 4, 2
    in_y = slabs // (in_x * in_z)
    devices = slabs * in_group
    points = point_xyz.shape[1]
    width = frequency.shape[0]
    _, nx, ny, nz = current_field.shape
    modes = 4 * HALF * HALF
    slots = devices * SLOTS
    weight, column = mode_tables()
    operands = (
        current_field, earlier_field, wave_coef, layer_mask, point_owner.reshape(1, points), point_xyz,
        cell_offset.reshape(1, points), wave_vector, frequency.reshape(1, width), amplitude,
        phase_index.reshape(1, width), phase_table.reshape(1, -1), jnp.asarray(weight), jnp.asarray(column),
    )
    like = [pltpu.VMEM(a.shape, a.dtype) for a in operands]
    dma = pltpu.SemaphoreType.DMA
    exchanges = STEPS
    held = pl.pallas_call(
        functools.partial(wave_kernel, (in_x, in_z, in_y, in_group)),
        out_shape=pltpu.VMEM((STEPS + 2, 3, nx, ny, nz), F32),
        in_specs=[pl.BlockSpec(memory_space=pl.ANY)] * len(operands),
        out_specs=pl.BlockSpec(memory_space=pltpu.VMEM),
        scratch_shapes=[
            like[2], like[3], pltpu.VMEM((nx, ny, nz), F32), *like[4:], dma((len(operands),)),
            pltpu.VMEM((in_group, 8, width), F32), dma((in_group,)), dma((in_group,)),
            pltpu.VMEM((in_y * in_x, in_z * in_group, 1, 4 * SLOTS), F32),
            pltpu.VMEM((in_y * in_x, in_z * in_group, 1, 4 * SLOTS), F32),
            pltpu.VMEM((in_z * in_group, in_y * in_x, 1, 4 * SLOTS), F32),
            dma((2, in_y * in_x)), dma((2, in_y * in_x)), dma((2,)),
            pltpu.VMEM((exchanges, 2, 3, 2, ny, nz), F32),
            pltpu.VMEM((exchanges, 2, 3, nx, 2, nz), F32),
            pltpu.VMEM((exchanges, 2, 3, nx, 2, nz), F32),
            dma((exchanges, 3, 4)), dma((exchanges, 3, 4)),
            pltpu.VMEM((2 * FIELDS * MODES, width), BF16),
            pltpu.VMEM((modes // 2, width), BF16),
            pltpu.VMEM((modes // 2, width), BF16),
            pltpu.VMEM((2, FIELDS * MODES, modes // 2), F32), dma((STEPS,)), dma((STEPS,)),
            pltpu.VMEM((STEPS, 6 * MODES, modes), BF16),
            pltpu.VMEM((3, MODES, slots), F32),
            pltpu.VMEM((modes, slots), BF16),
            pltpu.VMEM((modes, slots), BF16),
            pltpu.VMEM((STEPS, 3, slots), F32),
            pltpu.VMEM((nx * ny, slots), BF16),
            pltpu.VMEM((slots, nz), BF16),
            pltpu.VMEM((6 * nx * ny, slots), BF16),
            pltpu.VMEM((3, nx * ny, nz), F32),
        ],
        compiler_params=pltpu.CompilerParams(
            collective_id=0, has_side_effects=True, vmem_limit_bytes=59200 << 10
        ),
    )(*operands)
    return held[STEPS + 1], held[STEPS]


def solution(mesh):
    in_specs = (
        P(None, "slab", "comp", None),
        P(None, "slab", "comp", None),
        P("slab", "comp", None),
        P("slab", "comp", None),
        P(None, ("slab", "comp")),
        P(("slab", "comp"), None),
        P(("slab", "comp")),
        P(None, "comp"),
        P("comp"),
        P(None, "comp"),
        P("comp"),
        P(),
    )
    out_specs = (P(None, "slab", "comp", None), P(None, "slab", "comp", None))
    return jax.shard_map(local, mesh=mesh, in_specs=in_specs, out_specs=out_specs, check_vma=False)
```

```python
import functools

import jax
import jax.numpy as jnp
import numpy as np
from jax import lax
from jax.experimental import pallas as pl
from jax.experimental.pallas import tpu as pltpu
from jax.sharding import PartitionSpec as P

STEPS = 3
SLOTS = 16
HALF = 16
MODES = 2 * HALF
FIELDS = 9
F32 = jnp.float32
BF16 = jnp.bfloat16
MESH = pl.DeviceIdType.MESH

step_size = 0.05
near_weight = 4.0 / 3.0
far_weight = -1.0 / 12.0
centre_weight = -7.5


def turn_series(degree):
    fits = []
    for h in (
        lambda s: np.cos(2 * np.pi * np.sqrt(s)),
        lambda s: np.sinc(2 * np.sqrt(s)) * 2 * np.pi,
    ):
        fit = np.polynomial.chebyshev.Chebyshev.interpolate(h, degree, domain=[0, 0.25])
        fits.append([float(c) for c in fit.convert(kind=np.polynomial.Polynomial).coef])
    return fits


COS_SERIES, SIN_SERIES = turn_series(7)


def horner(series, s):
    total = jnp.full_like(s, series[-1])
    for c in series[-2::-1]:
        total = total * s + c
    return total


def cos_sin_turns(u):
    r = u - jnp.round(u)
    s = r * r
    return horner(COS_SERIES, s), r * horner(SIN_SERIES, s)


def mode_tables():
    a = np.arange(HALF)
    angle = (2 * a + 1) * np.pi / (2 * MODES)
    nodes = np.cos(angle)
    weight = np.zeros((6 * HALF, 6 * HALF))
    for dim in range(3):
        for parity in (0, 1):
            m = 2 * np.arange(HALF) + parity
            block = 4.0 / MODES * np.cos(m[:, None] * angle[None, :])
            if parity == 0:
                block[0] *= 0.5
            at = (parity * 3 + dim) * HALF
            weight[at : at + HALF, at : at + HALF] = block
    column = np.tile(nodes, 3)[:, None] * np.ones((1, 128))
    return weight.astype(np.float32), column.astype(np.float32)


def split2(x):
    high = x.astype(BF16)
    return high, (x - high.astype(F32)).astype(BF16)


def dot_nt(a, b):
    return lax.dot_general(a, b, (((1,), (1,)), ((), ())), preferred_element_type=F32)


def dot_nn(a, b):
    return lax.dot_general(a, b, (((1,), (0,)), ((), ())), preferred_element_type=F32)


def mode_sums(block, weight, column, odd, q, p_hi, p_lo):
    turn = 1.0 / (2.0 * np.pi)
    rows = FIELDS * MODES
    angles = jnp.concatenate(
        [column[d * HALF : (d + 1) * HALF, 0:1] * (block[d : d + 1, :] * (2.0 * turn)) for d in range(3)], axis=0
    )
    cosine, sine = cos_sin_turns(angles)
    series = lax.dot_general(
        weight, jnp.concatenate([cosine, sine], axis=0), (((1,), (0,)), ((), ())),
        precision=lax.Precision.HIGHEST, preferred_element_type=F32,
    )
    cx, cy, cz, sx, sy, sz = [series[i * HALF : (i + 1) * HALF, :] for i in range(6)]
    centre = (2.0 * turn) * (block[0:1, :] + block[1:2, :] + block[2:3, :]) + turn * block[7:8, :]
    for n in range(STEPS):
        shift_cos, shift_sin = cos_sin_turns(centre - block[3:4, :] * (turn * step_size * (n + 1)))
        outer = jnp.where(odd, -shift_sin, shift_cos)
        inner = jnp.where(odd, -shift_cos, -shift_sin)
        for i in range(3):
            amp = block[4 + i : 5 + i, :]
            at = (3 * n + i) * MODES
            for part, value in ((0, (amp * outer) * cz), (1, (amp * inner) * sz)):
                low = at + part * HALF
                q[low : low + HALF, :], q[rows + low : rows + low + HALF, :] = split2(value)
    even_y = jnp.where(odd, sy, cy)
    odd_y = jnp.where(odd, cy, -sy)
    for m in range(HALF):
        rows_a, rows_b = pl.ds(m * HALF, HALF), pl.ds((HALF + m) * HALF, HALF)
        p_hi[rows_a, :], p_lo[rows_a, :] = split2(cx[m : m + 1, :] * even_y)
        p_hi[rows_b, :], p_lo[rows_b, :] = split2(sx[m : m + 1, :] * odd_y)


def mode_products(q, p_hi, p_lo):
    rows = FIELDS * MODES
    both = dot_nt(q[...], p_hi[...])
    return both[:rows] + both[rows:] + dot_nt(q[:rows, :], p_lo[...])


def slot_rows(arrived):
    turned = arrived.T
    return [
        jnp.concatenate([turned[c * SLOTS + r : c * SLOTS + r + 1, :] for r in range(SLOTS)], axis=1)
        for c in range(4)
    ]


def point_modes(rows, t_ref):
    tau = jnp.concatenate([(r - 2.0) * 0.5 for r in rows], axis=0)
    older, old = jnp.ones_like(tau), tau
    for m in range(MODES):
        at = (m % 2) * HALF + m // 2
        for d in range(3):
            t_ref[d, at : at + 1, :] = older[d : d + 1, :]
        older, old = old, 2.0 * tau * old - older


def point_products(t_ref, lanes, w_hi, w_lo):
    tx, ty = t_ref[0, :, lanes], t_ref[1, :, lanes]
    half = [slice(0, HALF), slice(HALF, MODES)]
    for combo, (px, py) in enumerate(((0, 0), (1, 1), (0, 1), (1, 0))):
        other = ty[half[py], :]
        for m in range(HALF):
            rows = pl.ds((combo * HALF + m) * HALF, HALF)
            at = px * HALF + m
            w_hi[rows, lanes], w_lo[rows, lanes] = split2(tx[at : at + 1, :] * other)


def point_sums(n, t_ref, lanes, f, w_hi, w_lo, v_ref):
    tz = t_ref[2, :, lanes]
    count = 3 * MODES
    both = dot_nn(f[n], w_hi[:, lanes])
    sums = both[:count] + both[count:] + dot_nn(f[n, :count, :], w_lo[:, lanes])
    for i in range(3):
        v_ref[n, i : i + 1, lanes] = jnp.sum(sums[i * MODES : (i + 1) * MODES, :] * tz, axis=0, keepdims=True)


def hot_rows(cell, xy_hot, depth):
    place = jnp.floor((cell - 1.0) * (1.0 / depth))
    xy_hot[...] = jnp.where(
        place == lax.broadcasted_iota(jnp.int32, xy_hot.shape, 0).astype(F32), 1.0, 0.0
    ).astype(BF16)


def hot_columns(along, first, last, z_hot):
    depth = z_hot.shape[1]
    sources = along.shape[0]
    lane = lax.broadcasted_iota(jnp.int32, (sources, depth), 1).astype(F32)
    for r in range(first, last):
        z_hot[r * sources : (r + 1) * sources, :] = jnp.where(along[:, r : r + 1] == lane, 1.0, 0.0).astype(BF16)


def spread_fields(v, xy_hot, z_hot, spread, forcing):
    cells = xy_hot.shape[0]
    v_hi, v_lo = split2(v)
    for i in range(3):
        spread[2 * i * cells : (2 * i + 1) * cells, :] = xy_hot[...] * v_hi[i : i + 1, :]
        spread[(2 * i + 1) * cells : (2 * i + 2) * cells, :] = xy_hot[...] * v_lo[i : i + 1, :]
    total = dot_nn(spread[...], z_hot[...])
    for i in range(3):
        forcing[i] = total[2 * i * cells : (2 * i + 1) * cells] + total[(2 * i + 1) * cells : (2 * i + 2) * cells]


def pack_points(owner, xyz, offset, send, split):
    in_x, in_z, in_y, in_group = split
    points = owner.shape[1]
    devices = in_x * in_z * in_y * in_group
    bits = [n.bit_length() - 1 for n in (in_group, in_x, in_z)]
    c = owner & (in_group - 1)
    x = (owner >> bits[0]) & (in_x - 1)
    z = (owner >> (bits[0] + bits[1])) & (in_z - 1)
    y = owner >> (bits[0] + bits[1] + bits[2])
    place = ((y * in_x + x) * in_z + z) * in_group + c
    hit = place == lax.broadcasted_iota(jnp.int32, (devices, points), 0)
    match = jnp.where(hit, 1.0, 0.0)
    match16 = match.astype(BF16)
    run = min(points, 128)
    rows, columns = (lax.broadcasted_iota(jnp.int32, (run, 2 * run), d) for d in (0, 1))
    before = jnp.where((rows < columns) | (columns >= run), 1.0, 0.0).astype(BF16)
    offset_in = jnp.zeros((devices, run), F32)
    ranks = []
    for at in range(0, points, run):
        sums = dot_nn(match16[:, at : at + run], before)
        ranks.append(jnp.sum((sums[:, :run] + offset_in) * match[:, at : at + run], axis=0, keepdims=True))
        offset_in = offset_in + sums[:, run:]
    rank = jnp.concatenate(ranks, axis=1)
    slot = rank == lax.broadcasted_iota(jnp.int32, (SLOTS, points), 0).astype(F32)
    values = [xyz[i : i + 1, :] for i in range(3)] + [(offset + 1).astype(F32)]
    spread = jnp.concatenate([jnp.where(slot, v, 0.0) for v in values], axis=0)
    first = spread.astype(BF16)
    second, third = split2(spread - first.astype(F32))
    rows = dot_nt(match16, first) + dot_nt(match16, second) + dot_nt(match16, third)
    inner = in_z * in_group
    for d in range(devices):
        send[d // inner, d % inner] = rows[d : d + 1, :]


def wave_kernel(
    split,
    current_in, earlier_in, coef_in, mask_in, owner_in, xyz_in, offset_in, wave_in, freq_in, amp_in, index_in, table_in,
    weight_in, column_in,
    held,
    coef, mask, sign, owner, xyz, offset, wave, freq, amp, index, table, weight, column, load_sem,
    comps, comp_send, comp_recv,
    sent, first, second, hop_send, hop_recv, hop_own,
    x_in, y_in, y_out, halo_send, halo_recv,
    far_in, corner_in, wide_send, wide_recv, push_in, push_out, coef_far, flat_send, flat_recv,
    q, p_hi, p_lo, f_ref, f_send, f_recv, f, t_ref, w_hi, w_lo, v_ref, xy_hot, z_hot, spread, forcing,
):
    in_x, in_z, in_y, in_group = split
    slabs = in_x * in_z * in_y
    slab, comp = lax.axis_index("slab"), lax.axis_index("comp")
    x, z, y = slab % in_x, slab // in_x % in_z, slab // (in_x * in_z)
    nx, ny, nz = coef.shape
    after, before = lax.rem(slab + 1, slabs), lax.rem(slab + slabs - 1, slabs)
    right, left = lax.rem(comp + 1, in_group), lax.rem(comp + in_group - 1, in_group)
    outer, inner = y * in_x + x, z * in_group + comp
    outers, inners = in_y * in_x, in_z * in_group

    def outer_at(d):
        there = lax.rem(outer + d, outers)
        return there, ((there // in_x * in_z + z) * in_x + there % in_x, comp)

    def inner_at(d):
        there = lax.rem(inner + d, inners)
        return there, ((y * in_z + there // in_group) * in_x + x, there % in_group)

    def group_at(d):
        return comp + lax.rem(d, 2) * (1 - 2 * lax.rem(comp, 2)) + (d // 2) * (2 - 4 * (comp // 2))

    barrier = pltpu.get_barrier_semaphore()
    partners = [outer_at(d)[1] for d in range(1, outers)]
    partners += [inner_at(d)[1] for d in range(1, inners)]
    partners += [(a, c) for a in (after, before) for c in (comp, left, right)]
    loads = [
        pltpu.make_async_copy(a, b, load_sem.at[i])
        for i, (a, b) in enumerate((
            (owner_in, owner), (xyz_in, xyz), (offset_in, offset),
            (wave_in, wave), (freq_in, freq), (amp_in, amp), (index_in, index), (table_in, table),
            (current_in, held.at[1]), (column_in, column), (weight_in, weight),
            (coef_in, coef), (earlier_in, held.at[0]), (mask_in, mask),
        ))
    ]
    for load in loads[:3]:
        load.start()
    for partner in partners:
        pl.semaphore_signal(barrier, inc=1, device_id=partner, device_id_type=MESH)
    for load in loads[3:]:
        load.start()
    for load in loads[:3]:
        load.wait()
    pack_points(owner[...], xyz[...], offset[...], sent, split)
    for load in loads[3:8]:
        load.wait()
    found = index[...] == lax.broadcasted_iota(jnp.int32, (table.shape[1], index.shape[1]), 0)
    phase = lax.dot_general(
        table[...], jnp.where(found, 1.0, 0.0), (((1,), (0,)), ((), ())),
        precision=lax.Precision.HIGHEST, preferred_element_type=F32,
    )
    comps[0, 0:3, :] = wave[...]
    comps[0, 3:4, :] = freq[...]
    comps[0, 4:7, :] = amp[...]
    comps[0, 7:8, :] = phase
    loads[8].wait()

    def halo_copies(e, u, c):
        faces = (
            (u.at[c, pl.ds(0, 2)], x_in.at[e, 1, c], (before, comp)),
            (u.at[c, pl.ds(nx - 2, 2)], x_in.at[e, 0, c], (after, comp)),
            (y_out.at[e, 0, c], y_in.at[e, 1, c], (slab, left)),
            (y_out.at[e, 1, c], y_in.at[e, 0, c], (slab, right)),
        )
        return [
            pltpu.make_async_remote_copy(
                src_ref=a, dst_ref=b, send_sem=halo_send.at[e, c, i], recv_sem=halo_recv.at[e, c, i],
                device_id=target, device_id_type=MESH,
            )
            for i, (a, b, target) in enumerate(faces)
        ]

    def start_x(e, u, c):
        for copy in halo_copies(e, u, c)[:2]:
            copy.start()

    def start_y(e, u, c):
        y_out[e, 0, c] = u[c, :, 0:2, :]
        y_out[e, 1, c] = u[c, :, ny - 2 : ny, :]
        for copy in halo_copies(e, u, c)[2:]:
            copy.start()

    def start_halo(e, u, c):
        start_x(e, u, c)
        start_y(e, u, c)

    def wait_halo(e, u, c, faces):
        for copy in halo_copies(e, u, c)[faces]:
            copy.wait()

    def wide_copies(c):
        u, edge = held.at[2], y_out.at[1]
        moves = (
            (u.at[c, pl.ds(2, 2)], far_in.at[1, c], (before, comp)),
            (u.at[c, pl.ds(nx - 4, 2)], far_in.at[0, c], (after, comp)),
            (edge.at[0, c, pl.ds(0, 2)], corner_in.at[1, 1, c], (before, left)),
            (edge.at[1, c, pl.ds(0, 2)], corner_in.at[1, 0, c], (before, right)),
            (edge.at[0, c, pl.ds(nx - 2, 2)], corner_in.at[0, 1, c], (after, left)),
            (edge.at[1, c, pl.ds(nx - 2, 2)], corner_in.at[0, 0, c], (after, right)),
        )
        return [
            pltpu.make_async_remote_copy(
                src_ref=a, dst_ref=b, send_sem=wide_send.at[c, i], recv_sem=wide_recv.at[c, i],
                device_id=target, device_id_type=MESH,
            )
            for i, (a, b, target) in enumerate(moves)
        ]

    def flat_copies(kind):
        if kind == 0:
            moves = (
                (coef.at[pl.ds(0, 2)], coef_far.at[1], (before, comp)),
                (coef.at[pl.ds(nx - 2, 2)], coef_far.at[0], (after, comp)),
            )
        else:
            moves = (
                (push_out.at[0], push_in.at[1], (before, comp)),
                (push_out.at[1], push_in.at[0], (after, comp)),
            )
        return [
            pltpu.make_async_remote_copy(
                src_ref=a, dst_ref=b, send_sem=flat_send.at[kind, i], recv_sem=flat_recv.at[kind, i],
                device_id=target, device_id_type=MESH,
            )
            for i, (a, b, target) in enumerate(moves)
        ]

    def comp_copy(d):
        return pltpu.make_async_remote_copy(
            src_ref=comps.at[0], dst_ref=comps.at[d], send_sem=comp_send.at[d], recv_sem=comp_recv.at[d],
            device_id=(slab, group_at(d)), device_id_type=MESH,
        )

    def hop_copies(hop):
        if hop == 0:
            moves = [(sent.at[outer_at(d)[0]], first.at[outer], outer_at(d)[1]) for d in range(outers)]
        else:
            moves = [(first.at[:, inner_at(d)[0]], second.at[inner], inner_at(d)[1]) for d in range(inners)]
        own = pltpu.make_async_copy(moves[0][0], moves[0][1], hop_own.at[hop])
        return [own] + [
            pltpu.make_async_remote_copy(
                src_ref=a, dst_ref=b, send_sem=hop_send.at[hop, d], recv_sem=hop_recv.at[hop, d],
                device_id=target, device_id_type=MESH,
            )
            for d, (a, b, target) in enumerate(moves) if d > 0
        ]

    def start_hop(hop):
        for copy in hop_copies(hop):
            copy.start()

    def wait_hop(hop):
        for copy in hop_copies(hop):
            copy.wait()

    pl.semaphore_wait(barrier, len(partners))
    start_hop(0)
    for d in range(1, in_group):
        comp_copy(d).start()
    for c in range(3):
        start_halo(0, held.at[1], c)
    for load in loads[9:]:
        load.wait()
    for copy in flat_copies(0):
        copy.start()
    sign[...] = jnp.where(mask[...] == 1, 1.0, 0.0) - jnp.where(mask[...] == 2, 1.0, 0.0)

    lane = lax.broadcasted_iota(jnp.int32, (ny, nz), 1)
    outside = [0, 1, nx - 2, nx - 1]
    inside = list(range(2, nx - 2))

    def curve(row, back, front):
        u = row[2]
        tall = jnp.concatenate([jnp.where(comp > 0, back, 0.0), u, jnp.where(comp < in_group - 1, front, 0.0)], axis=0)
        near = row[1] + row[3]
        far = row[0] + row[4]
        near = near + (tall[1 : ny + 1] + tall[3 : ny + 3])
        far = far + (tall[0:ny] + tall[4 : ny + 4])
        near = near + jnp.where(lane >= 1, pltpu.roll(u, 1, 1), 0.0)
        near = near + jnp.where(lane < nz - 1, pltpu.roll(u, nz - 1, 1), 0.0)
        far = far + jnp.where(lane >= 2, pltpu.roll(u, 2, 1), 0.0)
        far = far + jnp.where(lane < nz - 2, pltpu.roll(u, nz - 2, 1), 0.0)
        return centre_weight * u + near_weight * near + far_weight * far

    def advance(i, source, faces, send):
        def one(c, carry):
            wait_halo(i, held.at[i + 1], c, faces)
            low, high = x_in[i, 0, c], x_in[i, 1, c]
            low, high = jnp.where(slab > 0, low, 0.0), jnp.where(slab < slabs - 1, high, 0.0)
            planes = [low[0], low[1]] + [held[i + 1, c, x] for x in range(nx)] + [high[0], high[1]]
            for x in range(nx):
                curved = curve(planes[x : x + 5], y_in[i, 0, c, x], y_in[i, 1, c, x])
                following = 2.0 * planes[x + 2] - held[i, c, x] + coef[x] * curved
                if source is not None:
                    following = following + source(c, x)
                held[i + 2, c, x] = following
            if send:
                start_y(i + 1, held.at[i + 2], c)
            return carry

        lax.fori_loop(0, 3, one, 0)

    def advance_outside(c, carry):
        for copy in wide_copies(c):
            copy.wait()
        near, own = [x_in[1, side, c] for side in (0, 1)], held.at[2, c]
        low = [far_in[0, c, 0], far_in[0, c, 1], near[0][0], near[0][1], own[0], own[1]]
        high = [own[nx - 2], own[nx - 1], near[1][0], near[1][1], far_in[1, c, 0], far_in[1, c, 1]]
        for side, row in enumerate((low, high)):
            for k in (0, 1):
                curved = curve(row[k : k + 5], corner_in[side, 0, c, k], corner_in[side, 1, c, k])
                x_in[2, side, c, k] = (
                    2.0 * row[k + 2] - x_in[0, side, c, k] + coef_far[side, k] * curved + push_in[side, c, k]
                )
        return carry

    wide = 2 * HALF * HALF
    core = lax.rem(comp, 2)
    odd = core == 1
    f_ref[core] = jnp.zeros((FIELDS * MODES, wide), F32)

    def one_block(i, carry):
        @pl.when(i > 0)
        def _():
            comp_copy(i).wait()

        mode_sums(comps[i], weight[...], column[...], odd, q, p_hi, p_lo)
        f_ref[core] += mode_products(q, p_hi, p_lo)

        @pl.when(i == 2)
        def _():
            wait_hop(0)
            start_hop(1)

        return carry

    lax.fori_loop(0, in_group, one_block, 0)
    half_copies = [
        pltpu.make_async_remote_copy(
            src_ref=f_ref.at[core, pl.ds(n * 3 * MODES, 3 * MODES)],
            dst_ref=f_ref.at[core, pl.ds(n * 3 * MODES, 3 * MODES)],
            send_sem=f_send.at[n], recv_sem=f_recv.at[n],
            device_id=(slab, comp + 1 - 2 * core), device_id_type=MESH,
        )
        for n in range(STEPS)
    ]
    for copy in half_copies:
        copy.start()
    advance(0, None, slice(0, 4), False)
    wait_hop(1)
    arrived = second[...].reshape(slabs * in_group, 4 * SLOTS)
    px, py, pz, cell = slot_rows(arrived)
    point_modes([px, py, pz], t_ref)
    cells = arrived[:, 3 * SLOTS :] - 1.0
    along = cells - jnp.floor(cells * (1.0 / nz)) * nz
    def lanes_of(i, chunk):
        return pl.ds(pl.multiple_of(i * chunk, chunk), chunk)

    slots = t_ref.shape[2]
    narrow, broad = slots // 4, min(slots, 1024)
    point_products(t_ref, pl.ds(0, narrow), w_hi, w_lo)
    rows = 3 * MODES

    def take_half(n):
        half_copies[n].wait()
        for which in (0, 1):
            lanes = pl.ds(which * wide, wide)
            f[n, :rows, lanes], f[n, rows:, lanes] = split2(f_ref[which, n * rows : (n + 1) * rows, :])

    take_half(0)
    for i in range(4):
        point_sums(0, t_ref, pl.ds(i * narrow, narrow), f, w_hi, w_lo, v_ref)
        if i < 3:
            point_products(t_ref, pl.ds((i + 1) * narrow, narrow), w_hi, w_lo)
            hot_columns(along, i * SLOTS // 4, (i + 1) * SLOTS // 4, z_hot)
        else:
            hot_columns(along, i * SLOTS // 4, SLOTS, z_hot)
            hot_rows(cell, xy_hot, nz)
    spread_fields(v_ref[0], xy_hot, z_hot, spread, forcing)

    def source(c, x):
        return sign[x] * forcing[c, x * ny : (x + 1) * ny, :]

    def first_outside(c, carry):
        for x in outside:
            held[2, c, x] += source(c, x)
        start_x(1, held.at[2], c)
        return carry

    def first_inside(c, carry):
        for x in inside:
            held[2, c, x] += source(c, x)
        start_y(1, held.at[2], c)
        for copy in wide_copies(c):
            copy.start()
        return carry

    lax.fori_loop(0, 3, first_outside, 0)
    lax.fori_loop(0, 3, first_inside, 0)

    def next_forcing(n):
        take_half(n)

        def one_chunk(i, carry):
            point_sums(n, t_ref, lanes_of(i, broad), f, w_hi, w_lo, v_ref)
            return carry

        lax.fori_loop(0, slots // broad, one_chunk, 0)
        spread_fields(v_ref[n], xy_hot, z_hot, spread, forcing)

    next_forcing(1)

    def push(c, carry):
        for side, first_plane in enumerate((0, nx - 2)):
            for k in (0, 1):
                push_out[side, c, k] = source(c, first_plane + k)
        return carry

    lax.fori_loop(0, 3, push, 0)
    for copy in flat_copies(1):
        copy.start()
    advance(1, source, slice(0, 4), True)
    next_forcing(2)
    for kind in (0, 1):
        for copy in flat_copies(kind):
            copy.wait()
    lax.fori_loop(0, 3, advance_outside, 0)
    advance(2, source, slice(2, 4), False)


def local(current_field, earlier_field, wave_coef, layer_mask, point_xyz, point_owner, cell_offset, wave_vector, frequency, amplitude, phase_index, phase_table):
    slabs, in_group = lax.axis_size("slab"), lax.axis_size("comp")
    in_x, in_z = 4, 2
    in_y = slabs // (in_x * in_z)
    devices = slabs * in_group
    points = point_xyz.shape[1]
    width = frequency.shape[0]
    _, nx, ny, nz = current_field.shape
    modes = 4 * HALF * HALF
    slots = devices * SLOTS
    weight, column = mode_tables()
    operands = (
        current_field, earlier_field, wave_coef, layer_mask, point_owner.reshape(1, points), point_xyz,
        cell_offset.reshape(1, points), wave_vector, frequency.reshape(1, width), amplitude,
        phase_index.reshape(1, width), phase_table.reshape(1, -1), jnp.asarray(weight), jnp.asarray(column),
    )
    like = [pltpu.VMEM(a.shape, a.dtype) for a in operands]
    dma = pltpu.SemaphoreType.DMA
    exchanges = STEPS
    held = pl.pallas_call(
        functools.partial(wave_kernel, (in_x, in_z, in_y, in_group)),
        out_shape=pltpu.VMEM((STEPS + 2, 3, nx, ny, nz), F32),
        in_specs=[pl.BlockSpec(memory_space=pl.ANY)] * len(operands),
        out_specs=pl.BlockSpec(memory_space=pltpu.VMEM),
        scratch_shapes=[
            like[2], like[3], pltpu.VMEM((nx, ny, nz), F32), *like[4:], dma((len(operands),)),
            pltpu.VMEM((in_group, 8, width), F32), dma((in_group,)), dma((in_group,)),
            pltpu.VMEM((in_y * in_x, in_z * in_group, 1, 4 * SLOTS), F32),
            pltpu.VMEM((in_y * in_x, in_z * in_group, 1, 4 * SLOTS), F32),
            pltpu.VMEM((in_z * in_group, in_y * in_x, 1, 4 * SLOTS), F32),
            dma((2, in_y * in_x)), dma((2, in_y * in_x)), dma((2,)),
            pltpu.VMEM((exchanges, 2, 3, 2, ny, nz), F32),
            pltpu.VMEM((exchanges, 2, 3, nx, 2, nz), F32),
            pltpu.VMEM((exchanges, 2, 3, nx, 2, nz), F32),
            dma((exchanges, 3, 4)), dma((exchanges, 3, 4)),
            pltpu.VMEM((2, 3, 2, ny, nz), F32), pltpu.VMEM((2, 2, 3, 2, 2, nz), F32), dma((3, 6)), dma((3, 6)),
            pltpu.VMEM((2, 3, 2, ny, nz), F32), pltpu.VMEM((2, 3, 2, ny, nz), F32), pltpu.VMEM((2, 2, ny, nz), F32),
            dma((2, 2)), dma((2, 2)),
            pltpu.VMEM((2 * FIELDS * MODES, width), BF16),
            pltpu.VMEM((modes // 2, width), BF16),
            pltpu.VMEM((modes // 2, width), BF16),
            pltpu.VMEM((2, FIELDS * MODES, modes // 2), F32), dma((STEPS,)), dma((STEPS,)),
            pltpu.VMEM((STEPS, 6 * MODES, modes), BF16),
            pltpu.VMEM((3, MODES, slots), F32),
            pltpu.VMEM((modes, slots), BF16),
            pltpu.VMEM((modes, slots), BF16),
            pltpu.VMEM((STEPS, 3, slots), F32),
            pltpu.VMEM((nx * ny, slots), BF16),
            pltpu.VMEM((slots, nz), BF16),
            pltpu.VMEM((6 * nx * ny, slots), BF16),
            pltpu.VMEM((3, nx * ny, nz), F32),
        ],
        compiler_params=pltpu.CompilerParams(
            collective_id=0, has_side_effects=True, vmem_limit_bytes=59200 << 10
        ),
    )(*operands)
    return held[STEPS + 1], held[STEPS]


def solution(mesh):
    in_specs = (
        P(None, "slab", "comp", None),
        P(None, "slab", "comp", None),
        P("slab", "comp", None),
        P("slab", "comp", None),
        P(None, ("slab", "comp")),
        P(("slab", "comp"), None),
        P(("slab", "comp")),
        P(None, "comp"),
        P("comp"),
        P(None, "comp"),
        P("comp"),
        P(),
    )
    out_specs = (P(None, "slab", "comp", None), P(None, "slab", "comp", None))
    return jax.shard_map(local, mesh=mesh, in_specs=in_specs, out_specs=out_specs, check_vma=False)
```

```python
import functools

import jax
import jax.numpy as jnp
import numpy as np
from jax import lax
from jax.experimental import pallas as pl
from jax.experimental.pallas import tpu as pltpu
from jax.sharding import PartitionSpec as P

STEPS = 3
SLOTS = 16
HALF = 16
MODES = 2 * HALF
FIELDS = 9
F32 = jnp.float32
BF16 = jnp.bfloat16
MESH = pl.DeviceIdType.MESH

step_size = 0.05
near_weight = 4.0 / 3.0
far_weight = -1.0 / 12.0
centre_weight = -7.5


def turn_series(degree):
    fits = []
    for h in (
        lambda s: np.cos(2 * np.pi * np.sqrt(s)),
        lambda s: np.sinc(2 * np.sqrt(s)) * 2 * np.pi,
    ):
        fit = np.polynomial.chebyshev.Chebyshev.interpolate(h, degree, domain=[0, 0.25])
        fits.append([float(c) for c in fit.convert(kind=np.polynomial.Polynomial).coef])
    return fits


COS_SERIES, SIN_SERIES = turn_series(7)


def horner(series, s):
    total = jnp.full_like(s, series[-1])
    for c in series[-2::-1]:
        total = total * s + c
    return total


def cos_sin_turns(u):
    r = u - jnp.round(u)
    s = r * r
    return horner(COS_SERIES, s), r * horner(SIN_SERIES, s)


def mode_tables():
    a = np.arange(HALF)
    angle = (2 * a + 1) * np.pi / (2 * MODES)
    nodes = np.cos(angle)
    weight = np.zeros((6 * HALF, 6 * HALF))
    for dim in range(3):
        for parity in (0, 1):
            m = 2 * np.arange(HALF) + parity
            block = 4.0 / MODES * np.cos(m[:, None] * angle[None, :])
            if parity == 0:
                block[0] *= 0.5
            at = (parity * 3 + dim) * HALF
            weight[at : at + HALF, at : at + HALF] = block
    column = np.tile(nodes, 3)[:, None] * np.ones((1, 128))
    return weight.astype(np.float32), column.astype(np.float32)


def split2(x):
    high = x.astype(BF16)
    return high, (x - high.astype(F32)).astype(BF16)


def dot_nt(a, b):
    return lax.dot_general(a, b, (((1,), (1,)), ((), ())), preferred_element_type=F32)


def dot_nn(a, b):
    return lax.dot_general(a, b, (((1,), (0,)), ((), ())), preferred_element_type=F32)


def mode_sums(block, weight, column, odd, q, p_hi, p_lo):
    turn = 1.0 / (2.0 * np.pi)
    rows = FIELDS * MODES
    angles = jnp.concatenate(
        [column[d * HALF : (d + 1) * HALF, 0:1] * (block[d : d + 1, :] * (2.0 * turn)) for d in range(3)], axis=0
    )
    cosine, sine = cos_sin_turns(angles)
    series = lax.dot_general(
        weight, jnp.concatenate([cosine, sine], axis=0), (((1,), (0,)), ((), ())),
        precision=lax.Precision.HIGHEST, preferred_element_type=F32,
    )
    cx, cy, cz, sx, sy, sz = [series[i * HALF : (i + 1) * HALF, :] for i in range(6)]
    centre = (2.0 * turn) * (block[0:1, :] + block[1:2, :] + block[2:3, :]) + turn * block[7:8, :]
    for n in range(STEPS):
        shift_cos, shift_sin = cos_sin_turns(centre - block[3:4, :] * (turn * step_size * (n + 1)))
        outer = jnp.where(odd, -shift_sin, shift_cos)
        inner = jnp.where(odd, -shift_cos, -shift_sin)
        for i in range(3):
            amp = block[4 + i : 5 + i, :]
            at = (3 * n + i) * MODES
            for part, value in ((0, (amp * outer) * cz), (1, (amp * inner) * sz)):
                low = at + part * HALF
                q[low : low + HALF, :], q[rows + low : rows + low + HALF, :] = split2(value)
    even_y = jnp.where(odd, sy, cy)
    odd_y = jnp.where(odd, cy, -sy)
    for m in range(HALF):
        rows_a, rows_b = pl.ds(m * HALF, HALF), pl.ds((HALF + m) * HALF, HALF)
        p_hi[rows_a, :], p_lo[rows_a, :] = split2(cx[m : m + 1, :] * even_y)
        p_hi[rows_b, :], p_lo[rows_b, :] = split2(sx[m : m + 1, :] * odd_y)


def mode_products(q, p_hi, p_lo):
    rows = FIELDS * MODES
    both = dot_nt(q[...], p_hi[...])
    return both[:rows] + both[rows:] + dot_nt(q[:rows, :], p_lo[...])


def slot_rows(arrived):
    turned = arrived.T
    return [
        jnp.concatenate([turned[c * SLOTS + r : c * SLOTS + r + 1, :] for r in range(SLOTS)], axis=1)
        for c in range(4)
    ]


def point_modes(rows, t_ref):
    tau = jnp.concatenate([(r - 2.0) * 0.5 for r in rows], axis=0)
    older, old = jnp.ones_like(tau), tau
    for m in range(MODES):
        at = (m % 2) * HALF + m // 2
        for d in range(3):
            t_ref[d, at : at + 1, :] = older[d : d + 1, :]
        older, old = old, 2.0 * tau * old - older


def point_products(t_ref, lanes, w_hi, w_lo):
    tx, ty = t_ref[0, :, lanes], t_ref[1, :, lanes]
    half = [slice(0, HALF), slice(HALF, MODES)]
    for combo, (px, py) in enumerate(((0, 0), (1, 1), (0, 1), (1, 0))):
        other = ty[half[py], :]
        for m in range(HALF):
            rows = pl.ds((combo * HALF + m) * HALF, HALF)
            at = px * HALF + m
            w_hi[rows, lanes], w_lo[rows, lanes] = split2(tx[at : at + 1, :] * other)


def point_sums(n, t_ref, lanes, f, w_hi, w_lo, v_ref):
    tz = t_ref[2, :, lanes]
    count = 3 * MODES
    both = dot_nn(f[n], w_hi[:, lanes])
    sums = both[:count] + both[count:] + dot_nn(f[n, :count, :], w_lo[:, lanes])
    for i in range(3):
        v_ref[n, i : i + 1, lanes] = jnp.sum(sums[i * MODES : (i + 1) * MODES, :] * tz, axis=0, keepdims=True)


def hot_rows(cell, xy_hot, depth):
    place = jnp.floor((cell - 1.0) * (1.0 / depth))
    xy_hot[...] = jnp.where(
        place == lax.broadcasted_iota(jnp.int32, xy_hot.shape, 0).astype(F32), 1.0, 0.0
    ).astype(BF16)


def hot_columns(along, first, last, z_hot):
    depth = z_hot.shape[1]
    sources = along.shape[0]
    lane = lax.broadcasted_iota(jnp.int32, (sources, depth), 1).astype(F32)
    for r in range(first, last):
        z_hot[r * sources : (r + 1) * sources, :] = jnp.where(along[:, r : r + 1] == lane, 1.0, 0.0).astype(BF16)


def spread_fields(v, xy_hot, z_hot, spread, forcing):
    cells = xy_hot.shape[0]
    v_hi, v_lo = split2(v)
    for i in range(3):
        spread[2 * i * cells : (2 * i + 1) * cells, :] = xy_hot[...] * v_hi[i : i + 1, :]
        spread[(2 * i + 1) * cells : (2 * i + 2) * cells, :] = xy_hot[...] * v_lo[i : i + 1, :]
    total = dot_nn(spread[...], z_hot[...])
    for i in range(3):
        forcing[i] = total[2 * i * cells : (2 * i + 1) * cells] + total[(2 * i + 1) * cells : (2 * i + 2) * cells]


def pack_points(owner, xyz, offset, send, split):
    in_x, in_z, in_y, in_group = split
    points = owner.shape[1]
    devices = in_x * in_z * in_y * in_group
    bits = [n.bit_length() - 1 for n in (in_group, in_x, in_z)]
    c = owner & (in_group - 1)
    x = (owner >> bits[0]) & (in_x - 1)
    z = (owner >> (bits[0] + bits[1])) & (in_z - 1)
    y = owner >> (bits[0] + bits[1] + bits[2])
    place = ((y * in_x + x) * in_z + z) * in_group + c
    hit = place == lax.broadcasted_iota(jnp.int32, (devices, points), 0)
    match = jnp.where(hit, 1.0, 0.0)
    match16 = match.astype(BF16)
    run = min(points, 128)
    rows, columns = (lax.broadcasted_iota(jnp.int32, (run, 2 * run), d) for d in (0, 1))
    before = jnp.where((rows < columns) | (columns >= run), 1.0, 0.0).astype(BF16)
    offset_in = jnp.zeros((devices, run), F32)
    ranks = []
    for at in range(0, points, run):
        sums = dot_nn(match16[:, at : at + run], before)
        ranks.append(jnp.sum((sums[:, :run] + offset_in) * match[:, at : at + run], axis=0, keepdims=True))
        offset_in = offset_in + sums[:, run:]
    rank = jnp.concatenate(ranks, axis=1)
    slot = rank == lax.broadcasted_iota(jnp.int32, (SLOTS, points), 0).astype(F32)
    values = [xyz[i : i + 1, :] for i in range(3)] + [(offset + 1).astype(F32)]
    spread = jnp.concatenate([jnp.where(slot, v, 0.0) for v in values], axis=0)
    first = spread.astype(BF16)
    second, third = split2(spread - first.astype(F32))
    rows = dot_nt(match16, first) + dot_nt(match16, second) + dot_nt(match16, third)
    inner = in_z * in_group
    for d in range(devices):
        send[d // inner, d % inner] = rows[d : d + 1, :]


def wave_kernel(
    split,
    current_in, earlier_in, coef_in, mask_in, owner_in, xyz_in, offset_in, wave_in, freq_in, amp_in, index_in, table_in,
    weight_in, column_in,
    held,
    coef, mask, sign, owner, xyz, offset, wave, freq, amp, index, table, weight, column, load_sem,
    comps, comp_send, comp_recv,
    sent, first, second, hop_send, hop_recv, hop_own,
    x_in, y_in, y_out, halo_send, halo_recv,
    q, p_hi, p_lo, f_ref, f_send, f_recv, f, t_ref, w_hi, w_lo, v_ref, xy_hot, z_hot, spread, forcing,
):
    in_x, in_z, in_y, in_group = split
    slabs = in_x * in_z * in_y
    slab, comp = lax.axis_index("slab"), lax.axis_index("comp")
    x, z, y = slab % in_x, slab // in_x % in_z, slab // (in_x * in_z)
    nx, ny, nz = coef.shape
    after, before = lax.rem(slab + 1, slabs), lax.rem(slab + slabs - 1, slabs)
    right, left = lax.rem(comp + 1, in_group), lax.rem(comp + in_group - 1, in_group)
    outer, inner = y * in_x + x, z * in_group + comp
    outers, inners = in_y * in_x, in_z * in_group

    def outer_at(d):
        there = lax.rem(outer + d, outers)
        return there, ((there // in_x * in_z + z) * in_x + there % in_x, comp)

    def inner_at(d):
        there = lax.rem(inner + d, inners)
        return there, ((y * in_z + there // in_group) * in_x + x, there % in_group)

    def group_at(d):
        return comp + lax.rem(d, 2) * (1 - 2 * lax.rem(comp, 2)) + (d // 2) * (2 - 4 * (comp // 2))

    barrier = pltpu.get_barrier_semaphore()
    partners = [outer_at(d)[1] for d in range(1, outers)]
    partners += [inner_at(d)[1] for d in range(1, inners)]
    partners += [(after, comp), (before, comp)]
    loads = [
        pltpu.make_async_copy(a, b, load_sem.at[i])
        for i, (a, b) in enumerate((
            (owner_in, owner), (xyz_in, xyz), (offset_in, offset),
            (wave_in, wave), (freq_in, freq), (amp_in, amp), (index_in, index), (table_in, table),
            (current_in, held.at[1]), (column_in, column), (weight_in, weight),
            (coef_in, coef), (earlier_in, held.at[0]), (mask_in, mask),
        ))
    ]
    for load in loads[:3]:
        load.start()
    for partner in partners:
        pl.semaphore_signal(barrier, inc=1, device_id=partner, device_id_type=MESH)
    for load in loads[3:]:
        load.start()
    for load in loads[:3]:
        load.wait()
    pack_points(owner[...], xyz[...], offset[...], sent, split)
    for load in loads[3:8]:
        load.wait()
    found = index[...] == lax.broadcasted_iota(jnp.int32, (table.shape[1], index.shape[1]), 0)
    phase = lax.dot_general(
        table[...], jnp.where(found, 1.0, 0.0), (((1,), (0,)), ((), ())),
        precision=lax.Precision.HIGHEST, preferred_element_type=F32,
    )
    comps[0, 0:3, :] = wave[...]
    comps[0, 3:4, :] = freq[...]
    comps[0, 4:7, :] = amp[...]
    comps[0, 7:8, :] = phase
    loads[8].wait()

    def halo_copies(e, u, c):
        faces = (
            (u.at[c, pl.ds(0, 2)], x_in.at[e, 1, c], (before, comp)),
            (u.at[c, pl.ds(nx - 2, 2)], x_in.at[e, 0, c], (after, comp)),
            (y_out.at[e, 0, c], y_in.at[e, 1, c], (slab, left)),
            (y_out.at[e, 1, c], y_in.at[e, 0, c], (slab, right)),
        )
        return [
            pltpu.make_async_remote_copy(
                src_ref=a, dst_ref=b, send_sem=halo_send.at[e, c, i], recv_sem=halo_recv.at[e, c, i],
                device_id=target, device_id_type=MESH,
            )
            for i, (a, b, target) in enumerate(faces)
        ]

    def start_x(e, u, c):
        for copy in halo_copies(e, u, c)[:2]:
            copy.start()

    def start_y(e, u, c):
        y_out[e, 0, c] = u[c, :, 0:2, :]
        y_out[e, 1, c] = u[c, :, ny - 2 : ny, :]
        for copy in halo_copies(e, u, c)[2:]:
            copy.start()

    def start_halo(e, u, c):
        start_x(e, u, c)
        start_y(e, u, c)

    def wait_halo(e, u, c, faces):
        for copy in halo_copies(e, u, c)[faces]:
            copy.wait()

    def comp_copy(d):
        return pltpu.make_async_remote_copy(
            src_ref=comps.at[0], dst_ref=comps.at[d], send_sem=comp_send.at[d], recv_sem=comp_recv.at[d],
            device_id=(slab, group_at(d)), device_id_type=MESH,
        )

    def hop_copies(hop):
        if hop == 0:
            moves = [(sent.at[outer_at(d)[0]], first.at[outer], outer_at(d)[1]) for d in range(outers)]
        else:
            moves = [(first.at[:, inner_at(d)[0]], second.at[inner], inner_at(d)[1]) for d in range(inners)]
        own = pltpu.make_async_copy(moves[0][0], moves[0][1], hop_own.at[hop])
        return [own] + [
            pltpu.make_async_remote_copy(
                src_ref=a, dst_ref=b, send_sem=hop_send.at[hop, d], recv_sem=hop_recv.at[hop, d],
                device_id=target, device_id_type=MESH,
            )
            for d, (a, b, target) in enumerate(moves) if d > 0
        ]

    def start_hop(hop):
        for copy in hop_copies(hop):
            copy.start()

    def wait_hop(hop):
        for copy in hop_copies(hop):
            copy.wait()

    pl.semaphore_wait(barrier, len(partners))
    start_hop(0)
    for d in range(1, in_group):
        comp_copy(d).start()
    for c in range(3):
        start_halo(0, held.at[1], c)
    for load in loads[9:]:
        load.wait()
    sign[...] = jnp.where(mask[...] == 1, 1.0, 0.0) - jnp.where(mask[...] == 2, 1.0, 0.0)

    lane = lax.broadcasted_iota(jnp.int32, (ny, nz), 1)
    outside = [0, 1, nx - 2, nx - 1]
    inside = list(range(2, nx - 2))

    def advance(i, source, send):
        def some(c, planes, which):
            for x in which:
                u = planes[x + 2]
                back = jnp.where(comp > 0, y_in[i, 0, c, x], 0.0)
                front = jnp.where(comp < in_group - 1, y_in[i, 1, c, x], 0.0)
                tall = jnp.concatenate([back, u, front], axis=0)
                near = planes[x + 1] + planes[x + 3]
                far = planes[x] + planes[x + 4]
                near = near + (tall[1 : ny + 1] + tall[3 : ny + 3])
                far = far + (tall[0:ny] + tall[4 : ny + 4])
                near = near + jnp.where(lane >= 1, pltpu.roll(u, 1, 1), 0.0)
                near = near + jnp.where(lane < nz - 1, pltpu.roll(u, nz - 1, 1), 0.0)
                far = far + jnp.where(lane >= 2, pltpu.roll(u, 2, 1), 0.0)
                far = far + jnp.where(lane < nz - 2, pltpu.roll(u, nz - 2, 1), 0.0)
                curved = centre_weight * u + near_weight * near + far_weight * far
                following = 2.0 * u - held[i, c, x] + coef[x] * curved
                if source is not None:
                    following = following + source(c, x)
                held[i + 2, c, x] = following

        def inner_planes(c, carry):
            wait_halo(i, held.at[i + 1], c, slice(2, 4))
            some(c, [None, None] + [held[i + 1, c, x] for x in range(nx)], inside)
            return carry

        def outer_planes(c, carry):
            wait_halo(i, held.at[i + 1], c, slice(0, 2))
            low, high = x_in[i, 0, c], x_in[i, 1, c]
            low, high = jnp.where(slab > 0, low, 0.0), jnp.where(slab < slabs - 1, high, 0.0)
            some(c, [low[0], low[1]] + [held[i + 1, c, x] for x in range(nx)] + [high[0], high[1]], outside)
            if send is not None:
                @pl.when(send)
                def _():
                    start_halo(i + 1, held.at[i + 2], c)

            return carry

        lax.fori_loop(0, 3, inner_planes, 0)
        lax.fori_loop(0, 3, outer_planes, 0)

    wide = 2 * HALF * HALF
    core = lax.rem(comp, 2)
    odd = core == 1
    f_ref[core] = jnp.zeros((FIELDS * MODES, wide), F32)

    def one_block(i, carry):
        @pl.when(i > 0)
        def _():
            comp_copy(i).wait()

        mode_sums(comps[i], weight[...], column[...], odd, q, p_hi, p_lo)
        f_ref[core] += mode_products(q, p_hi, p_lo)

        @pl.when(i == 2)
        def _():
            wait_hop(0)
            start_hop(1)

        return carry

    lax.fori_loop(0, in_group, one_block, 0)
    half_copies = [
        pltpu.make_async_remote_copy(
            src_ref=f_ref.at[core, pl.ds(n * 3 * MODES, 3 * MODES)],
            dst_ref=f_ref.at[core, pl.ds(n * 3 * MODES, 3 * MODES)],
            send_sem=f_send.at[n], recv_sem=f_recv.at[n],
            device_id=(slab, comp + 1 - 2 * core), device_id_type=MESH,
        )
        for n in range(STEPS)
    ]
    for copy in half_copies:
        copy.start()
    advance(0, None, None)
    wait_hop(1)
    arrived = second[...].reshape(slabs * in_group, 4 * SLOTS)
    px, py, pz, cell = slot_rows(arrived)
    point_modes([px, py, pz], t_ref)
    cells = arrived[:, 3 * SLOTS :] - 1.0
    along = cells - jnp.floor(cells * (1.0 / nz)) * nz
    def lanes_of(i, chunk):
        return pl.ds(pl.multiple_of(i * chunk, chunk), chunk)

    slots = t_ref.shape[2]
    narrow, broad = slots // 4, min(slots, 1024)
    point_products(t_ref, pl.ds(0, narrow), w_hi, w_lo)
    rows = 3 * MODES

    def take_half(n):
        half_copies[n].wait()
        for which in (0, 1):
            lanes = pl.ds(which * wide, wide)
            f[n, :rows, lanes], f[n, rows:, lanes] = split2(f_ref[which, n * rows : (n + 1) * rows, :])

    take_half(0)
    for i in range(4):
        point_sums(0, t_ref, pl.ds(i * narrow, narrow), f, w_hi, w_lo, v_ref)
        if i < 3:
            point_products(t_ref, pl.ds((i + 1) * narrow, narrow), w_hi, w_lo)
            hot_columns(along, i * SLOTS // 4, (i + 1) * SLOTS // 4, z_hot)
        else:
            hot_columns(along, i * SLOTS // 4, SLOTS, z_hot)
            hot_rows(cell, xy_hot, nz)
    spread_fields(v_ref[0], xy_hot, z_hot, spread, forcing)

    def source(c, x):
        return sign[x] * forcing[c, x * ny : (x + 1) * ny, :]

    def first_outside(c, carry):
        for x in outside:
            held[2, c, x] += source(c, x)
        start_x(1, held.at[2], c)
        return carry

    def first_inside(c, carry):
        for x in inside:
            held[2, c, x] += source(c, x)
        start_y(1, held.at[2], c)
        return carry

    lax.fori_loop(0, 3, first_outside, 0)
    lax.fori_loop(0, 3, first_inside, 0)

    def one_step(n, carry):
        for step in range(1, STEPS):
            @pl.when(n == step)
            def _(step=step):
                take_half(step)

        def one_chunk(i, inner):
            point_sums(n, t_ref, lanes_of(i, broad), f, w_hi, w_lo, v_ref)
            return inner

        lax.fori_loop(0, slots // broad, one_chunk, 0)
        spread_fields(v_ref[n], xy_hot, z_hot, spread, forcing)

        advance(n, source, n < STEPS - 1)
        return carry

    lax.fori_loop(1, STEPS, one_step, 0)

def local(current_field, earlier_field, wave_coef, layer_mask, point_xyz, point_owner, cell_offset, wave_vector, frequency, amplitude, phase_index, phase_table):
    slabs, in_group = lax.axis_size("slab"), lax.axis_size("comp")
    in_x, in_z = 4, 2
    in_y = slabs // (in_x * in_z)
    devices = slabs * in_group
    points = point_xyz.shape[1]
    width = frequency.shape[0]
    _, nx, ny, nz = current_field.shape
    modes = 4 * HALF * HALF
    slots = devices * SLOTS
    weight, column = mode_tables()
    operands = (
        current_field, earlier_field, wave_coef, layer_mask, point_owner.reshape(1, points), point_xyz,
        cell_offset.reshape(1, points), wave_vector, frequency.reshape(1, width), amplitude,
        phase_index.reshape(1, width), phase_table.reshape(1, -1), jnp.asarray(weight), jnp.asarray(column),
    )
    like = [pltpu.VMEM(a.shape, a.dtype) for a in operands]
    dma = pltpu.SemaphoreType.DMA
    exchanges = STEPS
    held = pl.pallas_call(
        functools.partial(wave_kernel, (in_x, in_z, in_y, in_group)),
        out_shape=pltpu.VMEM((STEPS + 2, 3, nx, ny, nz), F32),
        in_specs=[pl.BlockSpec(memory_space=pl.ANY)] * len(operands),
        out_specs=pl.BlockSpec(memory_space=pltpu.VMEM),
        scratch_shapes=[
            like[2], like[3], pltpu.VMEM((nx, ny, nz), F32), *like[4:], dma((len(operands),)),
            pltpu.VMEM((in_group, 8, width), F32), dma((in_group,)), dma((in_group,)),
            pltpu.VMEM((in_y * in_x, in_z * in_group, 1, 4 * SLOTS), F32),
            pltpu.VMEM((in_y * in_x, in_z * in_group, 1, 4 * SLOTS), F32),
            pltpu.VMEM((in_z * in_group, in_y * in_x, 1, 4 * SLOTS), F32),
            dma((2, in_y * in_x)), dma((2, in_y * in_x)), dma((2,)),
            pltpu.VMEM((exchanges, 2, 3, 2, ny, nz), F32),
            pltpu.VMEM((exchanges, 2, 3, nx, 2, nz), F32),
            pltpu.VMEM((exchanges, 2, 3, nx, 2, nz), F32),
            dma((exchanges, 3, 4)), dma((exchanges, 3, 4)),
            pltpu.VMEM((2 * FIELDS * MODES, width), BF16),
            pltpu.VMEM((modes // 2, width), BF16),
            pltpu.VMEM((modes // 2, width), BF16),
            pltpu.VMEM((2, FIELDS * MODES, modes // 2), F32), dma((STEPS,)), dma((STEPS,)),
            pltpu.VMEM((STEPS, 6 * MODES, modes), BF16),
            pltpu.VMEM((3, MODES, slots), F32),
            pltpu.VMEM((modes, slots), BF16),
            pltpu.VMEM((modes, slots), BF16),
            pltpu.VMEM((STEPS, 3, slots), F32),
            pltpu.VMEM((nx * ny, slots), BF16),
            pltpu.VMEM((slots, nz), BF16),
            pltpu.VMEM((6 * nx * ny, slots), BF16),
            pltpu.VMEM((3, nx * ny, nz), F32),
        ],
        compiler_params=pltpu.CompilerParams(
            collective_id=0, has_side_effects=True, vmem_limit_bytes=59200 << 10
        ),
    )(*operands)
    return held[STEPS + 1], held[STEPS]


def solution(mesh):
    in_specs = (
        P(None, "slab", "comp", None),
        P(None, "slab", "comp", None),
        P("slab", "comp", None),
        P("slab", "comp", None),
        P(None, ("slab", "comp")),
        P(("slab", "comp"), None),
        P(("slab", "comp")),
        P(None, "comp"),
        P("comp"),
        P(None, "comp"),
        P("comp"),
        P(),
    )
    out_specs = (P(None, "slab", "comp", None), P(None, "slab", "comp", None))
    return jax.shard_map(local, mesh=mesh, in_specs=in_specs, out_specs=out_specs, check_vma=False)
```

```python
import functools

import jax
import jax.numpy as jnp
import numpy as np
from jax import lax
from jax.experimental import pallas as pl
from jax.experimental.pallas import tpu as pltpu
from jax.sharding import PartitionSpec as P

STEPS = 3
SLOTS = 16
HALF = 16
MODES = 2 * HALF
FIELDS = 9
F32 = jnp.float32
BF16 = jnp.bfloat16
MESH = pl.DeviceIdType.MESH

step_size = 0.05
near_weight = 4.0 / 3.0
far_weight = -1.0 / 12.0
centre_weight = -7.5


def turn_series(degree):
    fits = []
    for h in (
        lambda s: np.cos(2 * np.pi * np.sqrt(s)),
        lambda s: np.sinc(2 * np.sqrt(s)) * 2 * np.pi,
    ):
        fit = np.polynomial.chebyshev.Chebyshev.interpolate(h, degree, domain=[0, 0.25])
        fits.append([float(c) for c in fit.convert(kind=np.polynomial.Polynomial).coef])
    return fits


COS_SERIES, SIN_SERIES = turn_series(7)


def horner(series, s):
    total = jnp.full_like(s, series[-1])
    for c in series[-2::-1]:
        total = total * s + c
    return total


def cos_sin_turns(u):
    r = u - jnp.round(u)
    s = r * r
    return horner(COS_SERIES, s), r * horner(SIN_SERIES, s)


def mode_tables():
    a = np.arange(HALF)
    angle = (2 * a + 1) * np.pi / (2 * MODES)
    nodes = np.cos(angle)
    weight = np.zeros((6 * HALF, 6 * HALF))
    for dim in range(3):
        for parity in (0, 1):
            m = 2 * np.arange(HALF) + parity
            block = 4.0 / MODES * np.cos(m[:, None] * angle[None, :])
            if parity == 0:
                block[0] *= 0.5
            at = (parity * 3 + dim) * HALF
            weight[at : at + HALF, at : at + HALF] = block
    column = np.tile(nodes, 3)[:, None] * np.ones((1, 128))
    return weight.astype(np.float32), column.astype(np.float32)


def split2(x):
    high = x.astype(BF16)
    return high, (x - high.astype(F32)).astype(BF16)


def dot_nt(a, b):
    return lax.dot_general(a, b, (((1,), (1,)), ((), ())), preferred_element_type=F32)


def dot_nn(a, b):
    return lax.dot_general(a, b, (((1,), (0,)), ((), ())), preferred_element_type=F32)


def mode_sums(block, weight, column, odd, q, p_hi, p_lo):
    turn = 1.0 / (2.0 * np.pi)
    rows = FIELDS * MODES
    angles = jnp.concatenate(
        [column[d * HALF : (d + 1) * HALF, 0:1] * (block[d : d + 1, :] * (2.0 * turn)) for d in range(3)], axis=0
    )
    cosine, sine = cos_sin_turns(angles)
    series = lax.dot_general(
        weight, jnp.concatenate([cosine, sine], axis=0), (((1,), (0,)), ((), ())),
        precision=lax.Precision.HIGHEST, preferred_element_type=F32,
    )
    cx, cy, cz, sx, sy, sz = [series[i * HALF : (i + 1) * HALF, :] for i in range(6)]
    centre = (2.0 * turn) * (block[0:1, :] + block[1:2, :] + block[2:3, :]) + turn * block[7:8, :]
    for n in range(STEPS):
        shift_cos, shift_sin = cos_sin_turns(centre - block[3:4, :] * (turn * step_size * (n + 1)))
        outer = jnp.where(odd, -shift_sin, shift_cos)
        inner = jnp.where(odd, -shift_cos, -shift_sin)
        for i in range(3):
            amp = block[4 + i : 5 + i, :]
            at = (3 * n + i) * MODES
            for part, value in ((0, (amp * outer) * cz), (1, (amp * inner) * sz)):
                low = at + part * HALF
                q[low : low + HALF, :], q[rows + low : rows + low + HALF, :] = split2(value)
    even_y = jnp.where(odd, sy, cy)
    odd_y = jnp.where(odd, cy, -sy)
    for m in range(HALF):
        rows_a, rows_b = pl.ds(m * HALF, HALF), pl.ds((HALF + m) * HALF, HALF)
        p_hi[rows_a, :], p_lo[rows_a, :] = split2(cx[m : m + 1, :] * even_y)
        p_hi[rows_b, :], p_lo[rows_b, :] = split2(sx[m : m + 1, :] * odd_y)


def mode_products(q, p_hi, p_lo):
    rows = FIELDS * MODES
    both = dot_nt(q[...], p_hi[...])
    return both[:rows] + both[rows:] + dot_nt(q[:rows, :], p_lo[...])


def slot_rows(arrived):
    turned = arrived.T
    return [
        jnp.concatenate([turned[c * SLOTS + r : c * SLOTS + r + 1, :] for r in range(SLOTS)], axis=1)
        for c in range(4)
    ]


def point_modes(rows, t_ref):
    tau = jnp.concatenate([(r - 2.0) * 0.5 for r in rows], axis=0)
    older, old = jnp.ones_like(tau), tau
    for m in range(MODES):
        at = (m % 2) * HALF + m // 2
        for d in range(3):
            t_ref[d, at : at + 1, :] = older[d : d + 1, :]
        older, old = old, 2.0 * tau * old - older


def point_products(t_ref, lanes, w_hi, w_lo):
    tx, ty = t_ref[0, :, lanes], t_ref[1, :, lanes]
    half = [slice(0, HALF), slice(HALF, MODES)]
    for combo, (px, py) in enumerate(((0, 0), (1, 1), (0, 1), (1, 0))):
        other = ty[half[py], :]
        for m in range(HALF):
            rows = pl.ds((combo * HALF + m) * HALF, HALF)
            at = px * HALF + m
            w_hi[rows, lanes], w_lo[rows, lanes] = split2(tx[at : at + 1, :] * other)


def point_sums(n, t_ref, lanes, f, w_hi, w_lo, v_ref):
    tz = t_ref[2, :, lanes]
    count = 3 * MODES
    both = dot_nn(f[n], w_hi[:, lanes])
    sums = both[:count] + both[count:] + dot_nn(f[n, :count, :], w_lo[:, lanes])
    for i in range(3):
        v_ref[n, i : i + 1, lanes] = jnp.sum(sums[i * MODES : (i + 1) * MODES, :] * tz, axis=0, keepdims=True)


def hot_rows(cell, xy_hot, depth):
    place = jnp.floor((cell - 1.0) * (1.0 / depth))
    xy_hot[...] = jnp.where(
        place == lax.broadcasted_iota(jnp.int32, xy_hot.shape, 0).astype(F32), 1.0, 0.0
    ).astype(BF16)


def hot_columns(along, first, last, z_hot):
    depth = z_hot.shape[1]
    sources = along.shape[0]
    lane = lax.broadcasted_iota(jnp.int32, (sources, depth), 1).astype(F32)
    for r in range(first, last):
        z_hot[r * sources : (r + 1) * sources, :] = jnp.where(along[:, r : r + 1] == lane, 1.0, 0.0).astype(BF16)


def spread_fields(v, xy_hot, z_hot, spread, forcing):
    cells = xy_hot.shape[0]
    v_hi, v_lo = split2(v)
    for i in range(3):
        spread[2 * i * cells : (2 * i + 1) * cells, :] = xy_hot[...] * v_hi[i : i + 1, :]
        spread[(2 * i + 1) * cells : (2 * i + 2) * cells, :] = xy_hot[...] * v_lo[i : i + 1, :]
    total = dot_nn(spread[...], z_hot[...])
    for i in range(3):
        forcing[i] = total[2 * i * cells : (2 * i + 1) * cells] + total[(2 * i + 1) * cells : (2 * i + 2) * cells]


def pack_points(owner, xyz, offset, send, split):
    in_x, in_z, in_y, in_group = split
    points = owner.shape[1]
    devices = in_x * in_z * in_y * in_group
    bits = [n.bit_length() - 1 for n in (in_group, in_x, in_z)]
    c = owner & (in_group - 1)
    x = (owner >> bits[0]) & (in_x - 1)
    z = (owner >> (bits[0] + bits[1])) & (in_z - 1)
    y = owner >> (bits[0] + bits[1] + bits[2])
    place = ((y * in_x + x) * in_z + z) * in_group + c
    hit = place == lax.broadcasted_iota(jnp.int32, (devices, points), 0)
    match = jnp.where(hit, 1.0, 0.0)
    match16 = match.astype(BF16)
    run = min(points, 128)
    rows, columns = (lax.broadcasted_iota(jnp.int32, (run, 2 * run), d) for d in (0, 1))
    before = jnp.where((rows < columns) | (columns >= run), 1.0, 0.0).astype(BF16)
    offset_in = jnp.zeros((devices, run), F32)
    ranks = []
    for at in range(0, points, run):
        sums = dot_nn(match16[:, at : at + run], before)
        ranks.append(jnp.sum((sums[:, :run] + offset_in) * match[:, at : at + run], axis=0, keepdims=True))
        offset_in = offset_in + sums[:, run:]
    rank = jnp.concatenate(ranks, axis=1)
    slot = rank == lax.broadcasted_iota(jnp.int32, (SLOTS, points), 0).astype(F32)
    values = [xyz[i : i + 1, :] for i in range(3)] + [(offset + 1).astype(F32)]
    spread = jnp.concatenate([jnp.where(slot, v, 0.0) for v in values], axis=0)
    first = spread.astype(BF16)
    second, third = split2(spread - first.astype(F32))
    rows = dot_nt(match16, first) + dot_nt(match16, second) + dot_nt(match16, third)
    inner = in_z * in_group
    for d in range(devices):
        send[d // inner, d % inner] = rows[d : d + 1, :]


def wave_kernel(
    split,
    current_in, earlier_in, coef_in, mask_in, owner_in, xyz_in, offset_in, wave_in, freq_in, amp_in, index_in, table_in,
    weight_in, column_in,
    held,
    coef, mask, sign, owner, xyz, offset, wave, freq, amp, index, table, weight, column, load_sem,
    comps, comp_send, comp_recv,
    sent, first, second, hop_send, hop_recv, hop_own,
    x_in, y_in, y_out, halo_send, halo_recv,
    q, p_hi, p_lo, f_ref, f_send, f_recv, f, t_ref, w_hi, w_lo, v_ref, xy_hot, z_hot, spread, forcing,
):
    in_x, in_z, in_y, in_group = split
    slabs = in_x * in_z * in_y
    slab, comp = lax.axis_index("slab"), lax.axis_index("comp")
    x, z, y = slab % in_x, slab // in_x % in_z, slab // (in_x * in_z)
    nx, ny, nz = coef.shape
    after, before = lax.rem(slab + 1, slabs), lax.rem(slab + slabs - 1, slabs)
    right, left = lax.rem(comp + 1, in_group), lax.rem(comp + in_group - 1, in_group)
    outer, inner = y * in_x + x, z * in_group + comp
    outers, inners = in_y * in_x, in_z * in_group

    def outer_at(d):
        there = lax.rem(outer + d, outers)
        return there, ((there // in_x * in_z + z) * in_x + there % in_x, comp)

    def inner_at(d):
        there = lax.rem(inner + d, inners)
        return there, ((y * in_z + there // in_group) * in_x + x, there % in_group)

    def group_at(d):
        return comp + lax.rem(d, 2) * (1 - 2 * lax.rem(comp, 2)) + (d // 2) * (2 - 4 * (comp // 2))

    barrier = pltpu.get_barrier_semaphore()
    partners = [outer_at(d)[1] for d in range(1, outers)]
    partners += [inner_at(d)[1] for d in range(1, inners)]
    partners += [(after, comp), (before, comp)]
    loads = [
        pltpu.make_async_copy(a, b, load_sem.at[i])
        for i, (a, b) in enumerate((
            (owner_in, owner), (xyz_in, xyz), (offset_in, offset),
            (wave_in, wave), (freq_in, freq), (amp_in, amp), (index_in, index), (table_in, table),
            (current_in, held.at[1]), (column_in, column), (weight_in, weight),
            (coef_in, coef), (earlier_in, held.at[0]), (mask_in, mask),
        ))
    ]
    for load in loads[:3]:
        load.start()
    for partner in partners:
        pl.semaphore_signal(barrier, inc=1, device_id=partner, device_id_type=MESH)
    for load in loads[3:]:
        load.start()
    for load in loads[:3]:
        load.wait()
    pack_points(owner[...], xyz[...], offset[...], sent, split)
    for load in loads[3:8]:
        load.wait()
    found = index[...] == lax.broadcasted_iota(jnp.int32, (table.shape[1], index.shape[1]), 0)
    phase = lax.dot_general(
        table[...], jnp.where(found, 1.0, 0.0), (((1,), (0,)), ((), ())),
        precision=lax.Precision.HIGHEST, preferred_element_type=F32,
    )
    comps[0, 0:3, :] = wave[...]
    comps[0, 3:4, :] = freq[...]
    comps[0, 4:7, :] = amp[...]
    comps[0, 7:8, :] = phase
    loads[8].wait()

    def halo_copies(e, u, c):
        faces = (
            (u.at[c, pl.ds(0, 2)], x_in.at[e, 1, c], (before, comp)),
            (u.at[c, pl.ds(nx - 2, 2)], x_in.at[e, 0, c], (after, comp)),
            (y_out.at[e, 0, c], y_in.at[e, 1, c], (slab, left)),
            (y_out.at[e, 1, c], y_in.at[e, 0, c], (slab, right)),
        )
        return [
            pltpu.make_async_remote_copy(
                src_ref=a, dst_ref=b, send_sem=halo_send.at[e, c, i], recv_sem=halo_recv.at[e, c, i],
                device_id=target, device_id_type=MESH,
            )
            for i, (a, b, target) in enumerate(faces)
        ]

    def start_x(e, u, c):
        for copy in halo_copies(e, u, c)[:2]:
            copy.start()

    def start_y(e, u, c):
        y_out[e, 0, c] = u[c, :, 0:2, :]
        y_out[e, 1, c] = u[c, :, ny - 2 : ny, :]
        for copy in halo_copies(e, u, c)[2:]:
            copy.start()

    def start_halo(e, u, c):
        start_x(e, u, c)
        start_y(e, u, c)

    def wait_halo(e, u, c, faces):
        for copy in halo_copies(e, u, c)[faces]:
            copy.wait()

    def comp_copy(d):
        return pltpu.make_async_remote_copy(
            src_ref=comps.at[0], dst_ref=comps.at[d], send_sem=comp_send.at[d], recv_sem=comp_recv.at[d],
            device_id=(slab, group_at(d)), device_id_type=MESH,
        )

    def hop_copies(hop):
        if hop == 0:
            moves = [(sent.at[outer_at(d)[0]], first.at[outer], outer_at(d)[1]) for d in range(outers)]
        else:
            moves = [(first.at[:, inner_at(d)[0]], second.at[inner], inner_at(d)[1]) for d in range(inners)]
        own = pltpu.make_async_copy(moves[0][0], moves[0][1], hop_own.at[hop])
        return [own] + [
            pltpu.make_async_remote_copy(
                src_ref=a, dst_ref=b, send_sem=hop_send.at[hop, d], recv_sem=hop_recv.at[hop, d],
                device_id=target, device_id_type=MESH,
            )
            for d, (a, b, target) in enumerate(moves) if d > 0
        ]

    def start_hop(hop):
        for copy in hop_copies(hop):
            copy.start()

    def wait_hop(hop):
        for copy in hop_copies(hop):
            copy.wait()

    pl.semaphore_wait(barrier, len(partners))
    start_hop(0)
    for d in range(1, in_group):
        comp_copy(d).start()
    for c in range(3):
        start_halo(0, held.at[1], c)
    for load in loads[9:]:
        load.wait()
    sign[...] = jnp.where(mask[...] == 1, 1.0, 0.0) - jnp.where(mask[...] == 2, 1.0, 0.0)

    lane = lax.broadcasted_iota(jnp.int32, (ny, nz), 1)
    outside = [0, 1, nx - 2, nx - 1]
    inside = list(range(2, nx - 2))

    def advance(i, source, send):
        def some(c, planes, which):
            for x in which:
                u = planes[x + 2]
                back = jnp.where(comp > 0, y_in[i, 0, c, x], 0.0)
                front = jnp.where(comp < in_group - 1, y_in[i, 1, c, x], 0.0)
                tall = jnp.concatenate([back, u, front], axis=0)
                near = planes[x + 1] + planes[x + 3]
                far = planes[x] + planes[x + 4]
                near = near + (tall[1 : ny + 1] + tall[3 : ny + 3])
                far = far + (tall[0:ny] + tall[4 : ny + 4])
                near = near + jnp.where(lane >= 1, pltpu.roll(u, 1, 1), 0.0)
                near = near + jnp.where(lane < nz - 1, pltpu.roll(u, nz - 1, 1), 0.0)
                far = far + jnp.where(lane >= 2, pltpu.roll(u, 2, 1), 0.0)
                far = far + jnp.where(lane < nz - 2, pltpu.roll(u, nz - 2, 1), 0.0)
                curved = centre_weight * u + near_weight * near + far_weight * far
                following = 2.0 * u - held[i, c, x] + coef[x] * curved
                if source is not None:
                    following = following + source(c, x)
                held[i + 2, c, x] = following

        def inner_planes(c, carry):
            wait_halo(i, held.at[i + 1], c, slice(2, 4))
            some(c, [None, None] + [held[i + 1, c, x] for x in range(nx)], inside)
            return carry

        def outer_planes(c, carry):
            wait_halo(i, held.at[i + 1], c, slice(0, 2))
            low, high = x_in[i, 0, c], x_in[i, 1, c]
            low, high = jnp.where(slab > 0, low, 0.0), jnp.where(slab < slabs - 1, high, 0.0)
            some(c, [low[0], low[1]] + [held[i + 1, c, x] for x in range(nx)] + [high[0], high[1]], outside)
            if send is not None:
                @pl.when(send)
                def _():
                    start_halo(i + 1, held.at[i + 2], c)

            return carry

        lax.fori_loop(0, 3, inner_planes, 0)
        lax.fori_loop(0, 3, outer_planes, 0)

    wide = 2 * HALF * HALF
    core = lax.rem(comp, 2)
    odd = core == 1
    f_ref[core] = jnp.zeros((FIELDS * MODES, wide), F32)

    def one_block(i, carry):
        @pl.when(i > 0)
        def _():
            comp_copy(i).wait()

        mode_sums(comps[i], weight[...], column[...], odd, q, p_hi, p_lo)
        f_ref[core] += mode_products(q, p_hi, p_lo)

        @pl.when(i == 1)
        def _():
            wait_hop(0)
            start_hop(1)

        return carry

    lax.fori_loop(0, in_group, one_block, 0)
    half_copies = [
        pltpu.make_async_remote_copy(
            src_ref=f_ref.at[core, pl.ds(n * 3 * MODES, 3 * MODES)],
            dst_ref=f_ref.at[core, pl.ds(n * 3 * MODES, 3 * MODES)],
            send_sem=f_send.at[n], recv_sem=f_recv.at[n],
            device_id=(slab, comp + 1 - 2 * core), device_id_type=MESH,
        )
        for n in range(STEPS)
    ]
    for copy in half_copies:
        copy.start()
    advance(0, None, None)
    wait_hop(1)
    arrived = second[...].reshape(slabs * in_group, 4 * SLOTS)
    px, py, pz, cell = slot_rows(arrived)
    point_modes([px, py, pz], t_ref)
    cells = arrived[:, 3 * SLOTS :] - 1.0
    along = cells - jnp.floor(cells * (1.0 / nz)) * nz
    def lanes_of(i, chunk):
        return pl.ds(pl.multiple_of(i * chunk, chunk), chunk)

    slots = t_ref.shape[2]
    narrow, broad = slots // 4, min(slots, 1024)
    point_products(t_ref, pl.ds(0, narrow), w_hi, w_lo)
    rows = 3 * MODES

    def take_half(n):
        half_copies[n].wait()
        for which in (0, 1):
            lanes = pl.ds(which * wide, wide)
            f[n, :rows, lanes], f[n, rows:, lanes] = split2(f_ref[which, n * rows : (n + 1) * rows, :])

    take_half(0)
    for i in range(4):
        point_sums(0, t_ref, pl.ds(i * narrow, narrow), f, w_hi, w_lo, v_ref)
        if i < 3:
            point_products(t_ref, pl.ds((i + 1) * narrow, narrow), w_hi, w_lo)
            hot_columns(along, i * SLOTS // 4, (i + 1) * SLOTS // 4, z_hot)
        else:
            hot_columns(along, i * SLOTS // 4, SLOTS, z_hot)
            hot_rows(cell, xy_hot, nz)
    spread_fields(v_ref[0], xy_hot, z_hot, spread, forcing)

    def source(c, x):
        return sign[x] * forcing[c, x * ny : (x + 1) * ny, :]

    def first_outside(c, carry):
        for x in outside:
            held[2, c, x] += source(c, x)
        start_x(1, held.at[2], c)
        return carry

    def first_inside(c, carry):
        for x in inside:
            held[2, c, x] += source(c, x)
        start_y(1, held.at[2], c)
        return carry

    lax.fori_loop(0, 3, first_outside, 0)
    lax.fori_loop(0, 3, first_inside, 0)

    def one_step(n, carry):
        for step in range(1, STEPS):
            @pl.when(n == step)
            def _(step=step):
                take_half(step)

        def one_chunk(i, inner):
            point_sums(n, t_ref, lanes_of(i, broad), f, w_hi, w_lo, v_ref)
            return inner

        lax.fori_loop(0, slots // broad, one_chunk, 0)
        spread_fields(v_ref[n], xy_hot, z_hot, spread, forcing)

        advance(n, source, n < STEPS - 1)
        return carry

    lax.fori_loop(1, STEPS, one_step, 0)

def local(current_field, earlier_field, wave_coef, layer_mask, point_xyz, point_owner, cell_offset, wave_vector, frequency, amplitude, phase_index, phase_table):
    slabs, in_group = lax.axis_size("slab"), lax.axis_size("comp")
    in_x, in_z = 4, 2
    in_y = slabs // (in_x * in_z)
    devices = slabs * in_group
    points = point_xyz.shape[1]
    width = frequency.shape[0]
    _, nx, ny, nz = current_field.shape
    modes = 4 * HALF * HALF
    slots = devices * SLOTS
    weight, column = mode_tables()
    operands = (
        current_field, earlier_field, wave_coef, layer_mask, point_owner.reshape(1, points), point_xyz,
        cell_offset.reshape(1, points), wave_vector, frequency.reshape(1, width), amplitude,
        phase_index.reshape(1, width), phase_table.reshape(1, -1), jnp.asarray(weight), jnp.asarray(column),
    )
    like = [pltpu.VMEM(a.shape, a.dtype) for a in operands]
    dma = pltpu.SemaphoreType.DMA
    exchanges = STEPS
    held = pl.pallas_call(
        functools.partial(wave_kernel, (in_x, in_z, in_y, in_group)),
        out_shape=pltpu.VMEM((STEPS + 2, 3, nx, ny, nz), F32),
        in_specs=[pl.BlockSpec(memory_space=pl.ANY)] * len(operands),
        out_specs=pl.BlockSpec(memory_space=pltpu.VMEM),
        scratch_shapes=[
            like[2], like[3], pltpu.VMEM((nx, ny, nz), F32), *like[4:], dma((len(operands),)),
            pltpu.VMEM((in_group, 8, width), F32), dma((in_group,)), dma((in_group,)),
            pltpu.VMEM((in_y * in_x, in_z * in_group, 1, 4 * SLOTS), F32),
            pltpu.VMEM((in_y * in_x, in_z * in_group, 1, 4 * SLOTS), F32),
            pltpu.VMEM((in_z * in_group, in_y * in_x, 1, 4 * SLOTS), F32),
            dma((2, in_y * in_x)), dma((2, in_y * in_x)), dma((2,)),
            pltpu.VMEM((exchanges, 2, 3, 2, ny, nz), F32),
            pltpu.VMEM((exchanges, 2, 3, nx, 2, nz), F32),
            pltpu.VMEM((exchanges, 2, 3, nx, 2, nz), F32),
            dma((exchanges, 3, 4)), dma((exchanges, 3, 4)),
            pltpu.VMEM((2 * FIELDS * MODES, width), BF16),
            pltpu.VMEM((modes // 2, width), BF16),
            pltpu.VMEM((modes // 2, width), BF16),
            pltpu.VMEM((2, FIELDS * MODES, modes // 2), F32), dma((STEPS,)), dma((STEPS,)),
            pltpu.VMEM((STEPS, 6 * MODES, modes), BF16),
            pltpu.VMEM((3, MODES, slots), F32),
            pltpu.VMEM((modes, slots), BF16),
            pltpu.VMEM((modes, slots), BF16),
            pltpu.VMEM((STEPS, 3, slots), F32),
            pltpu.VMEM((nx * ny, slots), BF16),
            pltpu.VMEM((slots, nz), BF16),
            pltpu.VMEM((6 * nx * ny, slots), BF16),
            pltpu.VMEM((3, nx * ny, nz), F32),
        ],
        compiler_params=pltpu.CompilerParams(
            collective_id=0, has_side_effects=True, vmem_limit_bytes=59200 << 10
        ),
    )(*operands)
    return held[STEPS + 1], held[STEPS]


def solution(mesh):
    in_specs = (
        P(None, "slab", "comp", None),
        P(None, "slab", "comp", None),
        P("slab", "comp", None),
        P("slab", "comp", None),
        P(None, ("slab", "comp")),
        P(("slab", "comp"), None),
        P(("slab", "comp")),
        P(None, "comp"),
        P("comp"),
        P(None, "comp"),
        P("comp"),
        P(),
    )
    out_specs = (P(None, "slab", "comp", None), P(None, "slab", "comp", None))
    return jax.shard_map(local, mesh=mesh, in_specs=in_specs, out_specs=out_specs, check_vma=False)
```

```python
import functools

import jax
import jax.numpy as jnp
import numpy as np
from jax import lax
from jax.experimental import pallas as pl
from jax.experimental.pallas import tpu as pltpu
from jax.sharding import PartitionSpec as P

STEPS = 3
SLOTS = 16
HALF = 16
MODES = 2 * HALF
FIELDS = 9
F32 = jnp.float32
BF16 = jnp.bfloat16
MESH = pl.DeviceIdType.MESH

step_size = 0.05
near_weight = 4.0 / 3.0
far_weight = -1.0 / 12.0
centre_weight = -7.5


def turn_series(degree):
    fits = []
    for h in (
        lambda s: np.cos(2 * np.pi * np.sqrt(s)),
        lambda s: np.sinc(2 * np.sqrt(s)) * 2 * np.pi,
    ):
        fit = np.polynomial.chebyshev.Chebyshev.interpolate(h, degree, domain=[0, 0.25])
        fits.append([float(c) for c in fit.convert(kind=np.polynomial.Polynomial).coef])
    return fits


COS_SERIES, SIN_SERIES = turn_series(7)


def horner(series, s):
    total = jnp.full_like(s, series[-1])
    for c in series[-2::-1]:
        total = total * s + c
    return total


def cos_sin_turns(u):
    r = u - jnp.round(u)
    s = r * r
    return horner(COS_SERIES, s), r * horner(SIN_SERIES, s)


def mode_tables():
    a = np.arange(HALF)
    angle = (2 * a + 1) * np.pi / (2 * MODES)
    nodes = np.cos(angle)
    weight = np.zeros((6 * HALF, 6 * HALF))
    for dim in range(3):
        for parity in (0, 1):
            m = 2 * np.arange(HALF) + parity
            block = 4.0 / MODES * np.cos(m[:, None] * angle[None, :])
            if parity == 0:
                block[0] *= 0.5
            at = (parity * 3 + dim) * HALF
            weight[at : at + HALF, at : at + HALF] = block
    column = np.tile(nodes, 3)[:, None] * np.ones((1, 128))
    return weight.astype(np.float32), column.astype(np.float32)


def split2(x):
    high = x.astype(BF16)
    return high, (x - high.astype(F32)).astype(BF16)


def dot_nt(a, b):
    return lax.dot_general(a, b, (((1,), (1,)), ((), ())), preferred_element_type=F32)


def dot_nn(a, b):
    return lax.dot_general(a, b, (((1,), (0,)), ((), ())), preferred_element_type=F32)


def mode_sums(block, weight, column, odd, q, p_hi, p_lo):
    turn = 1.0 / (2.0 * np.pi)
    rows = FIELDS * MODES
    angles = jnp.concatenate(
        [column[d * HALF : (d + 1) * HALF, 0:1] * (block[d : d + 1, :] * (2.0 * turn)) for d in range(3)], axis=0
    )
    cosine, sine = cos_sin_turns(angles)
    series = lax.dot_general(
        weight, jnp.concatenate([cosine, sine], axis=0), (((1,), (0,)), ((), ())),
        precision=lax.Precision.HIGHEST, preferred_element_type=F32,
    )
    cx, cy, cz, sx, sy, sz = [series[i * HALF : (i + 1) * HALF, :] for i in range(6)]
    centre = (2.0 * turn) * (block[0:1, :] + block[1:2, :] + block[2:3, :]) + turn * block[7:8, :]
    for n in range(STEPS):
        shift_cos, shift_sin = cos_sin_turns(centre - block[3:4, :] * (turn * step_size * (n + 1)))
        outer = jnp.where(odd, -shift_sin, shift_cos)
        inner = jnp.where(odd, -shift_cos, -shift_sin)
        for i in range(3):
            amp = block[4 + i : 5 + i, :]
            at = (3 * n + i) * MODES
            for part, value in ((0, (amp * outer) * cz), (1, (amp * inner) * sz)):
                low = at + part * HALF
                q[low : low + HALF, :], q[rows + low : rows + low + HALF, :] = split2(value)
    even_y = jnp.where(odd, sy, cy)
    odd_y = jnp.where(odd, cy, -sy)
    for m in range(HALF):
        rows_a, rows_b = pl.ds(m * HALF, HALF), pl.ds((HALF + m) * HALF, HALF)
        p_hi[rows_a, :], p_lo[rows_a, :] = split2(cx[m : m + 1, :] * even_y)
        p_hi[rows_b, :], p_lo[rows_b, :] = split2(sx[m : m + 1, :] * odd_y)


def mode_products(q, p_hi, p_lo):
    rows = FIELDS * MODES
    both = dot_nt(q[...], p_hi[...])
    return both[:rows] + both[rows:] + dot_nt(q[:rows, :], p_lo[...])


def slot_rows(arrived):
    turned = arrived.T
    return [
        jnp.concatenate([turned[c * SLOTS + r : c * SLOTS + r + 1, :] for r in range(SLOTS)], axis=1)
        for c in range(4)
    ]


def point_modes(rows, t_ref):
    tau = jnp.concatenate([(r - 2.0) * 0.5 for r in rows], axis=0)
    older, old = jnp.ones_like(tau), tau
    for m in range(MODES):
        at = (m % 2) * HALF + m // 2
        for d in range(3):
            t_ref[d, at : at + 1, :] = older[d : d + 1, :]
        older, old = old, 2.0 * tau * old - older


def point_products(t_ref, lanes, w_hi, w_lo):
    tx, ty = t_ref[0, :, lanes], t_ref[1, :, lanes]
    half = [slice(0, HALF), slice(HALF, MODES)]
    for combo, (px, py) in enumerate(((0, 0), (1, 1), (0, 1), (1, 0))):
        other = ty[half[py], :]
        for m in range(HALF):
            rows = pl.ds((combo * HALF + m) * HALF, HALF)
            at = px * HALF + m
            w_hi[rows, lanes], w_lo[rows, lanes] = split2(tx[at : at + 1, :] * other)


def point_sums(n, t_ref, lanes, f, w_hi, w_lo, v_ref):
    tz = t_ref[2, :, lanes]
    count = 3 * MODES
    both = dot_nn(f[n], w_hi[:, lanes])
    sums = both[:count] + both[count:] + dot_nn(f[n, :count, :], w_lo[:, lanes])
    for i in range(3):
        v_ref[n, i : i + 1, lanes] = jnp.sum(sums[i * MODES : (i + 1) * MODES, :] * tz, axis=0, keepdims=True)


def hot_rows(cell, xy_hot, depth):
    place = jnp.floor((cell - 1.0) * (1.0 / depth))
    xy_hot[...] = jnp.where(
        place == lax.broadcasted_iota(jnp.int32, xy_hot.shape, 0).astype(F32), 1.0, 0.0
    ).astype(BF16)


def hot_columns(along, first, last, z_hot):
    depth = z_hot.shape[1]
    sources = along.shape[0]
    lane = lax.broadcasted_iota(jnp.int32, (sources, depth), 1).astype(F32)
    for r in range(first, last):
        z_hot[r * sources : (r + 1) * sources, :] = jnp.where(along[:, r : r + 1] == lane, 1.0, 0.0).astype(BF16)


def spread_fields(v, xy_hot, z_hot, spread, forcing):
    cells = xy_hot.shape[0]
    v_hi, v_lo = split2(v)
    for i in range(3):
        spread[2 * i * cells : (2 * i + 1) * cells, :] = xy_hot[...] * v_hi[i : i + 1, :]
        spread[(2 * i + 1) * cells : (2 * i + 2) * cells, :] = xy_hot[...] * v_lo[i : i + 1, :]
    total = dot_nn(spread[...], z_hot[...])
    for i in range(3):
        forcing[i] = total[2 * i * cells : (2 * i + 1) * cells] + total[(2 * i + 1) * cells : (2 * i + 2) * cells]


def pack_points(owner, xyz, offset, send, split):
    in_x, in_z, in_y, in_group = split
    points = owner.shape[1]
    devices = in_x * in_z * in_y * in_group
    bits = [n.bit_length() - 1 for n in (in_group, in_x, in_z)]
    c = owner & (in_group - 1)
    x = (owner >> bits[0]) & (in_x - 1)
    z = (owner >> (bits[0] + bits[1])) & (in_z - 1)
    y = owner >> (bits[0] + bits[1] + bits[2])
    place = ((y * in_x + x) * in_z + z) * in_group + c
    hit = place == lax.broadcasted_iota(jnp.int32, (devices, points), 0)
    match = jnp.where(hit, 1.0, 0.0)
    match16 = match.astype(BF16)
    run = min(points, 128)
    rows, columns = (lax.broadcasted_iota(jnp.int32, (run, 2 * run), d) for d in (0, 1))
    before = jnp.where((rows < columns) | (columns >= run), 1.0, 0.0).astype(BF16)
    offset_in = jnp.zeros((devices, run), F32)
    ranks = []
    for at in range(0, points, run):
        sums = dot_nn(match16[:, at : at + run], before)
        ranks.append(jnp.sum((sums[:, :run] + offset_in) * match[:, at : at + run], axis=0, keepdims=True))
        offset_in = offset_in + sums[:, run:]
    rank = jnp.concatenate(ranks, axis=1)
    slot = rank == lax.broadcasted_iota(jnp.int32, (SLOTS, points), 0).astype(F32)
    values = [xyz[i : i + 1, :] for i in range(3)] + [(offset + 1).astype(F32)]
    spread = jnp.concatenate([jnp.where(slot, v, 0.0) for v in values], axis=0)
    first = spread.astype(BF16)
    second, third = split2(spread - first.astype(F32))
    rows = dot_nt(match16, first) + dot_nt(match16, second) + dot_nt(match16, third)
    inner = in_z * in_group
    for d in range(devices):
        send[d // inner, d % inner] = rows[d : d + 1, :]


def wave_kernel(
    split,
    current_in, earlier_in, coef_in, mask_in, owner_in, xyz_in, offset_in, wave_in, freq_in, amp_in, index_in, table_in,
    weight_in, column_in,
    held,
    coef, mask, sign, owner, xyz, offset, wave, freq, amp, index, table, weight, column, load_sem,
    comps, comp_send, comp_recv,
    sent, first, second, hop_send, hop_recv, hop_own,
    x_in, y_in, y_out, halo_send, halo_recv,
    q, p_hi, p_lo, f_ref, f_send, f_recv, f, t_ref, w_hi, w_lo, v_ref, xy_hot, z_hot, spread, forcing,
):
    in_x, in_z, in_y, in_group = split
    slabs = in_x * in_z * in_y
    slab, comp = lax.axis_index("slab"), lax.axis_index("comp")
    x, z, y = slab % in_x, slab // in_x % in_z, slab // (in_x * in_z)
    nx, ny, nz = coef.shape
    after, before = lax.rem(slab + 1, slabs), lax.rem(slab + slabs - 1, slabs)
    right, left = lax.rem(comp + 1, in_group), lax.rem(comp + in_group - 1, in_group)
    outer, inner = y * in_x + x, z * in_group + comp
    outers, inners = in_y * in_x, in_z * in_group

    def outer_at(d):
        there = lax.rem(outer + d, outers)
        return there, ((there // in_x * in_z + z) * in_x + there % in_x, comp)

    def inner_at(d):
        there = lax.rem(inner + d, inners)
        return there, ((y * in_z + there // in_group) * in_x + x, there % in_group)

    def group_at(d):
        return comp + lax.rem(d, 2) * (1 - 2 * lax.rem(comp, 2)) + (d // 2) * (2 - 4 * (comp // 2))

    barrier = pltpu.get_barrier_semaphore()
    partners = [outer_at(d)[1] for d in range(1, outers)]
    partners += [inner_at(d)[1] for d in range(1, inners)]
    partners += [(after, comp), (before, comp)]
    loads = [
        pltpu.make_async_copy(a, b, load_sem.at[i])
        for i, (a, b) in enumerate((
            (owner_in, owner), (xyz_in, xyz), (offset_in, offset),
            (wave_in, wave), (freq_in, freq), (amp_in, amp), (index_in, index), (table_in, table),
            (current_in, held.at[1]), (column_in, column), (weight_in, weight),
            (coef_in, coef), (earlier_in, held.at[0]), (mask_in, mask),
        ))
    ]
    for load in loads[:3]:
        load.start()
    for partner in partners:
        pl.semaphore_signal(barrier, inc=1, device_id=partner, device_id_type=MESH)
    for load in loads[3:]:
        load.start()
    for load in loads[:3]:
        load.wait()
    pack_points(owner[...], xyz[...], offset[...], sent, split)
    for load in loads[3:8]:
        load.wait()
    found = index[...] == lax.broadcasted_iota(jnp.int32, (table.shape[1], index.shape[1]), 0)
    phase = lax.dot_general(
        table[...], jnp.where(found, 1.0, 0.0), (((1,), (0,)), ((), ())),
        precision=lax.Precision.HIGHEST, preferred_element_type=F32,
    )
    comps[0, 0:3, :] = wave[...]
    comps[0, 3:4, :] = freq[...]
    comps[0, 4:7, :] = amp[...]
    comps[0, 7:8, :] = phase
    loads[8].wait()

    def halo_copies(e, u, c):
        faces = (
            (u.at[c, pl.ds(0, 2)], x_in.at[e, 1, c], (before, comp)),
            (u.at[c, pl.ds(nx - 2, 2)], x_in.at[e, 0, c], (after, comp)),
            (y_out.at[e, 0, c], y_in.at[e, 1, c], (slab, left)),
            (y_out.at[e, 1, c], y_in.at[e, 0, c], (slab, right)),
        )
        return [
            pltpu.make_async_remote_copy(
                src_ref=a, dst_ref=b, send_sem=halo_send.at[e, c, i], recv_sem=halo_recv.at[e, c, i],
                device_id=target, device_id_type=MESH,
            )
            for i, (a, b, target) in enumerate(faces)
        ]

    def start_x(e, u, c):
        for copy in halo_copies(e, u, c)[:2]:
            copy.start()

    def start_y(e, u, c):
        y_out[e, 0, c] = u[c, :, 0:2, :]
        y_out[e, 1, c] = u[c, :, ny - 2 : ny, :]
        for copy in halo_copies(e, u, c)[2:]:
            copy.start()

    def start_halo(e, u, c):
        start_x(e, u, c)
        start_y(e, u, c)

    def wait_halo(e, u, c, faces):
        for copy in halo_copies(e, u, c)[faces]:
            copy.wait()

    def comp_copy(d):
        return pltpu.make_async_remote_copy(
            src_ref=comps.at[0], dst_ref=comps.at[d], send_sem=comp_send.at[d], recv_sem=comp_recv.at[d],
            device_id=(slab, group_at(d)), device_id_type=MESH,
        )

    def hop_copies(hop):
        if hop == 0:
            moves = [(sent.at[outer_at(d)[0]], first.at[outer], outer_at(d)[1]) for d in range(outers)]
        else:
            moves = [(first.at[:, inner_at(d)[0]], second.at[inner], inner_at(d)[1]) for d in range(inners)]
        own = pltpu.make_async_copy(moves[0][0], moves[0][1], hop_own.at[hop])
        return [own] + [
            pltpu.make_async_remote_copy(
                src_ref=a, dst_ref=b, send_sem=hop_send.at[hop, d], recv_sem=hop_recv.at[hop, d],
                device_id=target, device_id_type=MESH,
            )
            for d, (a, b, target) in enumerate(moves) if d > 0
        ]

    def start_hop(hop):
        for copy in hop_copies(hop):
            copy.start()

    def wait_hop(hop):
        for copy in hop_copies(hop):
            copy.wait()

    pl.semaphore_wait(barrier, len(partners))
    for d in range(1, in_group):
        comp_copy(d).start()
    start_hop(0)
    for c in range(3):
        start_halo(0, held.at[1], c)
    for load in loads[9:]:
        load.wait()
    sign[...] = jnp.where(mask[...] == 1, 1.0, 0.0) - jnp.where(mask[...] == 2, 1.0, 0.0)

    lane = lax.broadcasted_iota(jnp.int32, (ny, nz), 1)
    outside = [0, 1, nx - 2, nx - 1]
    inside = list(range(2, nx - 2))

    def advance(i, source, send):
        def some(c, planes, which):
            for x in which:
                u = planes[x + 2]
                back = jnp.where(comp > 0, y_in[i, 0, c, x], 0.0)
                front = jnp.where(comp < in_group - 1, y_in[i, 1, c, x], 0.0)
                tall = jnp.concatenate([back, u, front], axis=0)
                near = planes[x + 1] + planes[x + 3]
                far = planes[x] + planes[x + 4]
                near = near + (tall[1 : ny + 1] + tall[3 : ny + 3])
                far = far + (tall[0:ny] + tall[4 : ny + 4])
                near = near + jnp.where(lane >= 1, pltpu.roll(u, 1, 1), 0.0)
                near = near + jnp.where(lane < nz - 1, pltpu.roll(u, nz - 1, 1), 0.0)
                far = far + jnp.where(lane >= 2, pltpu.roll(u, 2, 1), 0.0)
                far = far + jnp.where(lane < nz - 2, pltpu.roll(u, nz - 2, 1), 0.0)
                curved = centre_weight * u + near_weight * near + far_weight * far
                following = 2.0 * u - held[i, c, x] + coef[x] * curved
                if source is not None:
                    following = following + source(c, x)
                held[i + 2, c, x] = following

        def inner_planes(c, carry):
            wait_halo(i, held.at[i + 1], c, slice(2, 4))
            some(c, [None, None] + [held[i + 1, c, x] for x in range(nx)], inside)
            return carry

        def outer_planes(c, carry):
            wait_halo(i, held.at[i + 1], c, slice(0, 2))
            low, high = x_in[i, 0, c], x_in[i, 1, c]
            low, high = jnp.where(slab > 0, low, 0.0), jnp.where(slab < slabs - 1, high, 0.0)
            some(c, [low[0], low[1]] + [held[i + 1, c, x] for x in range(nx)] + [high[0], high[1]], outside)
            if send is not None:
                @pl.when(send)
                def _():
                    start_halo(i + 1, held.at[i + 2], c)

            return carry

        lax.fori_loop(0, 3, inner_planes, 0)
        lax.fori_loop(0, 3, outer_planes, 0)

    wide = 2 * HALF * HALF
    core = lax.rem(comp, 2)
    odd = core == 1
    f_ref[core] = jnp.zeros((FIELDS * MODES, wide), F32)

    def one_block(i, carry):
        @pl.when(i > 0)
        def _():
            comp_copy(i).wait()

        mode_sums(comps[i], weight[...], column[...], odd, q, p_hi, p_lo)
        f_ref[core] += mode_products(q, p_hi, p_lo)

        @pl.when(i == 2)
        def _():
            wait_hop(0)
            start_hop(1)

        return carry

    lax.fori_loop(0, in_group, one_block, 0)
    half_copies = [
        pltpu.make_async_remote_copy(
            src_ref=f_ref.at[core, pl.ds(n * 3 * MODES, 3 * MODES)],
            dst_ref=f_ref.at[core, pl.ds(n * 3 * MODES, 3 * MODES)],
            send_sem=f_send.at[n], recv_sem=f_recv.at[n],
            device_id=(slab, comp + 1 - 2 * core), device_id_type=MESH,
        )
        for n in range(STEPS)
    ]
    for copy in half_copies:
        copy.start()
    advance(0, None, None)
    wait_hop(1)
    arrived = second[...].reshape(slabs * in_group, 4 * SLOTS)
    px, py, pz, cell = slot_rows(arrived)
    point_modes([px, py, pz], t_ref)
    cells = arrived[:, 3 * SLOTS :] - 1.0
    along = cells - jnp.floor(cells * (1.0 / nz)) * nz
    def lanes_of(i, chunk):
        return pl.ds(pl.multiple_of(i * chunk, chunk), chunk)

    slots = t_ref.shape[2]
    narrow, broad = slots // 4, min(slots, 1024)
    point_products(t_ref, pl.ds(0, narrow), w_hi, w_lo)
    rows = 3 * MODES

    def take_half(n):
        half_copies[n].wait()
        for which in (0, 1):
            lanes = pl.ds(which * wide, wide)
            f[n, :rows, lanes], f[n, rows:, lanes] = split2(f_ref[which, n * rows : (n + 1) * rows, :])

    take_half(0)
    for i in range(4):
        point_sums(0, t_ref, pl.ds(i * narrow, narrow), f, w_hi, w_lo, v_ref)
        if i < 3:
            point_products(t_ref, pl.ds((i + 1) * narrow, narrow), w_hi, w_lo)
            hot_columns(along, i * SLOTS // 4, (i + 1) * SLOTS // 4, z_hot)
        else:
            hot_columns(along, i * SLOTS // 4, SLOTS, z_hot)
            hot_rows(cell, xy_hot, nz)
    spread_fields(v_ref[0], xy_hot, z_hot, spread, forcing)

    def source(c, x):
        return sign[x] * forcing[c, x * ny : (x + 1) * ny, :]

    def first_outside(c, carry):
        for x in outside:
            held[2, c, x] += source(c, x)
        start_x(1, held.at[2], c)
        return carry

    def first_inside(c, carry):
        for x in inside:
            held[2, c, x] += source(c, x)
        start_y(1, held.at[2], c)
        return carry

    lax.fori_loop(0, 3, first_outside, 0)
    lax.fori_loop(0, 3, first_inside, 0)

    def one_step(n, carry):
        for step in range(1, STEPS):
            @pl.when(n == step)
            def _(step=step):
                take_half(step)

        def one_chunk(i, inner):
            point_sums(n, t_ref, lanes_of(i, broad), f, w_hi, w_lo, v_ref)
            return inner

        lax.fori_loop(0, slots // broad, one_chunk, 0)
        spread_fields(v_ref[n], xy_hot, z_hot, spread, forcing)

        advance(n, source, n < STEPS - 1)
        return carry

    lax.fori_loop(1, STEPS, one_step, 0)

def local(current_field, earlier_field, wave_coef, layer_mask, point_xyz, point_owner, cell_offset, wave_vector, frequency, amplitude, phase_index, phase_table):
    slabs, in_group = lax.axis_size("slab"), lax.axis_size("comp")
    in_x, in_z = 4, 2
    in_y = slabs // (in_x * in_z)
    devices = slabs * in_group
    points = point_xyz.shape[1]
    width = frequency.shape[0]
    _, nx, ny, nz = current_field.shape
    modes = 4 * HALF * HALF
    slots = devices * SLOTS
    weight, column = mode_tables()
    operands = (
        current_field, earlier_field, wave_coef, layer_mask, point_owner.reshape(1, points), point_xyz,
        cell_offset.reshape(1, points), wave_vector, frequency.reshape(1, width), amplitude,
        phase_index.reshape(1, width), phase_table.reshape(1, -1), jnp.asarray(weight), jnp.asarray(column),
    )
    like = [pltpu.VMEM(a.shape, a.dtype) for a in operands]
    dma = pltpu.SemaphoreType.DMA
    exchanges = STEPS
    held = pl.pallas_call(
        functools.partial(wave_kernel, (in_x, in_z, in_y, in_group)),
        out_shape=pltpu.VMEM((STEPS + 2, 3, nx, ny, nz), F32),
        in_specs=[pl.BlockSpec(memory_space=pl.ANY)] * len(operands),
        out_specs=pl.BlockSpec(memory_space=pltpu.VMEM),
        scratch_shapes=[
            like[2], like[3], pltpu.VMEM((nx, ny, nz), F32), *like[4:], dma((len(operands),)),
            pltpu.VMEM((in_group, 8, width), F32), dma((in_group,)), dma((in_group,)),
            pltpu.VMEM((in_y * in_x, in_z * in_group, 1, 4 * SLOTS), F32),
            pltpu.VMEM((in_y * in_x, in_z * in_group, 1, 4 * SLOTS), F32),
            pltpu.VMEM((in_z * in_group, in_y * in_x, 1, 4 * SLOTS), F32),
            dma((2, in_y * in_x)), dma((2, in_y * in_x)), dma((2,)),
            pltpu.VMEM((exchanges, 2, 3, 2, ny, nz), F32),
            pltpu.VMEM((exchanges, 2, 3, nx, 2, nz), F32),
            pltpu.VMEM((exchanges, 2, 3, nx, 2, nz), F32),
            dma((exchanges, 3, 4)), dma((exchanges, 3, 4)),
            pltpu.VMEM((2 * FIELDS * MODES, width), BF16),
            pltpu.VMEM((modes // 2, width), BF16),
            pltpu.VMEM((modes // 2, width), BF16),
            pltpu.VMEM((2, FIELDS * MODES, modes // 2), F32), dma((STEPS,)), dma((STEPS,)),
            pltpu.VMEM((STEPS, 6 * MODES, modes), BF16),
            pltpu.VMEM((3, MODES, slots), F32),
            pltpu.VMEM((modes, slots), BF16),
            pltpu.VMEM((modes, slots), BF16),
            pltpu.VMEM((STEPS, 3, slots), F32),
            pltpu.VMEM((nx * ny, slots), BF16),
            pltpu.VMEM((slots, nz), BF16),
            pltpu.VMEM((6 * nx * ny, slots), BF16),
            pltpu.VMEM((3, nx * ny, nz), F32),
        ],
        compiler_params=pltpu.CompilerParams(
            collective_id=0, has_side_effects=True, vmem_limit_bytes=59200 << 10
        ),
    )(*operands)
    return held[STEPS + 1], held[STEPS]


def solution(mesh):
    in_specs = (
        P(None, "slab", "comp", None),
        P(None, "slab", "comp", None),
        P("slab", "comp", None),
        P("slab", "comp", None),
        P(None, ("slab", "comp")),
        P(("slab", "comp"), None),
        P(("slab", "comp")),
        P(None, "comp"),
        P("comp"),
        P(None, "comp"),
        P("comp"),
        P(),
    )
    out_specs = (P(None, "slab", "comp", None), P(None, "slab", "comp", None))
    return jax.shard_map(local, mesh=mesh, in_specs=in_specs, out_specs=out_specs, check_vma=False)
```
